32 devices in a mesh: tile: 8 (over z, x), dp: 4 (over y, core).
Axes of the slice: x: 2, y: 2, z: 4, core: 2. Of those that a mesh axis runs over, the one named last changes fastest.
Arguments:
- inputs: bfloat16 [4, 8, 32, 32, 128], P('dp', 'tile'), may hold values from -6 to 6
- weight_one: bfloat16 [9, 128, 128], replicated, may hold values from -0.1875 to 0.1875
- weight_two: bfloat16 [9, 128, 128], replicated, may hold values from -0.1875 to 0.1875
- cotangent: bfloat16 [4, 8, 32, 32, 128], P('dp', 'tile'), may hold values from -6 to 6
- edge_code: int32 [8, 4], replicated, may hold values from 0 to 7
- corner_code: int32 [8, 4], replicated, may hold values from 0 to 3
Outputs:
- output: bfloat16 [4, 8, 32, 32, 128], P('dp', 'tile')
- d_input: bfloat16 [4, 8, 32, 32, 128], P('dp', 'tile')
- grad_one: float32 [9, 128, 128], replicated
- grad_two: float32 [9, 128, 128], replicated
The draws below stay inside these ranges and needn't reach their ends.
Inputs may be any that keep to these rules, and one draw needn't show every extreme that they name: edge_code[t, k]: which border of the neighbour across side k fills that margin side (code mod 4), reversed for codes 4 to 7. corner_code[t, q]: which corner pixel of diagonal neighbour q fills margin corner q.
All inputs are finite; a program needn't handle non-finite values.
Results may differ from the reference program's by a relative error of at most 0.0036.
Values may be sent and summed in bfloat16 or wider, within the bound.
No kernel may reach another device: no remote copies, remote signals or barrier semaphores. Data moves between devices by JAX's collectives and lax.ppermute only.
A program may use at most 64 MiB of HBM per device.

```python
import math
from functools import partial
import jax
import jax.numpy as jnp
from jax import lax

C = 128
S = 32
RW = 4
NSUB = 8
BATCH = 4


def with_ends(entries, stream_key, least, high):
    shape = entries.shape
    spot = [jax.random.randint(jax.random.fold_in(stream_key, axis), (), 0, shape[axis]) for axis in range(len(shape))]
    entries = entries.at[tuple(spot)].set(least)
    longest = shape.index(max(shape))
    spot[longest] = (spot[longest] + 1) % shape[longest]
    return entries.at[tuple(spot)].set(high)


def shard_levels(stream_key, shape, shards, smallest, high):
    level = 1.0
    for axis_at, shards_of in shards:
        draws = jax.random.uniform(jax.random.fold_in(jax.random.fold_in(stream_key, 6), axis_at), (shards_of,), jnp.float32, smallest / len(shards), high / len(shards))
        level = level * jnp.repeat(jnp.exp(draws), shape[axis_at] // shards_of).reshape((-1,) + (1,) * (len(shape) - 1 - axis_at))
    return level


def noise(stream_key, shape, spread, most, shards=(), held_as=jnp.bfloat16):
    array = jax.random.normal(stream_key, shape, jnp.float32) * spread
    if len(shards) > 0:
        array = shard_levels(stream_key, shape, shards, -0.22, 0.18) * array
    return jnp.clip(array, min=-most, max=most).astype(held_as)


def setup_inputs(seed: int = 0) -> dict:
    keys = jax.random.split(jax.random.key(seed), 7)
    inputs = noise(keys[0], (BATCH, NSUB, S, S, C), 1.0, 6.0, ((0, 4), (1, 8)))
    weight_one = noise(keys[1], (9, C, C), (9 * C) ** -0.5, 0.1875)
    weight_two = noise(keys[2], (9, C, C), (9 * C) ** -0.5, 0.1875)
    cotangent = noise(keys[3], (BATCH, NSUB, S, S, C), 1.0, 6.0, ((0, 4), (1, 8)))
    edge_code = with_ends(jax.random.randint(keys[4], (NSUB, 4), 0, 8), jax.random.fold_in(keys[4], 1), 0, 7).astype(jnp.int32)
    corner_code = with_ends(jax.random.randint(keys[5], (NSUB, 4), 0, 4), jax.random.fold_in(keys[5], 1), 0, 3).astype(jnp.int32)
    return dict(inputs=inputs, weight_one=weight_one, weight_two=weight_two, cotangent=cotangent, edge_code=edge_code, corner_code=corner_code)


def side_offsets():
    return (-RW, 1, RW, -1)

def corner_offsets():
    return (-RW - 1, -RW + 1, RW + 1, RW - 1)

def build_halo(source, edge_code, corner_code):
    nsubs = source.shape[1]
    extent = source.shape[2]
    borders = jnp.stack([source[:, :, 0], source[:, :, :, extent - 1], source[:, :, extent - 1], source[:, :, :, 0]], axis=2)
    oriented = jnp.concatenate([borders, borders[:, :, :, ::-1]], axis=2)
    corners = jnp.stack([source[:, :, 0, 0], source[:, :, 0, extent - 1], source[:, :, extent - 1, extent - 1], source[:, :, extent - 1, 0]], axis=2)
    subtile_ids = jnp.arange(nsubs, dtype=jnp.int32)
    padded = jnp.pad(source, ((0, 0), (0, 0), (1, 1), (1, 1), (0, 0)))
    strips = []
    for edge_index, offset in enumerate(side_offsets()):
        partner = (subtile_ids + offset) % nsubs
        strips.append(oriented[:, partner, edge_code[:, edge_index]])
    padded = padded.at[:, :, 0, 1:extent + 1].set(strips[0])
    padded = padded.at[:, :, 1:extent + 1, extent + 1].set(strips[1])
    padded = padded.at[:, :, extent + 1, 1:extent + 1].set(strips[2])
    padded = padded.at[:, :, 1:extent + 1, 0].set(strips[3])
    places = ((0, 0), (0, extent + 1), (extent + 1, extent + 1), (extent + 1, 0))
    for corner_index, offset in enumerate(corner_offsets()):
        partner = (subtile_ids + offset) % nsubs
        picked = corners[:, partner, corner_code[:, corner_index]]
        padded = padded.at[:, :, places[corner_index][0], places[corner_index][1]].set(picked)
    return padded

def im2col(padded, extent):
    pieces = [padded[:, row_tap:row_tap + extent, col_tap:col_tap + extent, :] for row_tap in range(3) for col_tap in range(3)]
    return jnp.concatenate(pieces, axis=-1)

def conv_all(padded, weights):
    flat = weights.reshape(-1, weights.shape[2])

    def single(block):
        extent = block.shape[1] - 2
        cols = im2col(block, extent).reshape(-1, flat.shape[0])
        result = jnp.dot(cols, flat, preferred_element_type=jnp.float32)
        return result.reshape(block.shape[0], extent, extent, flat.shape[1])
    result = lax.map(single, jnp.moveaxis(padded, 1, 0))
    return jnp.moveaxis(result, 0, 1)

def conv_back(grad, weights):
    gpadded = jnp.pad(grad, ((0, 0), (0, 0), (2, 2), (2, 2), (0, 0)))
    flipped = jnp.transpose(weights[::-1], (0, 2, 1))
    return conv_all(gpadded, flipped)

def weight_grad(padded, grad):
    channels = grad.shape[-1]

    def single(pair):
        block, gblock = pair
        extent = gblock.shape[1]
        cols = im2col(block, extent).reshape(-1, 9 * block.shape[-1])
        return jnp.dot(cols.T, gblock.reshape(-1, channels), preferred_element_type=jnp.float32)
    terms = lax.map(single, (jnp.moveaxis(padded, 1, 0), jnp.moveaxis(grad, 1, 0)))
    return lax.optimization_barrier(jnp.sum(terms, axis=0)).reshape(9, -1, channels)

def return_halo(dpadded, edge_code, corner_code):
    nsubs = dpadded.shape[1]
    extent = dpadded.shape[2] - 2
    interior = dpadded[:, :, 1:extent + 1, 1:extent + 1]
    rims = [dpadded[:, :, 0, 1:extent + 1], dpadded[:, :, 1:extent + 1, extent + 1], dpadded[:, :, extent + 1, 1:extent + 1], dpadded[:, :, 1:extent + 1, 0]]
    subtile_ids = jnp.arange(nsubs, dtype=jnp.int32)
    shape_all = (dpadded.shape[0], nsubs, 8, extent, dpadded.shape[-1])
    gathered = jnp.zeros(shape_all, jnp.float32)
    for edge_index, offset in enumerate(side_offsets()):
        partner = (subtile_ids + offset) % nsubs
        gathered = gathered.at[:, partner, edge_code[:, edge_index]].add(rims[edge_index])
    borders = gathered[:, :, :4] + gathered[:, :, 4:, ::-1]
    result = interior.at[:, :, 0].add(borders[:, :, 0])
    result = result.at[:, :, :, extent - 1].add(borders[:, :, 1])
    result = result.at[:, :, extent - 1].add(borders[:, :, 2])
    result = result.at[:, :, :, 0].add(borders[:, :, 3])
    places = ((0, 0), (0, extent + 1), (extent + 1, extent + 1), (extent + 1, 0))
    cgathered = jnp.zeros((dpadded.shape[0], nsubs, 4, dpadded.shape[-1]), jnp.float32)
    for corner_index, offset in enumerate(corner_offsets()):
        partner = (subtile_ids + offset) % nsubs
        values = dpadded[:, :, places[corner_index][0], places[corner_index][1]]
        cgathered = cgathered.at[:, partner, corner_code[:, corner_index]].add(values)
    result = result.at[:, :, 0, 0].add(cgathered[:, :, 0])
    result = result.at[:, :, 0, extent - 1].add(cgathered[:, :, 1])
    result = result.at[:, :, extent - 1, extent - 1].add(cgathered[:, :, 2])
    result = result.at[:, :, extent - 1, 0].add(cgathered[:, :, 3])
    return result

def gelu_slope(values):
    return jax.vjp(partial(jax.nn.gelu, approximate=True), values)[1](jnp.ones_like(values))[0]

def reference(inputs, weight_one, weight_two, cotangent, edge_code, corner_code):
    counted = inputs.shape[0] * inputs.shape[1] * inputs.shape[2] * inputs.shape[3]
    factor = 1.0 / math.sqrt(counted)
    x_margin = build_halo(inputs, edge_code, corner_code)
    pre_one = conv_all(x_margin, weight_one)
    hidden = jax.nn.gelu(pre_one, approximate=True).astype(jnp.bfloat16)
    h_margin = build_halo(hidden, edge_code, corner_code)
    pre_two = conv_all(h_margin, weight_two)
    output = (inputs.astype(jnp.float32) + pre_two).astype(jnp.bfloat16)
    dh_margin = conv_back(cotangent, weight_two)
    d_hidden = return_halo(dh_margin, edge_code, corner_code)
    d_pre = (d_hidden * gelu_slope(pre_one)).astype(jnp.bfloat16)
    grad_two = weight_grad(h_margin, cotangent) * factor
    dx_margin = conv_back(d_pre, weight_one)
    d_input = (cotangent.astype(jnp.float32) + return_halo(dx_margin, edge_code, corner_code)).astype(jnp.bfloat16)
    grad_one = weight_grad(x_margin, d_pre) * factor
    return (output, d_input, grad_one, grad_two)
```

```python
import math

import jax
import jax.numpy as jnp
from jax import lax
from jax.experimental import pallas as pl
from jax.experimental.pallas import tpu as pltpu
from jax.sharding import PartitionSpec as P

RW = 4
SIDES = (-RW, 1, RW, -1)
CORNERS = (-RW - 1, -RW + 1, RW + 1, RW - 1)
F32 = jnp.float32
BF16 = jnp.bfloat16
AXES = ("tile", "dp")
LIMIT = 48 * 1024 * 1024

BLOCKS = ((0, (0, 1)), (2, (3, 2)), (1, ()), (3, ()))


def block_rows(extent):
    return (extent + 16, extent + 16, extent, extent)


def block_starts(extent):
    rows = block_rows(extent)
    return (0, rows[0], rows[0] + rows[1], rows[0] + rows[1] + rows[2])


def block_taps(position):
    return ((0, 1, 2), (6, 7, 8), (2, 5, 8), (0, 3, 6))[position]


def routes(tiles):
    found = {}
    for kind, offsets in (("a", SIDES), ("b", SIDES), ("ac", CORNERS), ("bc", CORNERS)):
        for which, offset in enumerate(offsets):
            distance = (-offset if kind[0] == "a" else offset) % tiles
            found.setdefault(distance, []).append((kind, which))
    plan = []
    for distance, parts in found.items():
        sides = [p for p in parts if len(p[0]) == 1]
        corners = [p for p in parts if len(p[0]) == 2]
        plan.append((distance, sides, corners))
    return plan


def route_rows(route, extent):
    return extent * len(route[1]) + (16 if route[2] else 0)


def iota(shape, axis):
    return lax.broadcasted_iota(jnp.int32, shape, axis)


def dot(a, b):
    return lax.dot_general(a, b, (((1,), (0,)), ((), ())), preferred_element_type=F32)


def dot_t(a, b):
    return lax.dot_general(a, b, (((0,), (0,)), ((), ())), preferred_element_type=F32)


def corner_pixel(code, extent):
    last = extent - 1
    return jnp.where(code == 0, 0, jnp.where(code == 1, last, jnp.where(code == 2, extent * extent - 1, extent * last)))


def side_line(code, extent):
    last = extent - 1
    border = code % 4
    base = jnp.where(border == 1, last, jnp.where(border == 2, extent * last, 0))
    step = jnp.where(border % 2 == 0, 1, extent)
    return jnp.where(code >= 4, base + last * step, base), jnp.where(code >= 4, -step, step)


def seam_lines(edge_ref, corner_ref, extent):
    tiles = edge_ref.shape[0]
    mine = lax.axis_index("tile")
    lines = [side_line(edge_ref[(mine - o + tiles + RW * tiles) % tiles, k], extent) for k, o in enumerate(SIDES)]
    pixels = [corner_pixel(corner_ref[(mine - o + tiles + RW * tiles) % tiles, q], extent) for q, o in enumerate(CORNERS)]
    return lines, pixels


def fixed_lines(extent):
    last = extent - 1
    lines = [(0, 1), (last, extent), (extent * last, 1), (0, extent)]
    return lines, [0, last, extent * extent - 1, extent * last]


def pick_rows(indices, count):
    return (iota((indices.shape[0], count), 1) == indices).astype(F32).astype(BF16)


def line_rows(line, extent, count):
    return pick_rows(line[0] + line[1] * iota((extent, 1), 0), count)


def spot_rows(spots, count):
    rows = iota((16, 1), 0)
    index = jnp.full((16, 1), -1, jnp.int32)
    for row, pixel in spots:
        index = jnp.where(rows == row, pixel, index)
    return pick_rows(index, count)


def gather_block(image, position, lines, pixels, extent):
    side, corners = BLOCKS[position]
    count = image.shape[0]
    rows = line_rows(lines[side], extent, count)
    if corners:
        rows = jnp.concatenate([rows, spot_rows([(i, pixels[q]) for i, q in enumerate(corners)], count)], axis=0)
    return dot(rows, image).astype(BF16)


def gather_blocks(image, lines, pixels, extent):
    return [gather_block(image, i, lines, pixels, extent) for i in range(4)]


def write_routes(a_blocks, b_blocks, plan, out_refs, extent):
    side_at = {side: i for i, (side, _) in enumerate(BLOCKS)}
    corner_at = {q: (i, extent + j) for i, (_, corners) in enumerate(BLOCKS) for j, q in enumerate(corners)}
    for route, out in zip(plan, out_refs):
        at = 0
        for kind, side in route[1]:
            blocks = a_blocks if kind == "a" else b_blocks
            out[at : at + extent, :] = blocks[side_at[side]][:extent]
            at += extent
        if route[2]:
            rows = iota((16, 1), 0)
            tile = jnp.zeros((16, out.shape[1]), F32)
            for i, (kind, q) in enumerate(route[2]):
                block, row = corner_at[q]
                source = (a_blocks if kind == "ac" else b_blocks)[block][extent : extent + 16].astype(F32)
                tile = jnp.where(rows == i, source[row - extent : row - extent + 1], tile)
            out[at : at + 16, :] = tile.astype(BF16)


def read_routes(plan, in_refs, extent):
    sides, corners = {}, {}
    for route, ref in zip(plan, in_refs):
        at = 0
        for key in route[1]:
            sides[key] = ref[at : at + extent, :]
            at += extent
        if route[2]:
            tile = ref[at : at + 16, :].astype(F32)
            for i, key in enumerate(route[2]):
                corners[key] = tile[i : i + 1]
    result = []
    rows = iota((16, 1), 0)
    for kind in ("a", "b"):
        blocks = []
        for side, ends in BLOCKS:
            block = sides[(kind, side)]
            if ends:
                tile = jnp.zeros((16, block.shape[1]), F32)
                for i, q in enumerate(ends):
                    tile = jnp.where(rows == i, corners[(kind + "c", q)], tile)
                block = jnp.concatenate([block, tile.astype(BF16)], axis=0)
            blocks.append(block)
        result.append(blocks)
    return result


def shifted(image, by, extent):
    if by == 0:
        return image
    column = iota((image.shape[0], 1), 0) % extent
    rolled = pltpu.roll(image, (-by) % image.shape[0], 0)
    return jnp.where(column == (extent - 1 if by == 1 else 0), 0.0, rolled)


def write_columns(q_ref, image, forward, extent):
    count, channels = image.shape
    zero = jnp.zeros((extent, q_ref.shape[1]), BF16)
    q_ref[0:extent, :] = zero
    q_ref[extent + count : 2 * extent + count, :] = zero
    wide = image.astype(F32)
    for b in range(3):
        by = b - 1 if forward else 1 - b
        q_ref[extent : extent + count, b * channels : (b + 1) * channels] = shifted(wide, by, extent).astype(BF16)


def window_product(q_ref, weight, forward, extent, chunk=256):
    count = q_ref.shape[0] - 2 * extent
    pieces = []
    for start in range(0, count, chunk):
        rows = [q_ref[(a if forward else 2 - a) * extent + start : (a if forward else 2 - a) * extent + start + chunk, :] for a in range(3)]
        pieces.append(dot(jnp.concatenate(rows, axis=1), weight))
    return jnp.concatenate(pieces, axis=0)


def tap_weight(weight, taps, channels):
    return jnp.concatenate([weight[t * channels : (t + 1) * channels, :] for t in taps], axis=0)


def halves(values):
    high = values.astype(BF16)
    return high, (values - high.astype(F32)).astype(BF16)


def margin_forward(strips, weight, extent):
    channels = strips[0].shape[1]
    count = extent * extent
    adds = []
    for position, (side, ends) in enumerate(BLOCKS):
        middle = strips[position][:extent].astype(F32)
        row = iota((extent, 1), 0)
        before, after = 0.0, 0.0
        if ends:
            tile = strips[position][extent : extent + 16].astype(F32)
            before, after = tile[0:1], tile[1:2]
        left = jnp.where(row == 0, before, pltpu.roll(middle, 1, 0))
        right = jnp.where(row == extent - 1, after, pltpu.roll(middle, extent - 1, 0))
        columns = jnp.concatenate([left, middle, right], axis=1).astype(BF16)
        adds.append(dot(columns, tap_weight(weight, block_taps(position), channels)))
    spread = jnp.concatenate(list(halves(adds[2])) + list(halves(adds[3])), axis=0)
    lane = iota((1, 4 * extent), 1)
    target = (lane % extent) * extent + jnp.where(lane < 2 * extent, extent - 1, 0)
    image = dot((iota((count, 1), 0) == target).astype(F32).astype(BF16), spread)
    top = image[:extent] + adds[0]
    bottom = image[count - extent :] + adds[1]
    return jnp.concatenate([top, image[extent : count - extent], bottom], axis=0)


def strip_columns(strips, extent):
    result = []
    for position, (side, ends) in enumerate(BLOCKS):
        middle = strips[position][:extent].astype(F32)
        row = iota((extent, 1), 0)
        after = jnp.where(row == extent - 1, 0.0, pltpu.roll(middle, extent - 1, 0))
        before = jnp.where(row == 0, 0.0, pltpu.roll(middle, 1, 0))
        columns = jnp.concatenate([after, middle, before], axis=1)
        if ends:
            tile = strips[position][extent : extent + 16].astype(F32)
            row = iota((16, 1), 0)
            low = jnp.where(row == 0, tile, 0.0)
            high = jnp.where(row == 1, tile, 0.0)
            columns = jnp.concatenate([columns, jnp.concatenate([low, jnp.zeros_like(tile), high], axis=1)], axis=0)
        result.append(columns.astype(BF16))
    return result


def margin_backward(columns, weight_t, lines, pixels, extent):
    channels = weight_t.shape[1]
    count = extent * extent
    adds = [dot(columns[i], tap_weight(weight_t, block_taps(i), channels)) for i in range(4)]
    stacked = jnp.concatenate(adds, axis=0)
    total = stacked.shape[0]
    lane = iota((1, total), 1)
    index = jnp.full((1, total), -1, jnp.int32)
    for start, (side, ends) in zip(block_starts(extent), BLOCKS):
        base, step = lines[side]
        index = jnp.where((lane >= start) & (lane < start + extent), base + step * (lane - start), index)
        for i, q in enumerate(ends):
            index = jnp.where(lane == start + extent + i, pixels[q], index)
    scatter = (iota((count, 1), 0) == index).astype(F32).astype(BF16)
    high, low = halves(stacked)
    return dot(scatter, high) + dot(scatter, low)


def weight_sum(out_ref, image_t, q_ref, strips, columns, extent):
    channels = image_t.shape[0]
    count = image_t.shape[1]
    wide = [dot_t(strips[i], columns[i]) for i in range(4)]
    for a in range(3):
        rows = q_ref[(2 - a) * extent : (2 - a) * extent + count, :]
        product = dot(image_t, rows)
        for b in range(3):
            tap = 3 * a + b
            value = product[:, b * channels : (b + 1) * channels]
            for position in range(4):
                taps = block_taps(position)
                if tap in taps:
                    at = taps.index(tap)
                    value = value + wide[position][:, at * channels : (at + 1) * channels]
            out_ref[tap * channels : (tap + 1) * channels, :] = value


def transpose_taps(out_ref, weight_ref):
    channels = out_ref.shape[1]
    for tap in range(9):
        block = weight_ref[tap * channels : (tap + 1) * channels, :]
        out_ref[tap * channels : (tap + 1) * channels, :] = jnp.transpose(block.astype(F32)).astype(BF16)


def gelu_parts(u):
    scale = math.sqrt(2.0 / math.pi)
    square = u * u
    t = jnp.tanh(scale * (u + 0.044715 * (square * u)))
    value = 0.5 * u * (1.0 + t)
    slope = 0.5 * (1.0 + t) + (0.5 * u) * (1.0 - t * t) * (scale * (1.0 + 3.0 * 0.044715 * square))
    return value, slope


def call(kernel, name, outs, ins, operands, scratch=(), flops=0):
    specs = [pl.BlockSpec(memory_space=pltpu.SMEM if i == "s" else pltpu.VMEM) for i in ins]
    moved = sum(math.prod(o.shape) * o.dtype.itemsize for o in list(outs) + list(operands))
    return pl.pallas_call(
        kernel,
        name=name,
        out_shape=outs,
        in_specs=specs,
        out_specs=[pl.BlockSpec(memory_space=pltpu.VMEM) for _ in outs],
        scratch_shapes=list(scratch),
        cost_estimate=pl.CostEstimate(flops=flops, bytes_accessed=moved, transcendentals=0),
        compiler_params=pltpu.CompilerParams(vmem_limit_bytes=LIMIT),
    )(*operands)


def sds(shape, dtype):
    return jax.ShapeDtypeStruct(shape, dtype)


def exchange(payloads, plan, tiles):
    return [
        lax.ppermute(p, "tile", [(i, (i + route[0]) % tiles) for i in range(tiles)]) for p, route in zip(payloads, plan)
    ]


def swap(value, mask, total):
    return lax.ppermute(value, AXES, [(i, i ^ mask) for i in range(total)])


def reduce_gradients(keep, send, total):
    rows, channels = keep.shape
    wire = BF16 if total <= 32 else F32
    me = lax.axis_index(AXES)
    own = keep + swap(send, 1, total).astype(F32)
    plane = (me >> 1) & 3
    parts = own.reshape(4, rows // 4, channels)
    sent = parts.astype(wire)
    arrived = [
        swap(lax.dynamic_index_in_dim(sent, plane ^ m, 0, keepdims=False), m << 1, total).astype(F32) for m in (3, 1, 2)
    ]
    part = lax.dynamic_index_in_dim(parts, plane, 0, keepdims=False)
    part = part + arrived[0] + arrived[1] + arrived[2]
    bit = 8
    while bit < total:
        mine = part.astype(wire)
        if 2 * bit < total:
            far, middle, near = [swap(mine, m * bit, total).astype(F32) for m in (3, 2, 1)]
            part = (mine.astype(F32) + near) + (middle + far)
            bit *= 4
        else:
            part = mine.astype(F32) + swap(mine, bit, total).astype(F32)
            bit *= 2
    mine = part.astype(wire)
    ring = jnp.stack([mine] + [swap(mine, m << 1, total) for m in (1, 2, 3)])
    whole = jnp.concatenate([lax.dynamic_index_in_dim(ring, plane ^ j, 0) for j in range(4)], axis=0)
    other = swap(whole, 1, total)
    first = (me & 1) == 0
    return jnp.where(first, whole, other), jnp.where(first, other, whole)


def per_device(inputs, weight_one, weight_two, cotangent, edge_code, corner_code):
    tiles, members = lax.axis_size("tile"), lax.axis_size("dp")
    extent, channels = inputs.shape[2], inputs.shape[4]
    count = extent * extent
    factor = 1.0 / math.sqrt(inputs.shape[0] * members * tiles * count)
    source = inputs.reshape(count, channels)
    grad_out = cotangent.reshape(count, channels)
    w_one = weight_one.reshape(9 * channels, channels)
    w_two = weight_two.reshape(9 * channels, channels)
    plan = routes(tiles)
    routed = [sds((route_rows(r, extent), channels), BF16) for r in plan]
    n_routes = len(plan)
    image_b, image_f = sds((count, channels), BF16), sds((count, channels), F32)
    columns_b = sds((count + 2 * extent, 3 * channels), BF16)
    taps_b, taps_f = sds((9 * channels, channels), BF16), sds((9 * channels, channels), F32)
    turned_b = sds((channels, count), BF16)
    conv = 2 * count * 9 * channels * channels

    def first_strips(edge_ref, corner_ref, x_ref, g_ref, *outs):
        lines, pixels = seam_lines(edge_ref, corner_ref, extent)
        a = gather_blocks(x_ref[...], lines, pixels, extent)
        b = gather_blocks(g_ref[...], *fixed_lines(extent), extent)
        write_routes(a, b, plan, outs, extent)

    first = call(first_strips, "first_strips", routed, "ssvv", (edge_code, corner_code, source, grad_out))
    first_arrived = exchange(first, plan, tiles)

    def inner(x_ref, g_ref, w1_ref, w2_ref, pre_ref, dh_ref, xt_ref, qg_ref, w1t_ref, w2t_ref, qx_ref):
        transpose_taps(w1t_ref, w1_ref)
        transpose_taps(w2t_ref, w2_ref)
        write_columns(qx_ref, x_ref[...], True, extent)
        pre_ref[...] = window_product(qx_ref, w1_ref[...], True, extent)
        write_columns(qg_ref, g_ref[...], False, extent)
        dh_ref[...] = window_product(qg_ref, w2t_ref[...], False, extent)
        xt_ref[...] = jnp.transpose(x_ref[...].astype(F32)).astype(BF16)

    pre, dh, xt, qg, w1t, w2t = call(
        inner,
        "inner_products",
        [image_f, image_f, turned_b, columns_b, taps_b, taps_b],
        "vvvv",
        (source, grad_out, w_one, w_two),
        scratch=[pltpu.VMEM(columns_b.shape, BF16)],
        flops=2 * conv,
    )

    def middle(edge_ref, corner_ref, pre_ref, dh_ref, xt_ref, qg_ref, w1_ref, w2t_ref, *refs):
        arrived = refs[:n_routes]
        keep_ref, send_ref, hid_ref, dpre_ref = refs[n_routes : n_routes + 4]
        outs = refs[n_routes + 4 : 2 * n_routes + 4]
        qd_ref, sum_ref = refs[2 * n_routes + 4 :]
        lines, pixels = seam_lines(edge_ref, corner_ref, extent)
        x_strips, g_strips = read_routes(plan, arrived, extent)
        columns = strip_columns(g_strips, extent)
        value, slope = gelu_parts(pre_ref[...] + margin_forward(x_strips, w1_ref[...], extent))
        hidden = value.astype(BF16)
        hid_ref[...] = hidden
        d_hidden = dh_ref[...] + margin_backward(columns, w2t_ref[...], lines, pixels, extent)
        d_pre = (d_hidden * slope).astype(BF16)
        dpre_ref[...] = d_pre
        a = gather_blocks(hidden, lines, pixels, extent)
        b = gather_blocks(d_pre, *fixed_lines(extent), extent)
        write_routes(a, b, plan, outs, extent)
        write_columns(qd_ref, d_pre, False, extent)
        weight_sum(sum_ref.at[0], xt_ref[...], qd_ref, x_strips, strip_columns(b, extent), extent)
        weight_sum(sum_ref.at[1], jnp.transpose(value).astype(BF16), qg_ref, a, columns, extent)
        core = lax.axis_index("dp") % 2
        keep_ref[...] = sum_ref[core]
        send_ref[...] = sum_ref[1 - core].astype(BF16)

    results = call(
        middle,
        "gradients",
        [taps_f, taps_b, image_b, image_b] + routed,
        "ss" + "v" * (6 + n_routes),
        (edge_code, corner_code, pre, dh, xt, qg, w_one, w2t, *first_arrived),
        scratch=[pltpu.VMEM(columns_b.shape, BF16), pltpu.VMEM((2,) + taps_f.shape, F32)],
        flops=2 * conv,
    )
    keep, send, hidden, d_pre = results[:4]
    second_arrived = exchange(results[4:], plan, tiles)

    def last(edge_ref, corner_ref, x_ref, g_ref, hid_ref, dpre_ref, w2_ref, w1t_ref, *refs):
        arrived = refs[:n_routes]
        out_ref, dx_ref, q_ref = refs[n_routes:]
        lines, pixels = seam_lines(edge_ref, corner_ref, extent)
        h_strips, d_strips = read_routes(plan, arrived, extent)
        write_columns(q_ref, hid_ref[...], True, extent)
        total = window_product(q_ref, w2_ref[...], True, extent) + margin_forward(h_strips, w2_ref[...], extent)
        out_ref[...] = (x_ref[...].astype(F32) + total).astype(BF16)
        write_columns(q_ref, dpre_ref[...], False, extent)
        total = window_product(q_ref, w1t_ref[...], False, extent)
        total = total + margin_backward(strip_columns(d_strips, extent), w1t_ref[...], lines, pixels, extent)
        dx_ref[...] = (g_ref[...].astype(F32) + total).astype(BF16)

    output, d_input = call(
        last,
        "outputs",
        [image_b, image_b],
        "ss" + "v" * (6 + n_routes),
        (edge_code, corner_code, source, grad_out, hidden, d_pre, w_two, w1t, *second_arrived),
        scratch=[pltpu.VMEM(columns_b.shape, BF16)],
        flops=2 * conv,
    )
    one, two = reduce_gradients(keep, send, tiles * members)
    shape = (9, channels, channels)
    return (
        output.reshape(inputs.shape),
        d_input.reshape(inputs.shape),
        (one.astype(F32) * factor).reshape(shape),
        (two.astype(F32) * factor).reshape(shape),
    )


def solution(mesh):
    split = P("dp", "tile", None, None, None)
    return jax.shard_map(
        per_device,
        mesh=mesh,
        in_specs=(split, P(), P(), split, P(), P()),
        out_specs=(split, split, P(), P()),
        check_vma=False,
    )
```

```python
import math

import jax
import jax.numpy as jnp
from jax import lax
from jax.experimental import pallas as pl
from jax.experimental.pallas import tpu as pltpu
from jax.sharding import PartitionSpec as P

RW = 4
SIDES = (-RW, 1, RW, -1)
CORNERS = (-RW - 1, -RW + 1, RW + 1, RW - 1)
F32 = jnp.float32
BF16 = jnp.bfloat16
AXES = ("tile", "dp")
LIMIT = 48 * 1024 * 1024

BLOCKS = ((0, (0, 1)), (2, (3, 2)), (1, ()), (3, ()))


def block_rows(extent):
    return (extent + 16, extent + 16, extent, extent)


def block_starts(extent):
    rows = block_rows(extent)
    return (0, rows[0], rows[0] + rows[1], rows[0] + rows[1] + rows[2])


def block_taps(position):
    return ((0, 1, 2), (6, 7, 8), (2, 5, 8), (0, 3, 6))[position]


def routes(tiles):
    found = {}
    for kind, offsets in (("a", SIDES), ("b", SIDES), ("ac", CORNERS), ("bc", CORNERS)):
        for which, offset in enumerate(offsets):
            distance = (-offset if kind[0] == "a" else offset) % tiles
            found.setdefault(distance, []).append((kind, which))
    plan = []
    for distance, parts in found.items():
        sides = [p for p in parts if len(p[0]) == 1]
        corners = [p for p in parts if len(p[0]) == 2]
        plan.append((distance, sides, corners))
    return plan


def route_rows(route, extent):
    return extent * len(route[1]) + (16 if route[2] else 0)


def iota(shape, axis):
    return lax.broadcasted_iota(jnp.int32, shape, axis)


def dot(a, b):
    return lax.dot_general(a, b, (((1,), (0,)), ((), ())), preferred_element_type=F32)


def dot_t(a, b):
    return lax.dot_general(a, b, (((0,), (0,)), ((), ())), preferred_element_type=F32)


def corner_pixel(code, extent):
    last = extent - 1
    return jnp.where(code == 0, 0, jnp.where(code == 1, last, jnp.where(code == 2, extent * extent - 1, extent * last)))


def side_line(code, extent):
    last = extent - 1
    border = code % 4
    base = jnp.where(border == 1, last, jnp.where(border == 2, extent * last, 0))
    step = jnp.where(border % 2 == 0, 1, extent)
    return jnp.where(code >= 4, base + last * step, base), jnp.where(code >= 4, -step, step)


def seam_lines(edge_ref, corner_ref, extent):
    tiles = edge_ref.shape[0]
    mine = lax.axis_index("tile")
    lines = [side_line(edge_ref[(mine - o + tiles + RW * tiles) % tiles, k], extent) for k, o in enumerate(SIDES)]
    pixels = [corner_pixel(corner_ref[(mine - o + tiles + RW * tiles) % tiles, q], extent) for q, o in enumerate(CORNERS)]
    return lines, pixels


def fixed_lines(extent):
    last = extent - 1
    lines = [(0, 1), (last, extent), (extent * last, 1), (0, extent)]
    return lines, [0, last, extent * extent - 1, extent * last]


def pick_rows(indices, count):
    return (iota((indices.shape[0], count), 1) == indices).astype(F32).astype(BF16)


def line_rows(line, extent, count):
    return pick_rows(line[0] + line[1] * iota((extent, 1), 0), count)


def spot_rows(spots, count):
    rows = iota((16, 1), 0)
    index = jnp.full((16, 1), -1, jnp.int32)
    for row, pixel in spots:
        index = jnp.where(rows == row, pixel, index)
    return pick_rows(index, count)


def gather_block(image, position, lines, pixels, extent):
    side, corners = BLOCKS[position]
    count = image.shape[0]
    rows = line_rows(lines[side], extent, count)
    if corners:
        rows = jnp.concatenate([rows, spot_rows([(i, pixels[q]) for i, q in enumerate(corners)], count)], axis=0)
    return dot(rows, image).astype(BF16)


def gather_blocks(image, lines, pixels, extent):
    return [gather_block(image, i, lines, pixels, extent) for i in range(4)]


def write_routes(a_blocks, b_blocks, plan, out_refs, extent):
    side_at = {side: i for i, (side, _) in enumerate(BLOCKS)}
    corner_at = {q: (i, extent + j) for i, (_, corners) in enumerate(BLOCKS) for j, q in enumerate(corners)}
    for route, out in zip(plan, out_refs):
        at = 0
        for kind, side in route[1]:
            blocks = a_blocks if kind == "a" else b_blocks
            out[at : at + extent, :] = blocks[side_at[side]][:extent]
            at += extent
        if route[2]:
            rows = iota((16, 1), 0)
            tile = jnp.zeros((16, out.shape[1]), F32)
            for i, (kind, q) in enumerate(route[2]):
                block, row = corner_at[q]
                source = (a_blocks if kind == "ac" else b_blocks)[block][extent : extent + 16].astype(F32)
                tile = jnp.where(rows == i, source[row - extent : row - extent + 1], tile)
            out[at : at + 16, :] = tile.astype(BF16)


def read_routes(plan, in_refs, extent):
    sides, corners = {}, {}
    for route, ref in zip(plan, in_refs):
        at = 0
        for key in route[1]:
            sides[key] = ref[at : at + extent, :]
            at += extent
        if route[2]:
            tile = ref[at : at + 16, :].astype(F32)
            for i, key in enumerate(route[2]):
                corners[key] = tile[i : i + 1]
    result = []
    rows = iota((16, 1), 0)
    for kind in ("a", "b"):
        blocks = []
        for side, ends in BLOCKS:
            block = sides[(kind, side)]
            if ends:
                tile = jnp.zeros((16, block.shape[1]), F32)
                for i, q in enumerate(ends):
                    tile = jnp.where(rows == i, corners[(kind + "c", q)], tile)
                block = jnp.concatenate([block, tile.astype(BF16)], axis=0)
            blocks.append(block)
        result.append(blocks)
    return result


def relayed(tiles):
    return tiles == 8


def write_relay(a_blocks, b_blocks, near_ref, far_ref, extent):
    for i, block in enumerate((a_blocks[2], a_blocks[3], b_blocks[2], b_blocks[3])):
        near_ref[i * extent : (i + 1) * extent, :] = block
    for i, block in enumerate((a_blocks[0], a_blocks[1], b_blocks[0], b_blocks[1])):
        far_ref[i * extent : (i + 1) * extent, :] = block[:extent]
    rows = iota((16, 1), 0)
    tile = jnp.zeros((16, near_ref.shape[1]), F32)
    at = 0
    for blocks in (a_blocks, b_blocks):
        ends = [blocks[i][extent : extent + 16].astype(F32) for i in range(2)]
        for block, row in ((0, 0), (0, 1), (1, 1), (1, 0)):
            tile = jnp.where(rows == at, ends[block][row : row + 1], tile)
            at += 1
    near_ref[4 * extent : 4 * extent + 16, :] = tile.astype(BF16)


def read_relay(refs, extent):
    across, one, three, far, opposite = refs
    mine = lax.axis_index("tile")
    left = mine % 2 == 0
    even = (mine // 2) % 2 == 0

    def pick(first, second, start, count):
        whole = [r[start : start + count, :].astype(F32) for r in (across, one, three)]
        above = jnp.where(even, whole[1], whole[2])
        below = jnp.where(even, whole[2], whole[1])
        return jnp.where(left, {"across": whole[0], "above": above, "below": below}[first], {"across": whole[0], "above": above, "below": below}[second])

    def side(i, first, second):
        return pick(first, second, i * extent, extent).astype(BF16)

    a_east, b_west = side(0, "across", "above"), side(3, "across", "above")
    a_west, b_east = side(1, "below", "across"), side(2, "below", "across")
    beside = pick("above", "below", 4 * extent, 16)
    beyond = opposite[0:16, :].astype(F32)
    third = jnp.where(left, beside, beyond)
    fifth = jnp.where(left, beyond, beside)
    corners = {("a", 0): third[0:1], ("a", 3): third[3:4], ("b", 1): third[5:6], ("b", 2): third[6:7]}
    corners.update({("a", 1): fifth[1:2], ("a", 2): fifth[2:3], ("b", 0): fifth[4:5], ("b", 3): fifth[7:8]})
    rows = iota((16, 1), 0)
    result = []
    for kind, first, east, west in (("a", 0, a_east, a_west), ("b", 2, b_east, b_west)):
        blocks = []
        for i, ends in enumerate(((0, 1), (3, 2))):
            tile = jnp.where(rows == 0, corners[(kind, ends[0])], jnp.where(rows == 1, corners[(kind, ends[1])], 0.0))
            strip = far[(first + i) * extent : (first + i + 1) * extent, :]
            blocks.append(jnp.concatenate([strip, tile.astype(BF16)], axis=0))
        result.append(blocks + [east, west])
    return result


def shifted(image, by, extent):
    if by == 0:
        return image
    column = iota((image.shape[0], 1), 0) % extent
    rolled = pltpu.roll(image, (-by) % image.shape[0], 0)
    return jnp.where(column == (extent - 1 if by == 1 else 0), 0.0, rolled)


def write_columns(q_ref, image, forward, extent):
    count, channels = image.shape
    zero = jnp.zeros((extent, q_ref.shape[1]), BF16)
    q_ref[0:extent, :] = zero
    q_ref[extent + count : 2 * extent + count, :] = zero
    wide = image.astype(F32)
    for b in range(3):
        by = b - 1 if forward else 1 - b
        q_ref[extent : extent + count, b * channels : (b + 1) * channels] = shifted(wide, by, extent).astype(BF16)


def window_product(q_ref, weight, forward, extent, chunk=256):
    count = q_ref.shape[0] - 2 * extent
    pieces = []
    for start in range(0, count, chunk):
        rows = [q_ref[(a if forward else 2 - a) * extent + start : (a if forward else 2 - a) * extent + start + chunk, :] for a in range(3)]
        pieces.append(dot(jnp.concatenate(rows, axis=1), weight))
    return jnp.concatenate(pieces, axis=0)


def tap_weight(weight, taps, channels):
    return jnp.concatenate([weight[t * channels : (t + 1) * channels, :] for t in taps], axis=0)


def halves(values):
    high = values.astype(BF16)
    return high, (values - high.astype(F32)).astype(BF16)


def margin_forward(strips, weight, extent):
    channels = strips[0].shape[1]
    count = extent * extent
    adds = []
    for position, (side, ends) in enumerate(BLOCKS):
        middle = strips[position][:extent].astype(F32)
        row = iota((extent, 1), 0)
        before, after = 0.0, 0.0
        if ends:
            tile = strips[position][extent : extent + 16].astype(F32)
            before, after = tile[0:1], tile[1:2]
        left = jnp.where(row == 0, before, pltpu.roll(middle, 1, 0))
        right = jnp.where(row == extent - 1, after, pltpu.roll(middle, extent - 1, 0))
        columns = jnp.concatenate([left, middle, right], axis=1).astype(BF16)
        adds.append(dot(columns, tap_weight(weight, block_taps(position), channels)))
    spread = jnp.concatenate(list(halves(adds[2])) + list(halves(adds[3])), axis=0)
    lane = iota((1, 4 * extent), 1)
    target = (lane % extent) * extent + jnp.where(lane < 2 * extent, extent - 1, 0)
    image = dot((iota((count, 1), 0) == target).astype(F32).astype(BF16), spread)
    top = image[:extent] + adds[0]
    bottom = image[count - extent :] + adds[1]
    return jnp.concatenate([top, image[extent : count - extent], bottom], axis=0)


def strip_columns(strips, extent):
    result = []
    for position, (side, ends) in enumerate(BLOCKS):
        middle = strips[position][:extent].astype(F32)
        row = iota((extent, 1), 0)
        after = jnp.where(row == extent - 1, 0.0, pltpu.roll(middle, extent - 1, 0))
        before = jnp.where(row == 0, 0.0, pltpu.roll(middle, 1, 0))
        columns = jnp.concatenate([after, middle, before], axis=1)
        if ends:
            tile = strips[position][extent : extent + 16].astype(F32)
            row = iota((16, 1), 0)
            low = jnp.where(row == 0, tile, 0.0)
            high = jnp.where(row == 1, tile, 0.0)
            columns = jnp.concatenate([columns, jnp.concatenate([low, jnp.zeros_like(tile), high], axis=1)], axis=0)
        result.append(columns.astype(BF16))
    return result


def margin_backward(columns, weight_t, lines, pixels, extent):
    channels = weight_t.shape[1]
    count = extent * extent
    adds = [dot(columns[i], tap_weight(weight_t, block_taps(i), channels)) for i in range(4)]
    stacked = jnp.concatenate(adds, axis=0)
    total = stacked.shape[0]
    lane = iota((1, total), 1)
    index = jnp.full((1, total), -1, jnp.int32)
    for start, (side, ends) in zip(block_starts(extent), BLOCKS):
        base, step = lines[side]
        index = jnp.where((lane >= start) & (lane < start + extent), base + step * (lane - start), index)
        for i, q in enumerate(ends):
            index = jnp.where(lane == start + extent + i, pixels[q], index)
    scatter = (iota((count, 1), 0) == index).astype(F32).astype(BF16)
    high, low = halves(stacked)
    return dot(scatter, high) + dot(scatter, low)


def weight_sum(out_ref, image_t, q_ref, strips, columns, extent):
    channels = image_t.shape[0]
    count = image_t.shape[1]
    wide = [dot_t(strips[i], columns[i]) for i in range(4)]
    for a in range(3):
        rows = q_ref[(2 - a) * extent : (2 - a) * extent + count, :]
        product = dot(image_t, rows)
        for b in range(3):
            tap = 3 * a + b
            value = product[:, b * channels : (b + 1) * channels]
            for position in range(4):
                taps = block_taps(position)
                if tap in taps:
                    at = taps.index(tap)
                    value = value + wide[position][:, at * channels : (at + 1) * channels]
            out_ref[tap * channels : (tap + 1) * channels, :] = value


def transpose_taps(out_ref, weight_ref):
    channels = out_ref.shape[1]
    for tap in range(9):
        block = weight_ref[tap * channels : (tap + 1) * channels, :]
        out_ref[tap * channels : (tap + 1) * channels, :] = jnp.transpose(block.astype(F32)).astype(BF16)


def gelu_parts(u):
    scale = math.sqrt(2.0 / math.pi)
    square = u * u
    t = jnp.tanh(scale * (u + 0.044715 * (square * u)))
    value = 0.5 * u * (1.0 + t)
    slope = 0.5 * (1.0 + t) + (0.5 * u) * (1.0 - t * t) * (scale * (1.0 + 3.0 * 0.044715 * square))
    return value, slope


def call(kernel, name, outs, ins, operands, scratch=(), flops=0):
    specs = [pl.BlockSpec(memory_space=pltpu.SMEM if i == "s" else pltpu.VMEM) for i in ins]
    moved = sum(math.prod(o.shape) * o.dtype.itemsize for o in list(outs) + list(operands))
    return pl.pallas_call(
        kernel,
        name=name,
        out_shape=outs,
        in_specs=specs,
        out_specs=[pl.BlockSpec(memory_space=pltpu.VMEM) for _ in outs],
        scratch_shapes=list(scratch),
        cost_estimate=pl.CostEstimate(flops=flops, bytes_accessed=moved, transcendentals=0),
        compiler_params=pltpu.CompilerParams(vmem_limit_bytes=LIMIT),
    )(*operands)


def sds(shape, dtype):
    return jax.ShapeDtypeStruct(shape, dtype)


def exchange(payloads, plan, tiles):
    return [
        lax.ppermute(p, "tile", [(i, (i + route[0]) % tiles) for i in range(tiles)]) for p, route in zip(payloads, plan)
    ]


def swap(value, mask, total):
    return lax.ppermute(value, AXES, [(i, i ^ mask) for i in range(total)])


def reduce_gradients(keep, send, total, near=None, far=None):
    rows, channels = keep.shape
    quarter = rows // 4
    wire = BF16 if total <= 32 else F32
    me = lax.axis_index(AXES)
    own = keep + swap(send, 1, total).astype(F32)
    plane = (me >> 1) & 3
    parts = own.reshape(4, quarter, channels)
    sent = parts.astype(wire)
    arrived = {}
    for m in (3, 1, 2):
        message = lax.dynamic_index_in_dim(sent, plane ^ m, 0, keepdims=False)
        if m == 2 and near is not None:
            message = jnp.concatenate([message, near], axis=0)
        arrived[m] = swap(message, m << 1, total)
    part = lax.dynamic_index_in_dim(parts, plane, 0, keepdims=False)
    for m in (3, 1, 2):
        part = part + arrived[m][:quarter].astype(F32)
    extras = None
    if near is not None:
        across = arrived[2][quarter:]
        riders = {1: (across,), 2: (far, across[-16:]), 3: (across,)}
    bit = 8
    while bit < total:
        mine = part.astype(wire)
        if 2 * bit < total:
            got = {}
            for m in (3, 2, 1):
                message = mine
                if near is not None:
                    message = jnp.concatenate([mine, *riders[m]], axis=0)
                got[m] = swap(message, m * bit, total)
            part = (mine.astype(F32) + got[1][:quarter].astype(F32)) + (got[2][:quarter].astype(F32) + got[3][:quarter].astype(F32))
            if near is not None:
                extras = [across, got[1][quarter:], got[3][quarter:], got[2][quarter:-16], got[2][-16:]]
            bit *= 4
        else:
            part = mine.astype(F32) + swap(mine, bit, total).astype(F32)
            bit *= 2
    mine = part.astype(wire)
    ring = jnp.stack([mine] + [swap(mine, m << 1, total) for m in (1, 2, 3)])
    whole = jnp.concatenate([lax.dynamic_index_in_dim(ring, plane ^ j, 0) for j in range(4)], axis=0)
    return whole, extras


def join_cores(whole, total):
    other = swap(whole, 1, total)
    low = (lax.axis_index(AXES) & 1) == 0
    return jnp.where(low, whole, other), jnp.where(low, other, whole)


def relay(near, far, total):
    across = swap(near, 4, total)
    three = swap(across, 24, total)
    two = swap(jnp.concatenate([far, across[-16:]], axis=0), 16, total)
    one = swap(across, 8, total)
    return [across, one, three, two[:-16], two[-16:]]


def relay_direct(near, far, total):
    return [swap(near, 4, total), swap(near, 12, total), swap(near, 28, total), swap(far, 16, total), swap(near[-16:], 20, total)]


def per_device(inputs, weight_one, weight_two, cotangent, edge_code, corner_code):
    tiles, members = lax.axis_size("tile"), lax.axis_size("dp")
    extent, channels = inputs.shape[2], inputs.shape[4]
    count = extent * extent
    factor = 1.0 / math.sqrt(inputs.shape[0] * members * tiles * count)
    source = inputs.reshape(count, channels)
    grad_out = cotangent.reshape(count, channels)
    w_one = weight_one.reshape(9 * channels, channels)
    w_two = weight_two.reshape(9 * channels, channels)
    plan = routes(tiles)
    total = tiles * members
    hops = relayed(tiles)
    if hops:
        routed = [sds((4 * extent + 16, channels), BF16), sds((4 * extent, channels), BF16)]
        n_routes = 5
    else:
        routed = [sds((route_rows(r, extent), channels), BF16) for r in plan]
        n_routes = len(plan)
    n_routed = len(routed)

    def write(a, b, outs):
        if hops:
            write_relay(a, b, *outs, extent)
        else:
            write_routes(a, b, plan, outs, extent)

    def read(refs):
        return read_relay(refs, extent) if hops else read_routes(plan, refs, extent)

    image_b, image_f = sds((count, channels), BF16), sds((count, channels), F32)
    columns_b = sds((count + 2 * extent, 3 * channels), BF16)
    taps_b, taps_f = sds((9 * channels, channels), BF16), sds((9 * channels, channels), F32)
    turned_b = sds((channels, count), BF16)
    conv = 2 * count * 9 * channels * channels

    def first_strips(edge_ref, corner_ref, x_ref, g_ref, *outs):
        lines, pixels = seam_lines(edge_ref, corner_ref, extent)
        a = gather_blocks(x_ref[...], lines, pixels, extent)
        b = gather_blocks(g_ref[...], *fixed_lines(extent), extent)
        write(a, b, outs)

    first = call(first_strips, "first_strips", routed, "ssvv", (edge_code, corner_code, source, grad_out))
    first_arrived = relay(*first, total) if hops else exchange(first, plan, tiles)

    def inner(x_ref, g_ref, w1_ref, w2_ref, pre_ref, dh_ref, xt_ref, qg_ref, w1t_ref, w2t_ref, qx_ref):
        transpose_taps(w1t_ref, w1_ref)
        transpose_taps(w2t_ref, w2_ref)
        write_columns(qx_ref, x_ref[...], True, extent)
        pre_ref[...] = window_product(qx_ref, w1_ref[...], True, extent)
        write_columns(qg_ref, g_ref[...], False, extent)
        dh_ref[...] = window_product(qg_ref, w2t_ref[...], False, extent)
        xt_ref[...] = jnp.transpose(x_ref[...].astype(F32)).astype(BF16)

    pre, dh, xt, qg, w1t, w2t = call(
        inner,
        "inner_products",
        [image_f, image_f, turned_b, columns_b, taps_b, taps_b],
        "vvvv",
        (source, grad_out, w_one, w_two),
        scratch=[pltpu.VMEM(columns_b.shape, BF16)],
        flops=2 * conv,
    )

    def middle(edge_ref, corner_ref, pre_ref, dh_ref, xt_ref, qg_ref, w1_ref, w2t_ref, *refs):
        arrived = refs[:n_routes]
        keep_ref, send_ref, hid_ref, dpre_ref = refs[n_routes : n_routes + 4]
        outs = refs[n_routes + 4 : n_routes + 4 + n_routed]
        qd_ref, sum_ref = refs[n_routes + 4 + n_routed :]
        lines, pixels = seam_lines(edge_ref, corner_ref, extent)
        x_strips, g_strips = read(arrived)
        columns = strip_columns(g_strips, extent)
        value, slope = gelu_parts(pre_ref[...] + margin_forward(x_strips, w1_ref[...], extent))
        hidden = value.astype(BF16)
        hid_ref[...] = hidden
        d_hidden = dh_ref[...] + margin_backward(columns, w2t_ref[...], lines, pixels, extent)
        d_pre = (d_hidden * slope).astype(BF16)
        dpre_ref[...] = d_pre
        a = gather_blocks(hidden, lines, pixels, extent)
        b = gather_blocks(d_pre, *fixed_lines(extent), extent)
        write(a, b, outs)
        write_columns(qd_ref, d_pre, False, extent)
        weight_sum(sum_ref.at[0], xt_ref[...], qd_ref, x_strips, strip_columns(b, extent), extent)
        weight_sum(sum_ref.at[1], jnp.transpose(value).astype(BF16), qg_ref, a, columns, extent)
        core = lax.axis_index("dp") % 2
        keep_ref[...] = sum_ref[core]
        send_ref[...] = sum_ref[1 - core].astype(BF16)

    results = call(
        middle,
        "gradients",
        [taps_f, taps_b, image_b, image_b] + routed,
        "ss" + "v" * (6 + n_routes),
        (edge_code, corner_code, pre, dh, xt, qg, w_one, w2t, *first_arrived),
        scratch=[pltpu.VMEM(columns_b.shape, BF16), pltpu.VMEM((2,) + taps_f.shape, F32)],
        flops=2 * conv,
    )
    keep, send, hidden, d_pre = results[:4]
    if hops:
        whole, second_arrived = reduce_gradients(keep, send, total, *results[4:])
    else:
        second_arrived = exchange(results[4:], plan, tiles)
        whole, _ = reduce_gradients(keep, send, total)

    def last(edge_ref, corner_ref, x_ref, g_ref, hid_ref, dpre_ref, w2_ref, w1t_ref, *refs):
        arrived = refs[:n_routes]
        out_ref, dx_ref, q_ref = refs[n_routes:]
        lines, pixels = seam_lines(edge_ref, corner_ref, extent)
        h_strips, d_strips = read(arrived)
        write_columns(q_ref, hid_ref[...], True, extent)
        total = window_product(q_ref, w2_ref[...], True, extent) + margin_forward(h_strips, w2_ref[...], extent)
        out_ref[...] = (x_ref[...].astype(F32) + total).astype(BF16)
        write_columns(q_ref, dpre_ref[...], False, extent)
        total = window_product(q_ref, w1t_ref[...], False, extent)
        total = total + margin_backward(strip_columns(d_strips, extent), w1t_ref[...], lines, pixels, extent)
        dx_ref[...] = (g_ref[...].astype(F32) + total).astype(BF16)

    output, d_input = call(
        last,
        "outputs",
        [image_b, image_b],
        "ss" + "v" * (6 + n_routes),
        (edge_code, corner_code, source, grad_out, hidden, d_pre, w_two, w1t, *second_arrived),
        scratch=[pltpu.VMEM(columns_b.shape, BF16)],
        flops=2 * conv,
    )
    whole, output, d_input = lax.optimization_barrier((whole, output, d_input))
    one, two = join_cores(whole, total)
    shape = (9, channels, channels)
    return (
        output.reshape(inputs.shape),
        d_input.reshape(inputs.shape),
        (one.astype(F32) * factor).reshape(shape),
        (two.astype(F32) * factor).reshape(shape),
    )


def solution(mesh):
    split = P("dp", "tile", None, None, None)
    return jax.shard_map(
        per_device,
        mesh=mesh,
        in_specs=(split, P(), P(), split, P(), P()),
        out_specs=(split, split, P(), P()),
        check_vma=False,
    )
```

```python
import math

import jax
import jax.numpy as jnp
from jax import lax
from jax.experimental import pallas as pl
from jax.experimental.pallas import tpu as pltpu
from jax.sharding import PartitionSpec as P

RW = 4
SIDES = (-RW, 1, RW, -1)
CORNERS = (-RW - 1, -RW + 1, RW + 1, RW - 1)
F32 = jnp.float32
BF16 = jnp.bfloat16
AXES = ("tile", "dp")
LIMIT = 20 * 1024 * 1024
ALONE = 60 * 1024 * 1024

BLOCKS = ((0, (0, 1)), (2, (3, 2)), (1, ()), (3, ()))


def block_rows(extent):
    return (extent + 16, extent + 16, extent, extent)


def block_starts(extent):
    rows = block_rows(extent)
    return (0, rows[0], rows[0] + rows[1], rows[0] + rows[1] + rows[2])


def block_taps(position):
    return ((0, 1, 2), (6, 7, 8), (2, 5, 8), (0, 3, 6))[position]


def routes(tiles):
    found = {}
    for kind, offsets in (("a", SIDES), ("b", SIDES), ("ac", CORNERS), ("bc", CORNERS)):
        for which, offset in enumerate(offsets):
            distance = (-offset if kind[0] == "a" else offset) % tiles
            found.setdefault(distance, []).append((kind, which))
    plan = []
    for distance, parts in found.items():
        sides = [p for p in parts if len(p[0]) == 1]
        corners = [p for p in parts if len(p[0]) == 2]
        plan.append((distance, sides, corners))
    return plan


def route_rows(route, extent):
    return extent * len(route[1]) + (16 if route[2] else 0)


def iota(shape, axis):
    return lax.broadcasted_iota(jnp.int32, shape, axis)


def dot(a, b):
    return lax.dot_general(a, b, (((1,), (0,)), ((), ())), preferred_element_type=F32)


def dot_nt(a, b):
    return lax.dot_general(a, b, (((1,), (1,)), ((), ())), preferred_element_type=F32)


def dot_t(a, b):
    return lax.dot_general(a, b, (((0,), (0,)), ((), ())), preferred_element_type=F32)


def corner_pixel(code, extent):
    last = extent - 1
    return jnp.where(code == 0, 0, jnp.where(code == 1, last, jnp.where(code == 2, extent * extent - 1, extent * last)))


def side_line(code, extent):
    last = extent - 1
    border = code % 4
    base = jnp.where(border == 1, last, jnp.where(border == 2, extent * last, 0))
    step = jnp.where(border % 2 == 0, 1, extent)
    return jnp.where(code >= 4, base + last * step, base), jnp.where(code >= 4, -step, step)


def seam_lines(edge_ref, corner_ref, extent):
    tiles = edge_ref.shape[1]
    mine = lax.axis_index("tile")
    lines = [side_line(edge_ref[k, (mine - o + tiles + RW * tiles) % tiles], extent) for k, o in enumerate(SIDES)]
    pixels = [corner_pixel(corner_ref[q, (mine - o + tiles + RW * tiles) % tiles], extent) for q, o in enumerate(CORNERS)]
    return lines, pixels


def fixed_lines(extent):
    last = extent - 1
    lines = [(0, 1), (last, extent), (extent * last, 1), (0, extent)]
    return lines, [0, last, extent * extent - 1, extent * last]


def pick_rows(indices, count):
    return (iota((indices.shape[0], count), 1) == indices).astype(F32).astype(BF16)


def line_rows(line, extent, count):
    return pick_rows(line[0] + line[1] * iota((extent, 1), 0), count)


def spot_rows(spots, count):
    rows = iota((16, 1), 0)
    index = jnp.full((16, 1), -1, jnp.int32)
    for row, pixel in spots:
        index = jnp.where(rows == row, pixel, index)
    return pick_rows(index, count)


def block_choice(lines, pixels, extent):
    count = extent * extent
    rows = []
    for side, corners in BLOCKS:
        rows.append(line_rows(lines[side], extent, count))
        if corners:
            rows.append(spot_rows([(i, pixels[q]) for i, q in enumerate(corners)], count))
    return jnp.concatenate(rows, axis=0)


def seam_scatter(lines, pixels, extent):
    starts = block_starts(extent)
    lane = iota((1, starts[3] + extent), 1)
    index = jnp.full(lane.shape, -1, jnp.int32)
    for start, (side, ends) in zip(starts, BLOCKS):
        base, step = lines[side]
        index = jnp.where((lane >= start) & (lane < start + extent), base + step * (lane - start), index)
        for i, q in enumerate(ends):
            index = jnp.where(lane == start + extent + i, pixels[q], index)
    return (iota((extent * extent, 1), 0) == index).astype(F32).astype(BF16)


def column_scatter(extent):
    lane = iota((1, 4 * extent), 1)
    target = (lane % extent) * extent + jnp.where(lane < 2 * extent, extent - 1, 0)
    return (iota((extent * extent, 1), 0) == target).astype(F32).astype(BF16)


def gather_blocks(choice, image, extent):
    strips = dot(choice, image).astype(BF16)
    starts = block_starts(extent)
    return [strips[start : start + rows] for start, rows in zip(starts, block_rows(extent))]


def write_routes(a_blocks, b_blocks, plan, out_refs, extent):
    side_at = {side: i for i, (side, _) in enumerate(BLOCKS)}
    corner_at = {q: (i, extent + j) for i, (_, corners) in enumerate(BLOCKS) for j, q in enumerate(corners)}
    for route, out in zip(plan, out_refs):
        at = 0
        for kind, side in route[1]:
            blocks = a_blocks if kind == "a" else b_blocks
            out[at : at + extent, :] = blocks[side_at[side]][:extent]
            at += extent
        if route[2]:
            rows = iota((16, 1), 0)
            tile = jnp.zeros((16, out.shape[1]), F32)
            for i, (kind, q) in enumerate(route[2]):
                block, row = corner_at[q]
                source = (a_blocks if kind == "ac" else b_blocks)[block][extent : extent + 16].astype(F32)
                tile = jnp.where(rows == i, source[row - extent : row - extent + 1], tile)
            out[at : at + 16, :] = tile.astype(BF16)


def read_routes(plan, in_refs, extent):
    sides, corners = {}, {}
    for route, ref in zip(plan, in_refs):
        at = 0
        for key in route[1]:
            sides[key] = ref[at : at + extent, :]
            at += extent
        if route[2]:
            tile = ref[at : at + 16, :].astype(F32)
            for i, key in enumerate(route[2]):
                corners[key] = tile[i : i + 1]
    result = []
    rows = iota((16, 1), 0)
    for kind in ("a", "b"):
        blocks = []
        for side, ends in BLOCKS:
            block = sides[(kind, side)]
            if ends:
                tile = jnp.zeros((16, block.shape[1]), F32)
                for i, q in enumerate(ends):
                    tile = jnp.where(rows == i, corners[(kind + "c", q)], tile)
                block = jnp.concatenate([block, tile.astype(BF16)], axis=0)
            blocks.append(block)
        result.append(blocks)
    return result


def relayed(tiles):
    return tiles == 8


def write_near(a_blocks, b_blocks, near_ref, extent):
    for i, block in enumerate((a_blocks[3], b_blocks[2], a_blocks[2], b_blocks[3])):
        near_ref[i * extent : (i + 1) * extent, :] = block
    rows = iota((16, 1), 0)
    tile = jnp.zeros((16, near_ref.shape[1]), F32)
    at = 0
    for blocks in (a_blocks, b_blocks):
        ends = [blocks[i][extent : extent + 16].astype(F32) for i in range(2)]
        for block, row in ((0, 0), (0, 1), (1, 1), (1, 0)):
            tile = jnp.where(rows == at, ends[block][row : row + 1], tile)
            at += 1
    near_ref[4 * extent : 4 * extent + 16, :] = tile.astype(BF16)


def write_far(a_blocks, b_blocks, far_ref, extent):
    for i, block in enumerate((a_blocks[0], a_blocks[1], b_blocks[0], b_blocks[1])):
        far_ref[i * extent : (i + 1) * extent, :] = block[:extent]


def near_starts(tile, extent):
    right = tile % 2
    odd = (tile // 2) % 2
    corners = 2 * extent + 16
    side = jnp.where(right == 1, 0, 2 * extent)
    one = jnp.where(right == odd, corners, side)
    three = jnp.where(right == odd, side, corners)
    return side_of_partner(right, extent), one, three


def side_of_partner(right, extent):
    return jnp.where(right == 1, 2 * extent, 0)


def read_relay(refs, extent):
    across, one, three, far, opposite = refs
    mine = lax.axis_index("tile")
    left = mine % 2 == 0
    odd = (mine // 2 + mine) % 2 == 1

    def rows_of(ref, start, count):
        return ref[start : start + count, :].astype(F32)

    def choose(start, count):
        return jnp.where(odd, rows_of(one, start, count), rows_of(three, start, count))

    pair = [(rows_of(across, i * extent, extent), choose(i * extent, extent)) for i in range(2)]
    a_east, b_west = [jnp.where(left, here, there).astype(BF16) for here, there in pair]
    a_west, b_east = [jnp.where(left, there, here).astype(BF16) for here, there in pair]
    tail = 2 * extent - 16
    beside = jnp.where(odd, rows_of(three, tail, 16), rows_of(one, tail, 16))
    beyond = opposite[0:16, :].astype(F32)
    third = jnp.where(left, beside, beyond)
    fifth = jnp.where(left, beyond, beside)
    corners = {("a", 0): third[0:1], ("a", 3): third[3:4], ("b", 1): third[5:6], ("b", 2): third[6:7]}
    corners.update({("a", 1): fifth[1:2], ("a", 2): fifth[2:3], ("b", 0): fifth[4:5], ("b", 3): fifth[7:8]})
    rows = iota((16, 1), 0)
    result = []
    for kind, first, east, west in (("a", 0, a_east, a_west), ("b", 2, b_east, b_west)):
        blocks = []
        for i, ends in enumerate(((0, 1), (3, 2))):
            tile = jnp.where(rows == 0, corners[(kind, ends[0])], jnp.where(rows == 1, corners[(kind, ends[1])], 0.0))
            strip = far[(first + i) * extent : (first + i + 1) * extent, :]
            blocks.append(jnp.concatenate([strip, tile.astype(BF16)], axis=0))
        result.append(blocks + [east, west])
    return result


def shifted(image, by, extent):
    if by == 0:
        return image
    column = iota((image.shape[0], 1), 0) % extent
    rolled = pltpu.roll(image, (-by) % image.shape[0], 0)
    return jnp.where(column == (extent - 1 if by == 1 else 0), 0.0, rolled)


def write_columns(q_ref, image, forward, extent):
    count, channels = image.shape
    zero = jnp.zeros((extent, q_ref.shape[1]), BF16)
    q_ref[0:extent, :] = zero
    q_ref[extent + count : 2 * extent + count, :] = zero
    wide = image.astype(F32)
    for b in range(3):
        by = b - 1 if forward else 1 - b
        q_ref[extent : extent + count, b * channels : (b + 1) * channels] = shifted(wide, by, extent).astype(BF16)


def window_product(q_ref, weight, forward, extent, chunk=256):
    count = q_ref.shape[0] - 2 * extent
    channels = weight.shape[1]
    if not forward:
        weight = tap_columns(weight, range(9), channels)
    pieces = []
    for start in range(0, count, chunk):
        rows = [q_ref[(a if forward else 2 - a) * extent + start : (a if forward else 2 - a) * extent + start + chunk, :] for a in range(3)]
        pieces.append((dot if forward else dot_nt)(jnp.concatenate(rows, axis=1), weight))
    return jnp.concatenate(pieces, axis=0)


def tap_weight(weight, taps, channels):
    return jnp.concatenate([weight[t * channels : (t + 1) * channels, :] for t in taps], axis=0)


def tap_columns(weight, taps, channels):
    return jnp.concatenate([weight[t * channels : (t + 1) * channels, :] for t in taps], axis=1)


def halves(values):
    high = values.astype(BF16)
    return high, (values - high.astype(F32)).astype(BF16)


def margin_forward(strips, weight, columns, extent):
    channels = strips[0].shape[1]
    count = extent * extent
    adds = []
    for position, (side, ends) in enumerate(BLOCKS):
        middle = strips[position][:extent].astype(F32)
        row = iota((extent, 1), 0)
        before, after = 0.0, 0.0
        if ends:
            tile = strips[position][extent : extent + 16].astype(F32)
            before, after = tile[0:1], tile[1:2]
        left = jnp.where(row == 0, before, pltpu.roll(middle, 1, 0))
        right = jnp.where(row == extent - 1, after, pltpu.roll(middle, extent - 1, 0))
        window = jnp.concatenate([left, middle, right], axis=1).astype(BF16)
        adds.append(dot(window, tap_weight(weight, block_taps(position), channels)))
    spread = jnp.concatenate(list(halves(adds[2])) + list(halves(adds[3])), axis=0)
    image = dot(columns, spread)
    top = image[:extent] + adds[0]
    bottom = image[count - extent :] + adds[1]
    return jnp.concatenate([top, image[extent : count - extent], bottom], axis=0)


def strip_columns(strips, extent):
    result = []
    for position, (side, ends) in enumerate(BLOCKS):
        middle = strips[position][:extent].astype(F32)
        row = iota((extent, 1), 0)
        after = jnp.where(row == extent - 1, 0.0, pltpu.roll(middle, extent - 1, 0))
        before = jnp.where(row == 0, 0.0, pltpu.roll(middle, 1, 0))
        columns = jnp.concatenate([after, middle, before], axis=1)
        if ends:
            tile = strips[position][extent : extent + 16].astype(F32)
            row = iota((16, 1), 0)
            low = jnp.where(row == 0, tile, 0.0)
            high = jnp.where(row == 1, tile, 0.0)
            columns = jnp.concatenate([columns, jnp.concatenate([low, jnp.zeros_like(tile), high], axis=1)], axis=0)
        result.append(columns.astype(BF16))
    return result


def margin_backward(columns, weight, scatter, extent):
    channels = weight.shape[1]
    adds = [dot_nt(columns[i], tap_columns(weight, block_taps(i), channels)) for i in range(4)]
    high, low = halves(jnp.concatenate(adds, axis=0))
    return dot(scatter, high) + dot(scatter, low)


def weight_sum(out_ref, image_t, q_ref, strips, columns, extent):
    channels = image_t.shape[0]
    count = image_t.shape[1]
    wide = [dot_t(strips[i], columns[i]) for i in range(4)]
    for a in range(3):
        rows = q_ref[(2 - a) * extent : (2 - a) * extent + count, :]
        product = dot(image_t, rows)
        for b in range(3):
            tap = 3 * a + b
            value = product[:, b * channels : (b + 1) * channels]
            for position in range(4):
                taps = block_taps(position)
                if tap in taps:
                    at = taps.index(tap)
                    value = value + wide[position][:, at * channels : (at + 1) * channels]
            out_ref[tap * channels : (tap + 1) * channels, :] = value


def gelu_parts(u):
    scale = math.sqrt(2.0 / math.pi)
    square = u * u
    t = jnp.tanh(scale * (u + 0.044715 * (square * u)))
    value = 0.5 * u * (1.0 + t)
    slope = 0.5 * (1.0 + t) + (0.5 * u) * (1.0 - t * t) * (scale * (1.0 + 3.0 * 0.044715 * square))
    return value, slope


def call(kernel, name, outs, ins, operands, scratch=(), flops=0, limit=LIMIT):
    specs = [pl.BlockSpec(memory_space={"a": pl.ANY, "s": pltpu.SMEM, "v": pltpu.VMEM}[i]) for i in ins]
    moved = sum(math.prod(o.shape) * o.dtype.itemsize for o in list(outs) + list(operands))
    return pl.pallas_call(
        kernel,
        name=name,
        out_shape=outs,
        in_specs=specs,
        out_specs=[pl.BlockSpec(memory_space=pltpu.VMEM) for _ in outs],
        scratch_shapes=list(scratch),
        cost_estimate=pl.CostEstimate(flops=flops, bytes_accessed=moved, transcendentals=0),
        compiler_params=pltpu.CompilerParams(vmem_limit_bytes=limit),
    )(*operands)


def sds(shape, dtype):
    return jax.ShapeDtypeStruct(shape, dtype)


def exchange(payloads, plan, tiles):
    return [
        lax.ppermute(p, "tile", [(i, (i + route[0]) % tiles) for i in range(tiles)]) for p, route in zip(payloads, plan)
    ]


def swap(value, mask, total):
    return lax.ppermute(value, AXES, [(i, i ^ mask) for i in range(total)])


def reduce_gradients(keep, send, total, work, near=None, far=None):
    rows, channels = keep.shape
    quarter = rows // 4
    wire = BF16 if total <= 32 else F32
    me = lax.axis_index(AXES)
    other = swap(send, 1, total)
    plane = (me >> 1) & 3

    def chunk(index):
        first = lax.dynamic_index_in_dim(keep.reshape(4, quarter, channels), index, 0, keepdims=False)
        second = lax.dynamic_index_in_dim(other.reshape(4, quarter, channels), index, 0, keepdims=False)
        return first + second.astype(F32)

    arrived = {}
    for m in (3, 1, 2):
        message = chunk(plane ^ m).astype(wire)
        if m == 2 and near is not None:
            message = jnp.concatenate([message, near], axis=0)
        arrived[m] = swap(message, m << 1, total)
    part = chunk(plane)
    for m in (3, 1, 2):
        part = part + arrived[m][:quarter].astype(F32)
    part, done = work(part)
    extras = None
    if near is not None:
        across = arrived[2][quarter:]
        extent = far.shape[0] // 4
        starts = near_starts(lax.axis_index("tile") ^ 1, extent)
        direct, one, three = [lax.dynamic_slice_in_dim(across, start, 2 * extent, 0) for start in starts]
        riders = {1: (one,), 2: (far, across[-16:]), 3: (three,)}
    bit = 8
    while bit < total:
        mine = part.astype(wire)
        if 2 * bit < total:
            got = {}
            for m in (3, 2, 1):
                message = mine
                if near is not None:
                    message = jnp.concatenate([mine, *riders[m]], axis=0)
                got[m] = swap(message, m * bit, total)
            part = (mine.astype(F32) + got[1][:quarter].astype(F32)) + (got[2][:quarter].astype(F32) + got[3][:quarter].astype(F32))
            if near is not None:
                extras = [direct, got[1][quarter:], got[3][quarter:], got[2][quarter:-16], got[2][-16:]]
            bit *= 4
        else:
            part = mine.astype(F32) + swap(mine, bit, total).astype(F32)
            bit *= 2
    part, done = lax.optimization_barrier((part, done))
    mine = part.astype(wire)
    ring = jnp.stack([mine] + [swap(mine, m << 1, total) for m in (1, 2, 3)])
    whole = jnp.concatenate([lax.dynamic_index_in_dim(ring, plane ^ j, 0) for j in range(4)], axis=0)
    return whole, extras, done


def join_cores(whole, total):
    other = swap(whole, 1, total)
    low = (lax.axis_index(AXES) & 1) == 0
    return jnp.where(low, whole, other), jnp.where(low, other, whole)


def reach_neighbours(across, one, three, far, corners, total):
    return [swap(across, 4, total), swap(one, 12, total), swap(three, 28, total), swap(far, 16, total), swap(corners, 20, total)]


def per_device(inputs, weight_one, weight_two, cotangent, edge_code, corner_code):
    tiles, members = lax.axis_size("tile"), lax.axis_size("dp")
    extent, channels = inputs.shape[2], inputs.shape[4]
    count = extent * extent
    factor = 1.0 / math.sqrt(inputs.shape[0] * members * tiles * count)
    source = inputs.reshape(count, channels)
    grad_out = cotangent.reshape(count, channels)
    w_one = weight_one.reshape(9 * channels, channels)
    w_two = weight_two.reshape(9 * channels, channels)
    plan = routes(tiles)
    total = tiles * members
    hops = relayed(tiles)
    near_b, far_b, corner_b = sds((4 * extent + 16, channels), BF16), sds((4 * extent, channels), BF16), sds((16, channels), BF16)
    pair_b = sds((2 * extent, channels), BF16)
    if hops:
        first_routed, second_routed = [pair_b, pair_b, pair_b, far_b, corner_b], [near_b, far_b]
        n_routes = 5
    else:
        first_routed = second_routed = [sds((route_rows(r, extent), channels), BF16) for r in plan]
        n_routes = len(plan)
    n_first, n_second = len(first_routed), len(second_routed)

    def write_first(a, b, outs, near_ref):
        if hops:
            write_near(a, b, near_ref, extent)
            write_far(a, b, outs[3], extent)
            for start, out in zip(near_starts(lax.axis_index("tile"), extent), outs):
                out[...] = near_ref[pl.ds(pl.multiple_of(start, 16), 2 * extent), :]
            outs[4][...] = near_ref[4 * extent : 4 * extent + 16, :]
        else:
            write_routes(a, b, plan, outs, extent)

    def write_second(a, b, outs):
        if hops:
            write_near(a, b, outs[0], extent)
            write_far(a, b, outs[1], extent)
        else:
            write_routes(a, b, plan, outs, extent)

    def read(refs):
        return read_relay(refs, extent) if hops else read_routes(plan, refs, extent)

    image_b, image_f = sds((count, channels), BF16), sds((count, channels), F32)
    columns_b = sds((count + 2 * extent, 3 * channels), BF16)
    taps_b, taps_f = sds((9 * channels, channels), BF16), sds((9 * channels, channels), F32)
    turned_b = sds((channels, count), BF16)
    conv = 2 * count * 9 * channels * channels

    strip_rows = block_starts(extent)[3] + extent
    choice_b = sds((strip_rows, count), BF16)
    scatter_b, column_b = sds((count, strip_rows), BF16), sds((count, 4 * extent), BF16)
    pieces = 2

    def first_strips(x_hbm, g_hbm, edge_hbm, corner_hbm, *refs):
        outs = refs[:n_first]
        x_ref, g_ref, near_ref, edge_ref, corner_ref, sems = refs[n_first:]
        pairs = [(edge_hbm, edge_ref), (corner_hbm, corner_ref)]
        step = count // pieces
        for source_ref, target_ref in ((x_hbm, x_ref), (g_hbm, g_ref)):
            for i in range(pieces):
                pairs.append((source_ref.at[pl.ds(i * step, step)], target_ref.at[pl.ds(i * step, step)]))
        copies = [pltpu.make_async_copy(a, b, sems.at[i]) for i, (a, b) in enumerate(pairs)]
        for copy in copies:
            copy.start()
        fixed = block_choice(*fixed_lines(extent), extent)
        for copy in copies[:2]:
            copy.wait()
        seam = block_choice(*seam_lines(edge_ref, corner_ref, extent), extent)
        for copy in copies[2:]:
            copy.wait()
        a = gather_blocks(seam, x_ref[...], extent)
        b = gather_blocks(fixed, g_ref[...], extent)
        write_first(a, b, outs, near_ref)

    first = call(
        first_strips,
        "first_strips",
        first_routed,
        "aaaa",
        (source, grad_out, edge_code.T, corner_code.T),
        scratch=[
            pltpu.VMEM((count, channels), BF16),
            pltpu.VMEM((count, channels), BF16),
            pltpu.VMEM(near_b.shape, BF16),
            pltpu.SMEM((4, tiles), jnp.int32),
            pltpu.SMEM((4, tiles), jnp.int32),
            pltpu.SemaphoreType.DMA((2 + 2 * pieces,)),
        ],
        limit=ALONE,
        flops=10 * conv,
    )
    first_arrived = reach_neighbours(*first, total) if hops else exchange(first, plan, tiles)

    def selections(edge_ref, corner_ref, seam_ref, fixed_ref, scatter_ref, column_ref):
        lines, pixels = seam_lines(edge_ref, corner_ref, extent)
        seam_ref[...] = block_choice(lines, pixels, extent)
        scatter_ref[...] = seam_scatter(lines, pixels, extent)
        fixed_ref[...] = block_choice(*fixed_lines(extent), extent)
        column_ref[...] = column_scatter(extent)

    seam, fixed, scatter, column = call(
        selections,
        "selections",
        [choice_b, choice_b, scatter_b, column_b],
        "ss",
        (edge_code.T, corner_code.T),
    )

    def inner(x_ref, g_ref, w1_ref, w2_ref, pre_ref, dh_ref, xt_ref, qg_ref, qx_ref):
        write_columns(qx_ref, x_ref[...], True, extent)
        pre_ref[...] = window_product(qx_ref, w1_ref[...], True, extent)
        write_columns(qg_ref, g_ref[...], False, extent)
        dh_ref[...] = window_product(qg_ref, w2_ref[...], False, extent)
        xt_ref[...] = jnp.transpose(x_ref[...].astype(F32)).astype(BF16)

    pre, dh, xt, qg = call(
        inner,
        "inner_products",
        [image_f, image_f, turned_b, columns_b],
        "vvvv",
        (source, grad_out, w_one, w_two),
        scratch=[pltpu.VMEM(columns_b.shape, BF16)],
        flops=2 * conv,
    )

    def middle(seam_ref, fixed_ref, scatter_ref, column_ref, pre_ref, dh_ref, xt_ref, qg_ref, w1_ref, w2_ref, *refs):
        arrived = refs[:n_routes]
        keep_ref, send_ref, hid_ref, dpre_ref = refs[n_routes : n_routes + 4]
        outs = refs[n_routes + 4 : n_routes + 4 + n_second]
        qd_ref, sum_ref = refs[n_routes + 4 + n_second :]
        x_strips, g_strips = read(arrived)
        columns = strip_columns(g_strips, extent)
        value, slope = gelu_parts(pre_ref[...] + margin_forward(x_strips, w1_ref[...], column_ref[...], extent))
        hidden = value.astype(BF16)
        hid_ref[...] = hidden
        d_hidden = dh_ref[...] + margin_backward(columns, w2_ref[...], scatter_ref[...], extent)
        d_pre = (d_hidden * slope).astype(BF16)
        dpre_ref[...] = d_pre
        a = gather_blocks(seam_ref[...], hidden, extent)
        b = gather_blocks(fixed_ref[...], d_pre, extent)
        write_second(a, b, outs)
        write_columns(qd_ref, d_pre, False, extent)
        weight_sum(sum_ref.at[0], xt_ref[...], qd_ref, x_strips, strip_columns(b, extent), extent)
        weight_sum(sum_ref.at[1], jnp.transpose(value).astype(BF16), qg_ref, a, columns, extent)
        core = lax.axis_index("dp") % 2
        keep_ref[...] = sum_ref[core]
        send_ref[...] = sum_ref[1 - core].astype(BF16)

    results = call(
        middle,
        "gradients",
        [taps_f, taps_b, image_b, image_b] + second_routed,
        "v" * (10 + n_routes),
        (seam, fixed, scatter, column, pre, dh, xt, qg, w_one, w_two, *first_arrived),
        scratch=[pltpu.VMEM(columns_b.shape, BF16), pltpu.VMEM((2,) + taps_f.shape, F32)],
        flops=2 * conv,
    )
    keep, send, hidden, d_pre = results[:4]
    def later(edge_ref, corner_ref, x_ref, g_ref, hid_ref, dpre_ref, w1_ref, w2_ref, out_ref, dx_ref, scatter_ref, column_ref, q_ref):
        lines, pixels = seam_lines(edge_ref, corner_ref, extent)
        scatter_ref[...] = seam_scatter(lines, pixels, extent)
        column_ref[...] = column_scatter(extent)
        write_columns(q_ref, hid_ref[...], True, extent)
        out_ref[...] = x_ref[...].astype(F32) + window_product(q_ref, w2_ref[...], True, extent)
        write_columns(q_ref, dpre_ref[...], False, extent)
        dx_ref[...] = g_ref[...].astype(F32) + window_product(q_ref, w1_ref[...], False, extent)

    def later_parts(token):
        token, inner_arrays = lax.optimization_barrier((token, (hidden, d_pre)))
        return token, call(
            later,
            "later_products",
            [image_f, image_f, scatter_b, column_b],
            "ssvvvvvv",
            (edge_code.T, corner_code.T, source, grad_out, *inner_arrays, w_one, w_two),
            scratch=[pltpu.VMEM(columns_b.shape, BF16)],
            flops=2 * conv,
        )

    if hops:
        whole, second_arrived, parts = reduce_gradients(keep, send, total, later_parts, *results[4:])
    else:
        second_arrived = exchange(results[4:], plan, tiles)
        whole, _, parts = reduce_gradients(keep, send, total, later_parts)

    def last(part_ref, dpart_ref, scatter_ref, column_ref, w1_ref, w2_ref, *refs):
        arrived = refs[:n_routes]
        out_ref, dx_ref = refs[n_routes:]
        h_strips, d_strips = read(arrived)
        out_ref[...] = (part_ref[...] + margin_forward(h_strips, w2_ref[...], column_ref[...], extent)).astype(BF16)
        add = margin_backward(strip_columns(d_strips, extent), w1_ref[...], scatter_ref[...], extent)
        dx_ref[...] = (dpart_ref[...] + add).astype(BF16)

    output, d_input = call(
        last,
        "outputs",
        [image_b, image_b],
        "v" * (6 + n_routes),
        (*parts, w_one, w_two, *second_arrived),
        flops=conv // 4,
    )
    whole, output, d_input = lax.optimization_barrier((whole, output, d_input))
    one, two = join_cores(whole, total)
    shape = (9, channels, channels)
    return (
        output.reshape(inputs.shape),
        d_input.reshape(inputs.shape),
        (one.astype(F32) * factor).reshape(shape),
        (two.astype(F32) * factor).reshape(shape),
    )


def solution(mesh):
    split = P("dp", "tile", None, None, None)
    return jax.shard_map(
        per_device,
        mesh=mesh,
        in_specs=(split, P(), P(), split, P(), P()),
        out_specs=(split, split, P(), P()),
        check_vma=False,
    )
```

```python
import math

import jax
import jax.numpy as jnp
from jax import lax
from jax.experimental import pallas as pl
from jax.experimental.pallas import tpu as pltpu
from jax.sharding import PartitionSpec as P

RW = 4
SIDES = (-RW, 1, RW, -1)
CORNERS = (-RW - 1, -RW + 1, RW + 1, RW - 1)
F32 = jnp.float32
BF16 = jnp.bfloat16
AXES = ("tile", "dp")
LIMIT = 20 * 1024 * 1024
ALONE = 60 * 1024 * 1024

BLOCKS = ((0, (0, 1)), (2, (3, 2)), (1, ()), (3, ()))


def block_rows(extent):
    return (extent + 16, extent + 16, extent, extent)


def block_starts(extent):
    rows = block_rows(extent)
    return (0, rows[0], rows[0] + rows[1], rows[0] + rows[1] + rows[2])


def block_taps(position):
    return ((0, 1, 2), (6, 7, 8), (2, 5, 8), (0, 3, 6))[position]


def routes(tiles):
    found = {}
    for kind, offsets in (("a", SIDES), ("b", SIDES), ("ac", CORNERS), ("bc", CORNERS)):
        for which, offset in enumerate(offsets):
            distance = (-offset if kind[0] == "a" else offset) % tiles
            found.setdefault(distance, []).append((kind, which))
    plan = []
    for distance, parts in found.items():
        sides = [p for p in parts if len(p[0]) == 1]
        corners = [p for p in parts if len(p[0]) == 2]
        plan.append((distance, sides, corners))
    return plan


def route_rows(route, extent):
    return extent * len(route[1]) + (16 if route[2] else 0)


def iota(shape, axis):
    return lax.broadcasted_iota(jnp.int32, shape, axis)


def dot(a, b):
    return lax.dot_general(a, b, (((1,), (0,)), ((), ())), preferred_element_type=F32)


def dot_nt(a, b):
    return lax.dot_general(a, b, (((1,), (1,)), ((), ())), preferred_element_type=F32)


def dot_t(a, b):
    return lax.dot_general(a, b, (((0,), (0,)), ((), ())), preferred_element_type=F32)


def corner_pixel(code, extent):
    last = extent - 1
    return jnp.where(code == 0, 0, jnp.where(code == 1, last, jnp.where(code == 2, extent * extent - 1, extent * last)))


def side_line(code, extent):
    last = extent - 1
    border = code % 4
    base = jnp.where(border == 1, last, jnp.where(border == 2, extent * last, 0))
    step = jnp.where(border % 2 == 0, 1, extent)
    return jnp.where(code >= 4, base + last * step, base), jnp.where(code >= 4, -step, step)


def seam_lines(edge_ref, corner_ref, extent):
    tiles = edge_ref.shape[1]
    mine = lax.axis_index("tile")
    lines = [side_line(edge_ref[k, (mine - o + tiles + RW * tiles) % tiles], extent) for k, o in enumerate(SIDES)]
    pixels = [corner_pixel(corner_ref[q, (mine - o + tiles + RW * tiles) % tiles], extent) for q, o in enumerate(CORNERS)]
    return lines, pixels


def fixed_lines(extent):
    last = extent - 1
    lines = [(0, 1), (last, extent), (extent * last, 1), (0, extent)]
    return lines, [0, last, extent * extent - 1, extent * last]


def pick_rows(indices, count):
    return (iota((indices.shape[0], count), 1) == indices).astype(F32).astype(BF16)


def line_rows(line, extent, count):
    return pick_rows(line[0] + line[1] * iota((extent, 1), 0), count)


def spot_rows(spots, count):
    rows = iota((16, 1), 0)
    index = jnp.full((16, 1), -1, jnp.int32)
    for row, pixel in spots:
        index = jnp.where(rows == row, pixel, index)
    return pick_rows(index, count)


def block_choice(lines, pixels, extent):
    count = extent * extent
    rows = []
    for side, corners in BLOCKS:
        rows.append(line_rows(lines[side], extent, count))
        if corners:
            rows.append(spot_rows([(i, pixels[q]) for i, q in enumerate(corners)], count))
    return jnp.concatenate(rows, axis=0)


def block_index(lines, pixels, axis, extent):
    starts = block_starts(extent)
    total = starts[3] + extent
    place = iota((total, 1) if axis == 0 else (1, total), axis)
    index = jnp.full(place.shape, -1, jnp.int32)
    for start, (side, ends) in zip(starts, BLOCKS):
        base, step = lines[side]
        index = jnp.where((place >= start) & (place < start + extent), base + step * (place - start), index)
        for i, q in enumerate(ends):
            index = jnp.where(place == start + extent + i, pixels[q], index)
    return index


def seam_scatter(lines, pixels, extent):
    return (iota((extent * extent, 1), 0) == block_index(lines, pixels, 1, extent)).astype(F32).astype(BF16)


def column_scatter(extent):
    lane = iota((1, 4 * extent), 1)
    target = (lane % extent) * extent + jnp.where(lane < 2 * extent, extent - 1, 0)
    return (iota((extent * extent, 1), 0) == target).astype(F32).astype(BF16)


def gather_blocks(choice, image, extent):
    strips = dot(choice, image).astype(BF16)
    starts = block_starts(extent)
    return [strips[start : start + rows] for start, rows in zip(starts, block_rows(extent))]


def write_routes(a_blocks, b_blocks, plan, out_refs, extent):
    side_at = {side: i for i, (side, _) in enumerate(BLOCKS)}
    corner_at = {q: (i, extent + j) for i, (_, corners) in enumerate(BLOCKS) for j, q in enumerate(corners)}
    for route, out in zip(plan, out_refs):
        at = 0
        for kind, side in route[1]:
            blocks = a_blocks if kind == "a" else b_blocks
            out[at : at + extent, :] = blocks[side_at[side]][:extent]
            at += extent
        if route[2]:
            rows = iota((16, 1), 0)
            tile = jnp.zeros((16, out.shape[1]), F32)
            for i, (kind, q) in enumerate(route[2]):
                block, row = corner_at[q]
                source = (a_blocks if kind == "ac" else b_blocks)[block][extent : extent + 16].astype(F32)
                tile = jnp.where(rows == i, source[row - extent : row - extent + 1], tile)
            out[at : at + 16, :] = tile.astype(BF16)


def read_routes(plan, in_refs, extent):
    sides, corners = {}, {}
    for route, ref in zip(plan, in_refs):
        at = 0
        for key in route[1]:
            sides[key] = ref[at : at + extent, :]
            at += extent
        if route[2]:
            tile = ref[at : at + 16, :].astype(F32)
            for i, key in enumerate(route[2]):
                corners[key] = tile[i : i + 1]
    result = []
    rows = iota((16, 1), 0)
    for kind in ("a", "b"):
        blocks = []
        for side, ends in BLOCKS:
            block = sides[(kind, side)]
            if ends:
                tile = jnp.zeros((16, block.shape[1]), F32)
                for i, q in enumerate(ends):
                    tile = jnp.where(rows == i, corners[(kind + "c", q)], tile)
                block = jnp.concatenate([block, tile.astype(BF16)], axis=0)
            blocks.append(block)
        result.append(blocks)
    return result


def relayed(tiles):
    return tiles == 8


def write_near(a_blocks, b_blocks, near_ref, extent):
    for i, block in enumerate((a_blocks[3], b_blocks[2], a_blocks[2], b_blocks[3])):
        near_ref[i * extent : (i + 1) * extent, :] = block
    rows = iota((16, 1), 0)
    tile = jnp.zeros((16, near_ref.shape[1]), F32)
    at = 0
    for blocks in (a_blocks, b_blocks):
        ends = [blocks[i][extent : extent + 16].astype(F32) for i in range(2)]
        for block, row in ((0, 0), (0, 1), (1, 1), (1, 0)):
            tile = jnp.where(rows == at, ends[block][row : row + 1], tile)
            at += 1
    near_ref[4 * extent : 4 * extent + 16, :] = tile.astype(BF16)


def write_far(a_blocks, b_blocks, far_ref, extent):
    for i, block in enumerate((a_blocks[0], a_blocks[1], b_blocks[0], b_blocks[1])):
        far_ref[i * extent : (i + 1) * extent, :] = block[:extent]


def near_starts(tile, extent):
    right = tile % 2
    odd = (tile // 2) % 2
    corners = 2 * extent + 16
    side = jnp.where(right == 1, 0, 2 * extent)
    one = jnp.where(right == odd, corners, side)
    three = jnp.where(right == odd, side, corners)
    return side_of_partner(right, extent), one, three


def side_of_partner(right, extent):
    return jnp.where(right == 1, 2 * extent, 0)


def read_relay(refs, extent):
    across, one, three, far, opposite = refs
    mine = lax.axis_index("tile")
    left = mine % 2 == 0
    odd = (mine // 2 + mine) % 2 == 1

    def rows_of(ref, start, count):
        return ref[start : start + count, :].astype(F32)

    def choose(start, count):
        return jnp.where(odd, rows_of(one, start, count), rows_of(three, start, count))

    pair = [(rows_of(across, i * extent, extent), choose(i * extent, extent)) for i in range(2)]
    a_east, b_west = [jnp.where(left, here, there).astype(BF16) for here, there in pair]
    a_west, b_east = [jnp.where(left, there, here).astype(BF16) for here, there in pair]
    tail = 2 * extent - 16
    beside = jnp.where(odd, rows_of(three, tail, 16), rows_of(one, tail, 16))
    beyond = opposite[0:16, :].astype(F32)
    third = jnp.where(left, beside, beyond)
    fifth = jnp.where(left, beyond, beside)
    corners = {("a", 0): third[0:1], ("a", 3): third[3:4], ("b", 1): third[5:6], ("b", 2): third[6:7]}
    corners.update({("a", 1): fifth[1:2], ("a", 2): fifth[2:3], ("b", 0): fifth[4:5], ("b", 3): fifth[7:8]})
    rows = iota((16, 1), 0)
    result = []
    for kind, first, east, west in (("a", 0, a_east, a_west), ("b", 2, b_east, b_west)):
        blocks = []
        for i, ends in enumerate(((0, 1), (3, 2))):
            tile = jnp.where(rows == 0, corners[(kind, ends[0])], jnp.where(rows == 1, corners[(kind, ends[1])], 0.0))
            strip = far[(first + i) * extent : (first + i + 1) * extent, :]
            blocks.append(jnp.concatenate([strip, tile.astype(BF16)], axis=0))
        result.append(blocks + [east, west])
    return result


def shifted(image, by, extent):
    if by == 0:
        return image
    column = iota((image.shape[0], 1), 0) % extent
    rolled = pltpu.roll(image, (-by) % image.shape[0], 0)
    return jnp.where(column == (extent - 1 if by == 1 else 0), 0.0, rolled)


def write_columns(q_ref, image, forward, extent):
    count, channels = image.shape
    zero = jnp.zeros((extent, q_ref.shape[1]), BF16)
    q_ref[0:extent, :] = zero
    q_ref[extent + count : 2 * extent + count, :] = zero
    wide = image.astype(F32)
    for b in range(3):
        by = b - 1 if forward else 1 - b
        q_ref[extent : extent + count, b * channels : (b + 1) * channels] = shifted(wide, by, extent).astype(BF16)


def window_product(q_ref, weight, forward, extent, chunk=256):
    count = q_ref.shape[0] - 2 * extent
    channels = weight.shape[1]
    if not forward:
        weight = tap_columns(weight, range(9), channels)
    pieces = []
    for start in range(0, count, chunk):
        rows = [q_ref[(a if forward else 2 - a) * extent + start : (a if forward else 2 - a) * extent + start + chunk, :] for a in range(3)]
        pieces.append((dot if forward else dot_nt)(jnp.concatenate(rows, axis=1), weight))
    return jnp.concatenate(pieces, axis=0)


def tap_weight(weight, taps, channels):
    return jnp.concatenate([weight[t * channels : (t + 1) * channels, :] for t in taps], axis=0)


def tap_columns(weight, taps, channels):
    return jnp.concatenate([weight[t * channels : (t + 1) * channels, :] for t in taps], axis=1)


def halves(values):
    high = values.astype(BF16)
    return high, (values - high.astype(F32)).astype(BF16)


def margin_adds(strips, weight, extent):
    channels = strips[0].shape[1]
    adds = []
    for position, (side, ends) in enumerate(BLOCKS):
        middle = strips[position][:extent].astype(F32)
        row = iota((extent, 1), 0)
        before, after = 0.0, 0.0
        if ends:
            tile = strips[position][extent : extent + 16].astype(F32)
            before, after = tile[0:1], tile[1:2]
        left = jnp.where(row == 0, before, pltpu.roll(middle, 1, 0))
        right = jnp.where(row == extent - 1, after, pltpu.roll(middle, extent - 1, 0))
        window = jnp.concatenate([left, middle, right], axis=1).astype(BF16)
        adds.append(dot(window, tap_weight(weight, block_taps(position), channels)))
    return adds


def margin_forward(strips, weight, columns, extent):
    count = extent * extent
    adds = margin_adds(strips, weight, extent)
    spread = jnp.concatenate(list(halves(adds[2])) + list(halves(adds[3])), axis=0)
    image = dot(columns, spread)
    top = image[:extent] + adds[0]
    bottom = image[count - extent :] + adds[1]
    return jnp.concatenate([top, image[extent : count - extent], bottom], axis=0)


def strip_columns(strips, extent):
    result = []
    for position, (side, ends) in enumerate(BLOCKS):
        middle = strips[position][:extent].astype(F32)
        row = iota((extent, 1), 0)
        after = jnp.where(row == extent - 1, 0.0, pltpu.roll(middle, extent - 1, 0))
        before = jnp.where(row == 0, 0.0, pltpu.roll(middle, 1, 0))
        columns = jnp.concatenate([after, middle, before], axis=1)
        if ends:
            tile = strips[position][extent : extent + 16].astype(F32)
            row = iota((16, 1), 0)
            low = jnp.where(row == 0, tile, 0.0)
            high = jnp.where(row == 1, tile, 0.0)
            columns = jnp.concatenate([columns, jnp.concatenate([low, jnp.zeros_like(tile), high], axis=1)], axis=0)
        result.append(columns.astype(BF16))
    return result


def margin_backward(columns, weight, scatter, extent):
    channels = weight.shape[1]
    adds = [dot_nt(columns[i], tap_columns(weight, block_taps(i), channels)) for i in range(4)]
    high, low = halves(jnp.concatenate(adds, axis=0))
    return dot(scatter, high) + dot(scatter, low)


def weight_sum(out_ref, image_t, q_ref, extent):
    channels = image_t.shape[0]
    count = image_t.shape[1]
    for a in range(3):
        product = dot(image_t, q_ref[(2 - a) * extent : (2 - a) * extent + count, :])
        for b in range(3):
            tap = 3 * a + b
            out_ref[tap * channels : (tap + 1) * channels, :] = product[:, b * channels : (b + 1) * channels]


def margin_weight(strips, columns):
    channels = strips[0].shape[1]
    wide = [dot_t(strips[i], columns[i]) for i in range(4)]
    result = []
    for tap in range(9):
        value = None
        for position in range(4):
            taps = block_taps(position)
            if tap in taps:
                at = taps.index(tap)
                part = wide[position][:, at * channels : (at + 1) * channels]
                value = part if value is None else value + part
        result.append(value)
    return result


def border_index(place, extent, unique):
    last = extent - 1
    part, j = place // extent, place % extent
    index = jnp.where(part == 0, j, jnp.where(part == 1, extent * last + j, jnp.where(part == 2, extent * j + last, extent * j)))
    if unique:
        index = jnp.where((part >= 2) & ((j == 0) | (j == last)), -2, index)
    return index


def border_choice(extent):
    return pick_rows(border_index(iota((4 * extent, 1), 0), extent, True), extent * extent)


def border_of(ref, extent):
    count = extent * extent
    east = ref[pl.ds(extent - 1, extent, stride=extent), :]
    west = ref[pl.ds(0, extent, stride=extent), :]
    return jnp.concatenate([ref[0:extent, :], ref[count - extent : count, :], east, west], axis=0)


def without_repeats(border, extent):
    place = iota((border.shape[0], 1), 0)
    return jnp.where(border_index(place, extent, True) < 0, 0.0, border)


def moved(column, by, extent):
    if by == 0:
        return column
    row = iota((extent, 1), 0)
    return jnp.where(row == (extent - 1 if by == 1 else 0), 0.0, pltpu.roll(column, (-by) % extent, 0))


def border_windows(out_ref, wide_ref, q_ref, forward, extent):
    count, channels = wide_ref.shape
    columns = {c: wide_ref[pl.ds(c, extent, stride=extent), :] for c in (0, 1, extent - 2, extent - 1)}
    nothing = jnp.zeros((extent, channels), F32)
    row = iota((extent, 1), 0)
    inside = (row > 0) & (row < extent - 1)
    for a in range(3):
        start = (a if forward else 2 - a) * extent
        lanes = slice(a * 3 * channels, (a + 1) * 3 * channels)
        out_ref[0:extent, lanes] = q_ref[start : start + extent, :]
        out_ref[extent : 2 * extent, lanes] = q_ref[start + count - extent : start + count, :]
        for part, column in ((2, extent - 1), (3, 0)):
            pieces = []
            for b in range(3):
                at = column + (b - 1 if forward else 1 - b)
                pieces.append(moved(columns[at], a - 1 if forward else 1 - a, extent) if at in columns else nothing)
            value = jnp.where(inside, jnp.concatenate(pieces, axis=1), 0.0)
            out_ref[part * extent : (part + 1) * extent, lanes] = value.astype(BF16)


def gelu_parts(u):
    scale = math.sqrt(2.0 / math.pi)
    square = u * u
    t = jnp.tanh(scale * (u + 0.044715 * (square * u)))
    value = 0.5 * u * (1.0 + t)
    slope = 0.5 * (1.0 + t) + (0.5 * u) * (1.0 - t * t) * (scale * (1.0 + 3.0 * 0.044715 * square))
    return value, slope


def call(kernel, name, outs, ins, operands, scratch=(), flops=0, limit=LIMIT):
    specs = [pl.BlockSpec(memory_space={"a": pl.ANY, "s": pltpu.SMEM, "v": pltpu.VMEM}[i]) for i in ins]
    moved = sum(math.prod(o.shape) * o.dtype.itemsize for o in list(outs) + list(operands))
    return pl.pallas_call(
        kernel,
        name=name,
        out_shape=outs,
        in_specs=specs,
        out_specs=[pl.BlockSpec(memory_space=pltpu.VMEM) for _ in outs],
        scratch_shapes=list(scratch),
        cost_estimate=pl.CostEstimate(flops=flops, bytes_accessed=moved, transcendentals=0),
        compiler_params=pltpu.CompilerParams(vmem_limit_bytes=limit),
    )(*operands)


def sds(shape, dtype):
    return jax.ShapeDtypeStruct(shape, dtype)


def exchange(payloads, plan, tiles):
    return [
        lax.ppermute(p, "tile", [(i, (i + route[0]) % tiles) for i in range(tiles)]) for p, route in zip(payloads, plan)
    ]


def swap(value, mask, total):
    return lax.ppermute(value, AXES, [(i, i ^ mask) for i in range(total)])


def reduce_gradients(keep, send, total, work, near=None, far=None):
    rows, channels = keep.shape
    quarter = rows // 4
    wire = BF16 if total <= 32 else F32
    me = lax.axis_index(AXES)
    other = swap(send, 1, total)
    plane = (me >> 1) & 3

    def chunk(index):
        first = lax.dynamic_index_in_dim(keep.reshape(4, quarter, channels), index, 0, keepdims=False)
        second = lax.dynamic_index_in_dim(other.reshape(4, quarter, channels), index, 0, keepdims=False)
        return first + second.astype(F32)

    arrived = {}
    for m in (3, 1, 2):
        message = chunk(plane ^ m).astype(wire)
        if m == 2 and near is not None:
            message = jnp.concatenate([message, near], axis=0)
        arrived[m] = swap(message, m << 1, total)
    part = chunk(plane)
    for m in (3, 1, 2):
        part = part + arrived[m][:quarter].astype(F32)
    part, done = work(part)
    extras = None
    if near is not None:
        across = arrived[2][quarter:]
        extent = far.shape[0] // 4
        starts = near_starts(lax.axis_index("tile") ^ 1, extent)
        direct, one, three = [lax.dynamic_slice_in_dim(across, start, 2 * extent, 0) for start in starts]
        riders = {1: (one,), 2: (far, across[-16:]), 3: (three,)}
    bit = 8
    while bit < total:
        mine = part.astype(wire)
        if 2 * bit < total:
            got = {}
            for m in (3, 2, 1):
                message = mine
                if near is not None:
                    message = jnp.concatenate([mine, *riders[m]], axis=0)
                got[m] = swap(message, m * bit, total)
            part = (mine.astype(F32) + got[1][:quarter].astype(F32)) + (got[2][:quarter].astype(F32) + got[3][:quarter].astype(F32))
            if near is not None:
                extras = [direct, got[1][quarter:], got[3][quarter:], got[2][quarter:-16], got[2][-16:]]
            bit *= 4
        else:
            part = mine.astype(F32) + swap(mine, bit, total).astype(F32)
            bit *= 2
    part, done = lax.optimization_barrier((part, done))
    mine = part.astype(wire)
    ring = jnp.stack([mine] + [swap(mine, m << 1, total) for m in (1, 2, 3)])
    whole = jnp.concatenate([lax.dynamic_index_in_dim(ring, plane ^ j, 0) for j in range(4)], axis=0)
    return whole, extras, done


def join_cores(whole, total):
    other = swap(whole, 1, total)
    low = (lax.axis_index(AXES) & 1) == 0
    return jnp.where(low, whole, other), jnp.where(low, other, whole)


def reach_neighbours(across, one, three, far, corners, total):
    return [swap(across, 4, total), swap(one, 12, total), swap(three, 28, total), swap(far, 16, total), swap(corners, 20, total)]


def per_device(inputs, weight_one, weight_two, cotangent, edge_code, corner_code):
    tiles, members = lax.axis_size("tile"), lax.axis_size("dp")
    extent, channels = inputs.shape[2], inputs.shape[4]
    count = extent * extent
    factor = 1.0 / math.sqrt(inputs.shape[0] * members * tiles * count)
    source = inputs.reshape(count, channels)
    grad_out = cotangent.reshape(count, channels)
    w_one = weight_one.reshape(9 * channels, channels)
    w_two = weight_two.reshape(9 * channels, channels)
    plan = routes(tiles)
    total = tiles * members
    hops = relayed(tiles)
    near_b, far_b, corner_b = sds((4 * extent + 16, channels), BF16), sds((4 * extent, channels), BF16), sds((16, channels), BF16)
    pair_b = sds((2 * extent, channels), BF16)
    if hops:
        first_routed, second_routed = [pair_b, pair_b, pair_b, far_b, corner_b], [near_b, far_b]
        n_routes = 5
    else:
        first_routed = second_routed = [sds((route_rows(r, extent), channels), BF16) for r in plan]
        n_routes = len(plan)
    n_first, n_second = len(first_routed), len(second_routed)

    def write_first(a, b, outs, near_ref):
        if hops:
            write_near(a, b, near_ref, extent)
            write_far(a, b, outs[3], extent)
            for start, out in zip(near_starts(lax.axis_index("tile"), extent), outs):
                out[...] = near_ref[pl.ds(pl.multiple_of(start, 16), 2 * extent), :]
            outs[4][...] = near_ref[4 * extent : 4 * extent + 16, :]
        else:
            write_routes(a, b, plan, outs, extent)

    def write_second(a, b, outs):
        if hops:
            write_near(a, b, outs[0], extent)
            write_far(a, b, outs[1], extent)
        else:
            write_routes(a, b, plan, outs, extent)

    def read(refs):
        return read_relay(refs, extent) if hops else read_routes(plan, refs, extent)

    image_b, image_f = sds((count, channels), BF16), sds((count, channels), F32)
    columns_b = sds((count + 2 * extent, 3 * channels), BF16)
    taps_b, taps_f = sds((9 * channels, channels), BF16), sds((9 * channels, channels), F32)
    conv = 2 * count * 9 * channels * channels

    strip_rows = block_starts(extent)[3] + extent
    scatter_b, column_b = sds((count, strip_rows), BF16), sds((count, 4 * extent), BF16)
    pieces = 2

    def first_strips(x_hbm, g_hbm, edge_hbm, corner_hbm, *refs):
        outs = refs[:n_first]
        x_ref, g_ref, near_ref, edge_ref, corner_ref, sems = refs[n_first:]
        pairs = [(edge_hbm, edge_ref), (corner_hbm, corner_ref)]
        step = count // pieces
        for source_ref, target_ref in ((x_hbm, x_ref), (g_hbm, g_ref)):
            for i in range(pieces):
                pairs.append((source_ref.at[pl.ds(i * step, step)], target_ref.at[pl.ds(i * step, step)]))
        copies = [pltpu.make_async_copy(a, b, sems.at[i]) for i, (a, b) in enumerate(pairs)]
        for copy in copies:
            copy.start()
        fixed = block_choice(*fixed_lines(extent), extent)
        for copy in copies[:2]:
            copy.wait()
        seam = block_choice(*seam_lines(edge_ref, corner_ref, extent), extent)
        for copy in copies[2:]:
            copy.wait()
        a = gather_blocks(seam, x_ref[...], extent)
        b = gather_blocks(fixed, g_ref[...], extent)
        write_first(a, b, outs, near_ref)

    first = call(
        first_strips,
        "first_strips",
        first_routed,
        "aaaa",
        (source, grad_out, edge_code.T, corner_code.T),
        scratch=[
            pltpu.VMEM((count, channels), BF16),
            pltpu.VMEM((count, channels), BF16),
            pltpu.VMEM(near_b.shape, BF16),
            pltpu.SMEM((4, tiles), jnp.int32),
            pltpu.SMEM((4, tiles), jnp.int32),
            pltpu.SemaphoreType.DMA((2 + 2 * pieces,)),
        ],
        limit=ALONE,
        flops=10 * conv,
    )
    first_arrived = reach_neighbours(*first, total) if hops else exchange(first, plan, tiles)

    border = 4 * extent
    border_b, border_f = sds((border, channels), BF16), sds((border, channels), F32)
    windows_b = sds((border, 9 * channels), BF16)

    def inner(edge_ref, corner_ref, x_ref, g_ref, w1_ref, w2_ref, *refs):
        hid_ref, dpre_ref, preb_ref, dhb_ref, sum_ref, seam_ref, back_ref, wx_ref, wg_ref = refs[:9]
        qx_ref, qg_ref, qd_ref, pre_ref, dh_ref, wide_ref = refs[9:]
        wide_ref[...] = x_ref[...].astype(F32)
        write_columns(qx_ref, x_ref[...], True, extent)
        border_windows(wx_ref, wide_ref, qx_ref, True, extent)
        pre_ref[...] = window_product(qx_ref, w1_ref[...], True, extent)
        wide_ref[...] = g_ref[...].astype(F32)
        write_columns(qg_ref, g_ref[...], False, extent)
        border_windows(wg_ref, wide_ref, qg_ref, False, extent)
        dh_ref[...] = window_product(qg_ref, w2_ref[...], False, extent)
        preb_ref[...] = border_of(pre_ref, extent)
        dhb_ref[...] = border_of(dh_ref, extent)
        place = iota((count, 1), 0)
        row, column = place // extent, place % extent
        inside = (row > 0) & (row < extent - 1) & (column > 0) & (column < extent - 1)
        value, slope = gelu_parts(pre_ref[...])
        value = jnp.where(inside, value, 0.0)
        hid_ref[...] = value.astype(BF16)
        dpre_ref[...] = jnp.where(inside, dh_ref[...] * slope, 0.0).astype(BF16)
        write_columns(qd_ref, dpre_ref[...], False, extent)
        weight_sum(sum_ref.at[0], jnp.transpose(x_ref[...].astype(F32)).astype(BF16), qd_ref, extent)
        weight_sum(sum_ref.at[1], jnp.transpose(value).astype(BF16), qg_ref, extent)
        lines, pixels = seam_lines(edge_ref, corner_ref, extent)
        across = border_index(iota((1, border), 1), extent, True)
        seam_ref[...] = (block_index(lines, pixels, 0, extent) == across).astype(F32).astype(BF16)
        down = border_index(iota((border, 1), 0), extent, False)
        back_ref[...] = (down == block_index(lines, pixels, 1, extent)).astype(F32).astype(BF16)

    hid_in, dpre_in, pre_b, dh_b, sums, seam_b, back_b, wx_b, wg_b = call(
        inner,
        "inner_products",
        [
            image_b,
            image_b,
            border_f,
            border_f,
            sds((2,) + taps_f.shape, F32),
            sds((strip_rows, border), BF16),
            sds((border, strip_rows), BF16),
            windows_b,
            windows_b,
        ],
        "ssvvvv",
        (edge_code.T, corner_code.T, source, grad_out, w_one, w_two),
        scratch=[pltpu.VMEM(columns_b.shape, BF16)] * 3 + [pltpu.VMEM(image_f.shape, F32)] * 3,
        flops=4 * conv,
    )

    def middle(preb_ref, dhb_ref, sums_ref, seam_ref, back_ref, wx_ref, wg_ref, w1_ref, w2_ref, *refs):
        arrived = refs[:n_routes]
        keep_ref, send_ref, hid_ref, dpre_ref = refs[n_routes : n_routes + 4]
        outs = refs[n_routes + 4 : n_routes + 4 + n_second]
        (sum_ref,) = refs[n_routes + 4 + n_second :]
        x_strips, g_strips = read(arrived)
        columns = strip_columns(g_strips, extent)
        adds = margin_adds(x_strips, w1_ref[...], extent)
        row = iota((extent, 1), 0)
        first, final = row == 0, row == extent - 1

        def ends(low, high):
            return jnp.where(first, low, 0.0) + jnp.where(final, high, 0.0)

        def end_rows(part):
            return adds[part][0:1], adds[part][extent - 1 : extent]

        (east_low, east_high), (west_low, west_high) = end_rows(2), end_rows(3)
        north = preb_ref[0:extent, :] + adds[0] + ends(west_low, east_low)
        south = preb_ref[extent : 2 * extent, :] + adds[1] + ends(west_high, east_high)

        def side(part, at):
            value = preb_ref[part * extent : (part + 1) * extent, :] + adds[part]
            return jnp.where(first, north[at : at + 1], jnp.where(final, south[at : at + 1], value))

        value, slope = gelu_parts(jnp.concatenate([north, south, side(2, extent - 1), side(3, 0)], axis=0))
        dadds = [dot_nt(columns[i], tap_columns(w2_ref[...], block_taps(i), channels)) for i in range(4)]
        high, low = halves(jnp.concatenate(dadds, axis=0))
        d_hidden = dhb_ref[...] + dot(back_ref[...], high) + dot(back_ref[...], low)
        d_pre = d_hidden * slope
        hidden = without_repeats(value, extent).astype(BF16)
        hid_ref[...] = hidden
        d_once = without_repeats(d_pre, extent).astype(BF16)
        dpre_ref[...] = d_once
        strips = dot(seam_ref[...], hidden).astype(BF16)
        a = [strips[start : start + rows] for start, rows in zip(block_starts(extent), block_rows(extent))]
        b = []
        tall = iota((16, 1), 0)
        for part in range(4):
            block = d_pre[part * extent : (part + 1) * extent]
            if part < 2:
                tile = jnp.where(tall == 0, block[0:1], jnp.where(tall == 1, block[extent - 1 : extent], 0.0))
                block = jnp.concatenate([block, tile], axis=0)
            b.append(block.astype(BF16))
        write_second(a, b, outs)
        own = dot_t(wx_ref[...], d_once)
        margin = margin_weight(x_strips, strip_columns(b, extent))
        for tap in range(9):
            span = slice(tap * channels, (tap + 1) * channels)
            total = sums_ref[0, span, :] + own[span]
            sum_ref[0, span, :] = total if margin[tap] is None else total + margin[tap]
        own = dot_t(hidden, wg_ref[...])
        margin = margin_weight(a, columns)
        for tap in range(9):
            span = slice(tap * channels, (tap + 1) * channels)
            total = sums_ref[1, span, :] + own[:, span]
            sum_ref[1, span, :] = total if margin[tap] is None else total + margin[tap]
        core = lax.axis_index("dp") % 2
        keep_ref[...] = sum_ref[core]
        send_ref[...] = sum_ref[1 - core].astype(BF16)

    results = call(
        middle,
        "gradients",
        [taps_f, taps_b, border_b, border_b] + second_routed,
        "v" * (9 + n_routes),
        (pre_b, dh_b, sums, seam_b, back_b, wx_b, wg_b, w_one, w_two, *first_arrived),
        scratch=[pltpu.VMEM((2,) + taps_f.shape, F32)],
        flops=conv // 4,
    )
    keep, send, hid_edge, dpre_edge = results[:4]

    def later(edge_ref, corner_ref, x_ref, g_ref, hid_ref, dpre_ref, hidb_ref, dpreb_ref, w1_ref, w2_ref, out_ref, dx_ref, scatter_ref, column_ref, q_ref):
        lines, pixels = seam_lines(edge_ref, corner_ref, extent)
        scatter_ref[...] = seam_scatter(lines, pixels, extent)
        column_ref[...] = column_scatter(extent)
        choice = border_choice(extent)
        hidden = hid_ref[...].astype(F32) + dot_t(choice, hidb_ref[...])
        d_pre = dpre_ref[...].astype(F32) + dot_t(choice, dpreb_ref[...])
        write_columns(q_ref, hidden, True, extent)
        out_ref[...] = x_ref[...].astype(F32) + window_product(q_ref, w2_ref[...], True, extent)
        write_columns(q_ref, d_pre, False, extent)
        dx_ref[...] = g_ref[...].astype(F32) + window_product(q_ref, w1_ref[...], False, extent)

    def later_parts(token):
        token, inner_arrays = lax.optimization_barrier((token, (hid_in, dpre_in, hid_edge, dpre_edge)))
        return token, call(
            later,
            "later_products",
            [image_f, image_f, scatter_b, column_b],
            "ss" + "v" * 8,
            (edge_code.T, corner_code.T, source, grad_out, *inner_arrays, w_one, w_two),
            scratch=[pltpu.VMEM(columns_b.shape, BF16)],
            flops=2 * conv,
        )

    if hops:
        whole, second_arrived, parts = reduce_gradients(keep, send, total, later_parts, *results[4:])
    else:
        second_arrived = exchange(results[4:], plan, tiles)
        whole, _, parts = reduce_gradients(keep, send, total, later_parts)

    def last(part_ref, dpart_ref, scatter_ref, column_ref, w1_ref, w2_ref, *refs):
        arrived = refs[:n_routes]
        out_ref, dx_ref = refs[n_routes:]
        h_strips, d_strips = read(arrived)
        out_ref[...] = (part_ref[...] + margin_forward(h_strips, w2_ref[...], column_ref[...], extent)).astype(BF16)
        add = margin_backward(strip_columns(d_strips, extent), w1_ref[...], scatter_ref[...], extent)
        dx_ref[...] = (dpart_ref[...] + add).astype(BF16)

    output, d_input = call(
        last,
        "outputs",
        [image_b, image_b],
        "v" * (6 + n_routes),
        (*parts, w_one, w_two, *second_arrived),
        flops=conv // 4,
    )
    whole, output, d_input = lax.optimization_barrier((whole, output, d_input))
    one, two = join_cores(whole, total)
    shape = (9, channels, channels)
    return (
        output.reshape(inputs.shape),
        d_input.reshape(inputs.shape),
        (one.astype(F32) * factor).reshape(shape),
        (two.astype(F32) * factor).reshape(shape),
    )


def solution(mesh):
    split = P("dp", "tile", None, None, None)
    return jax.shard_map(
        per_device,
        mesh=mesh,
        in_specs=(split, P(), P(), split, P(), P()),
        out_specs=(split, split, P(), P()),
        check_vma=False,
    )
```

```python
import math

import jax
import jax.numpy as jnp
from jax import lax
from jax.experimental import pallas as pl
from jax.experimental.pallas import tpu as pltpu
from jax.sharding import PartitionSpec as P

RW = 4
SIDES = (-RW, 1, RW, -1)
CORNERS = (-RW - 1, -RW + 1, RW + 1, RW - 1)
F32 = jnp.float32
BF16 = jnp.bfloat16
AXES = ("tile", "dp")
LIMIT = 20 * 1024 * 1024
ALONE = 60 * 1024 * 1024

BLOCKS = ((0, (0, 1)), (2, (3, 2)), (1, ()), (3, ()))


def block_rows(extent):
    return (extent + 16, extent + 16, extent, extent)


def block_starts(extent):
    rows = block_rows(extent)
    return (0, rows[0], rows[0] + rows[1], rows[0] + rows[1] + rows[2])


def block_taps(position):
    return ((0, 1, 2), (6, 7, 8), (2, 5, 8), (0, 3, 6))[position]


def routes(tiles):
    found = {}
    for kind, offsets in (("a", SIDES), ("b", SIDES), ("ac", CORNERS), ("bc", CORNERS)):
        for which, offset in enumerate(offsets):
            distance = (-offset if kind[0] == "a" else offset) % tiles
            found.setdefault(distance, []).append((kind, which))
    plan = []
    for distance, parts in found.items():
        sides = [p for p in parts if len(p[0]) == 1]
        corners = [p for p in parts if len(p[0]) == 2]
        plan.append((distance, sides, corners))
    return plan


def route_rows(route, extent):
    return extent * len(route[1]) + (16 if route[2] else 0)


def iota(shape, axis):
    return lax.broadcasted_iota(jnp.int32, shape, axis)


def dot(a, b):
    return lax.dot_general(a, b, (((1,), (0,)), ((), ())), preferred_element_type=F32)


def dot_nt(a, b):
    return lax.dot_general(a, b, (((1,), (1,)), ((), ())), preferred_element_type=F32)


def dot_t(a, b):
    return lax.dot_general(a, b, (((0,), (0,)), ((), ())), preferred_element_type=F32)


def corner_pixel(code, extent):
    last = extent - 1
    return jnp.where(code == 0, 0, jnp.where(code == 1, last, jnp.where(code == 2, extent * extent - 1, extent * last)))


def side_line(code, extent):
    last = extent - 1
    border = code % 4
    base = jnp.where(border == 1, last, jnp.where(border == 2, extent * last, 0))
    step = jnp.where(border % 2 == 0, 1, extent)
    return jnp.where(code >= 4, base + last * step, base), jnp.where(code >= 4, -step, step)


def seam_lines(edge_ref, corner_ref, extent):
    tiles = edge_ref.shape[1]
    mine = lax.axis_index("tile")
    lines = [side_line(edge_ref[k, (mine - o + tiles + RW * tiles) % tiles], extent) for k, o in enumerate(SIDES)]
    pixels = [corner_pixel(corner_ref[q, (mine - o + tiles + RW * tiles) % tiles], extent) for q, o in enumerate(CORNERS)]
    return lines, pixels


def fixed_lines(extent):
    last = extent - 1
    lines = [(0, 1), (last, extent), (extent * last, 1), (0, extent)]
    return lines, [0, last, extent * extent - 1, extent * last]


def pick_rows(indices, count):
    return (iota((indices.shape[0], count), 1) == indices).astype(F32).astype(BF16)


def line_rows(line, extent, count):
    return pick_rows(line[0] + line[1] * iota((extent, 1), 0), count)


def spot_rows(spots, count):
    rows = iota((16, 1), 0)
    index = jnp.full((16, 1), -1, jnp.int32)
    for row, pixel in spots:
        index = jnp.where(rows == row, pixel, index)
    return pick_rows(index, count)


def block_choice(lines, pixels, extent):
    count = extent * extent
    rows = []
    for side, corners in BLOCKS:
        rows.append(line_rows(lines[side], extent, count))
        if corners:
            rows.append(spot_rows([(i, pixels[q]) for i, q in enumerate(corners)], count))
    return jnp.concatenate(rows, axis=0)


def block_index(lines, pixels, axis, extent):
    starts = block_starts(extent)
    total = starts[3] + extent
    place = iota((total, 1) if axis == 0 else (1, total), axis)
    index = jnp.full(place.shape, -1, jnp.int32)
    for start, (side, ends) in zip(starts, BLOCKS):
        base, step = lines[side]
        index = jnp.where((place >= start) & (place < start + extent), base + step * (place - start), index)
        for i, q in enumerate(ends):
            index = jnp.where(place == start + extent + i, pixels[q], index)
    return index


def seam_scatter(lines, pixels, extent):
    return (iota((extent * extent, 1), 0) == block_index(lines, pixels, 1, extent)).astype(F32).astype(BF16)


def column_scatter(extent):
    lane = iota((1, 4 * extent), 1)
    target = (lane % extent) * extent + jnp.where(lane < 2 * extent, extent - 1, 0)
    return (iota((extent * extent, 1), 0) == target).astype(F32).astype(BF16)


def gather_blocks(choice, image, extent):
    strips = dot(choice, image).astype(BF16)
    starts = block_starts(extent)
    return [strips[start : start + rows] for start, rows in zip(starts, block_rows(extent))]


def write_routes(a_blocks, b_blocks, plan, out_refs, extent):
    side_at = {side: i for i, (side, _) in enumerate(BLOCKS)}
    corner_at = {q: (i, extent + j) for i, (_, corners) in enumerate(BLOCKS) for j, q in enumerate(corners)}
    for route, out in zip(plan, out_refs):
        at = 0
        for kind, side in route[1]:
            blocks = a_blocks if kind == "a" else b_blocks
            out[at : at + extent, :] = blocks[side_at[side]][:extent]
            at += extent
        if route[2]:
            rows = iota((16, 1), 0)
            tile = jnp.zeros((16, out.shape[1]), F32)
            for i, (kind, q) in enumerate(route[2]):
                block, row = corner_at[q]
                source = (a_blocks if kind == "ac" else b_blocks)[block][extent : extent + 16].astype(F32)
                tile = jnp.where(rows == i, source[row - extent : row - extent + 1], tile)
            out[at : at + 16, :] = tile.astype(BF16)


def read_routes(plan, in_refs, extent):
    sides, corners = {}, {}
    for route, ref in zip(plan, in_refs):
        at = 0
        for key in route[1]:
            sides[key] = ref[at : at + extent, :]
            at += extent
        if route[2]:
            tile = ref[at : at + 16, :].astype(F32)
            for i, key in enumerate(route[2]):
                corners[key] = tile[i : i + 1]
    result = []
    rows = iota((16, 1), 0)
    for kind in ("a", "b"):
        blocks = []
        for side, ends in BLOCKS:
            block = sides[(kind, side)]
            if ends:
                tile = jnp.zeros((16, block.shape[1]), F32)
                for i, q in enumerate(ends):
                    tile = jnp.where(rows == i, corners[(kind + "c", q)], tile)
                block = jnp.concatenate([block, tile.astype(BF16)], axis=0)
            blocks.append(block)
        result.append(blocks)
    return result


def relayed(tiles):
    return tiles == 8


def write_near(a_blocks, b_blocks, near_ref, extent):
    for i, block in enumerate((a_blocks[3], b_blocks[2], a_blocks[2], b_blocks[3])):
        near_ref[i * extent : (i + 1) * extent, :] = block
    rows = iota((16, 1), 0)
    tile = jnp.zeros((16, near_ref.shape[1]), F32)
    at = 0
    for blocks in (a_blocks, b_blocks):
        ends = [blocks[i][extent : extent + 16].astype(F32) for i in range(2)]
        for block, row in ((0, 0), (0, 1), (1, 1), (1, 0)):
            tile = jnp.where(rows == at, ends[block][row : row + 1], tile)
            at += 1
    near_ref[4 * extent : 4 * extent + 16, :] = tile.astype(BF16)


def write_far(a_blocks, b_blocks, far_ref, extent):
    for i, block in enumerate((a_blocks[0], a_blocks[1], b_blocks[0], b_blocks[1])):
        far_ref[i * extent : (i + 1) * extent, :] = block[:extent]


def near_starts(tile, extent):
    right = tile % 2
    odd = (tile // 2) % 2
    corners = 2 * extent + 16
    side = jnp.where(right == 1, 0, 2 * extent)
    one = jnp.where(right == odd, corners, side)
    three = jnp.where(right == odd, side, corners)
    return side_of_partner(right, extent), one, three


def side_of_partner(right, extent):
    return jnp.where(right == 1, 2 * extent, 0)


def read_relay(refs, extent):
    across, one, three, far, opposite = refs
    mine = lax.axis_index("tile")
    left = mine % 2 == 0
    odd = (mine // 2 + mine) % 2 == 1

    def rows_of(ref, start, count):
        return ref[start : start + count, :].astype(F32)

    def choose(start, count):
        return jnp.where(odd, rows_of(one, start, count), rows_of(three, start, count))

    pair = [(rows_of(across, i * extent, extent), choose(i * extent, extent)) for i in range(2)]
    a_east, b_west = [jnp.where(left, here, there).astype(BF16) for here, there in pair]
    a_west, b_east = [jnp.where(left, there, here).astype(BF16) for here, there in pair]
    tail = 2 * extent - 16
    beside = jnp.where(odd, rows_of(three, tail, 16), rows_of(one, tail, 16))
    beyond = opposite[0:16, :].astype(F32)
    third = jnp.where(left, beside, beyond)
    fifth = jnp.where(left, beyond, beside)
    corners = {("a", 0): third[0:1], ("a", 3): third[3:4], ("b", 1): third[5:6], ("b", 2): third[6:7]}
    corners.update({("a", 1): fifth[1:2], ("a", 2): fifth[2:3], ("b", 0): fifth[4:5], ("b", 3): fifth[7:8]})
    rows = iota((16, 1), 0)
    result = []
    for kind, first, east, west in (("a", 0, a_east, a_west), ("b", 2, b_east, b_west)):
        blocks = []
        for i, ends in enumerate(((0, 1), (3, 2))):
            tile = jnp.where(rows == 0, corners[(kind, ends[0])], jnp.where(rows == 1, corners[(kind, ends[1])], 0.0))
            strip = far[(first + i) * extent : (first + i + 1) * extent, :]
            blocks.append(jnp.concatenate([strip, tile.astype(BF16)], axis=0))
        result.append(blocks + [east, west])
    return result


def shifted(image, by, extent):
    if by == 0:
        return image
    column = iota((image.shape[0], 1), 0) % extent
    rolled = pltpu.roll(image, (-by) % image.shape[0], 0)
    return jnp.where(column == (extent - 1 if by == 1 else 0), 0.0, rolled)


def write_columns(q_ref, image, forward, extent):
    count, channels = image.shape
    zero = jnp.zeros((extent, q_ref.shape[1]), BF16)
    q_ref[0:extent, :] = zero
    q_ref[extent + count : 2 * extent + count, :] = zero
    wide = image.astype(F32)
    for b in range(3):
        by = b - 1 if forward else 1 - b
        q_ref[extent : extent + count, b * channels : (b + 1) * channels] = shifted(wide, by, extent).astype(BF16)


def window_product(q_ref, weight, forward, extent, out_ref, chunk=8):
    channels = weight.shape[1]
    if forward:
        taps = tap_weight(weight, range(9), channels)
        nothing = jnp.zeros((3 * channels, channels), weight.dtype)
        both = jnp.concatenate([jnp.concatenate([taps, nothing], axis=0), jnp.concatenate([nothing, taps], axis=0)], axis=1)
    else:
        taps = tap_columns(weight, (6, 7, 8, 3, 4, 5, 0, 1, 2), channels)
        nothing = jnp.zeros((channels, 3 * channels), weight.dtype)
        both = jnp.concatenate([jnp.concatenate([taps, nothing], axis=1), jnp.concatenate([nothing, taps], axis=1)], axis=0)
    for start in range(0, extent // 2, chunk):
        rows = []
        for a in range(4):
            rows.append(jnp.concatenate([q_ref[(2 * i + a) * extent : (2 * i + a + 1) * extent, :] for i in range(start, start + chunk)], axis=0))
        product = (dot if forward else dot_nt)(jnp.concatenate(rows, axis=1), both)
        for i in range(chunk):
            for half in range(2):
                at = (2 * (start + i) + half) * extent
                out_ref[at : at + extent, :] = product[i * extent : (i + 1) * extent, half * channels : (half + 1) * channels]


def tap_weight(weight, taps, channels):
    return jnp.concatenate([weight[t * channels : (t + 1) * channels, :] for t in taps], axis=0)


def tap_columns(weight, taps, channels):
    return jnp.concatenate([weight[t * channels : (t + 1) * channels, :] for t in taps], axis=1)


def halves(values):
    high = values.astype(BF16)
    return high, (values - high.astype(F32)).astype(BF16)


def margin_adds(strips, weight, extent):
    channels = strips[0].shape[1]
    adds = []
    for position, (side, ends) in enumerate(BLOCKS):
        middle = strips[position][:extent].astype(F32)
        row = iota((extent, 1), 0)
        before, after = 0.0, 0.0
        if ends:
            tile = strips[position][extent : extent + 16].astype(F32)
            before, after = tile[0:1], tile[1:2]
        left = jnp.where(row == 0, before, pltpu.roll(middle, 1, 0))
        right = jnp.where(row == extent - 1, after, pltpu.roll(middle, extent - 1, 0))
        window = jnp.concatenate([left, middle, right], axis=1).astype(BF16)
        adds.append(dot(window, tap_weight(weight, block_taps(position), channels)))
    return adds


def margin_forward(strips, weight, columns, extent):
    count = extent * extent
    adds = margin_adds(strips, weight, extent)
    spread = jnp.concatenate(list(halves(adds[2])) + list(halves(adds[3])), axis=0)
    image = dot(columns, spread)
    top = image[:extent] + adds[0]
    bottom = image[count - extent :] + adds[1]
    return jnp.concatenate([top, image[extent : count - extent], bottom], axis=0)


def strip_columns(strips, extent):
    result = []
    for position, (side, ends) in enumerate(BLOCKS):
        middle = strips[position][:extent].astype(F32)
        row = iota((extent, 1), 0)
        after = jnp.where(row == extent - 1, 0.0, pltpu.roll(middle, extent - 1, 0))
        before = jnp.where(row == 0, 0.0, pltpu.roll(middle, 1, 0))
        columns = jnp.concatenate([after, middle, before], axis=1)
        if ends:
            tile = strips[position][extent : extent + 16].astype(F32)
            row = iota((16, 1), 0)
            low = jnp.where(row == 0, tile, 0.0)
            high = jnp.where(row == 1, tile, 0.0)
            columns = jnp.concatenate([columns, jnp.concatenate([low, jnp.zeros_like(tile), high], axis=1)], axis=0)
        result.append(columns.astype(BF16))
    return result


def margin_backward(columns, weight, scatter, extent):
    channels = weight.shape[1]
    adds = [dot_nt(columns[i], tap_columns(weight, block_taps(i), channels)) for i in range(4)]
    high, low = halves(jnp.concatenate(adds, axis=0))
    return dot(scatter, high) + dot(scatter, low)


def weight_sum(out_ref, image_t, q_ref, extent):
    channels = image_t.shape[0]
    count = image_t.shape[1]
    rows = jnp.concatenate([q_ref[(2 - a) * extent : (2 - a) * extent + count, :] for a in range(3)], axis=1)
    product = dot(image_t, rows)
    for tap in range(9):
        out_ref[tap * channels : (tap + 1) * channels, :] = product[:, tap * channels : (tap + 1) * channels]


def margin_weight(strips, columns):
    channels = strips[0].shape[1]
    wide = [dot_t(strips[i], columns[i]) for i in range(4)]
    result = []
    for tap in range(9):
        value = None
        for position in range(4):
            taps = block_taps(position)
            if tap in taps:
                at = taps.index(tap)
                part = wide[position][:, at * channels : (at + 1) * channels]
                value = part if value is None else value + part
        result.append(value)
    return result


def border_index(place, extent, unique):
    last = extent - 1
    part, j = place // extent, place % extent
    index = jnp.where(part == 0, j, jnp.where(part == 1, extent * last + j, jnp.where(part == 2, extent * j + last, extent * j)))
    if unique:
        index = jnp.where((part >= 2) & ((j == 0) | (j == last)), -2, index)
    return index


def border_choice(extent):
    return pick_rows(border_index(iota((4 * extent, 1), 0), extent, True), extent * extent)


def border_of(ref, extent):
    count = extent * extent
    east = ref[pl.ds(extent - 1, extent, stride=extent), :]
    west = ref[pl.ds(0, extent, stride=extent), :]
    return jnp.concatenate([ref[0:extent, :], ref[count - extent : count, :], east, west], axis=0)


def without_repeats(border, extent):
    place = iota((border.shape[0], 1), 0)
    return jnp.where(border_index(place, extent, True) < 0, 0.0, border)


def moved(column, by, extent):
    if by == 0:
        return column
    row = iota((extent, 1), 0)
    return jnp.where(row == (extent - 1 if by == 1 else 0), 0.0, pltpu.roll(column, (-by) % extent, 0))


def border_windows(out_ref, wide_ref, q_ref, forward, extent):
    count, channels = wide_ref.shape
    columns = {c: wide_ref[pl.ds(c, extent, stride=extent), :] for c in (0, 1, extent - 2, extent - 1)}
    nothing = jnp.zeros((extent, channels), F32)
    row = iota((extent, 1), 0)
    inside = (row > 0) & (row < extent - 1)
    for a in range(3):
        start = (a if forward else 2 - a) * extent
        lanes = slice(a * 3 * channels, (a + 1) * 3 * channels)
        out_ref[0:extent, lanes] = q_ref[start : start + extent, :]
        out_ref[extent : 2 * extent, lanes] = q_ref[start + count - extent : start + count, :]
        for part, column in ((2, extent - 1), (3, 0)):
            pieces = []
            for b in range(3):
                at = column + (b - 1 if forward else 1 - b)
                pieces.append(moved(columns[at], a - 1 if forward else 1 - a, extent) if at in columns else nothing)
            value = jnp.where(inside, jnp.concatenate(pieces, axis=1), 0.0)
            out_ref[part * extent : (part + 1) * extent, lanes] = value.astype(BF16)


def gelu_parts(u):
    scale = math.sqrt(2.0 / math.pi)
    square = u * u
    half = 0.5 * u
    t = jnp.tanh(u * (scale + (scale * 0.044715) * square))
    value = half + half * t
    slope = (0.5 + 0.5 * t) + (half * (1.0 - t * t)) * (scale + (scale * 3.0 * 0.044715) * square)
    return value, slope


def call(kernel, name, outs, ins, operands, scratch=(), flops=0, limit=LIMIT):
    specs = [pl.BlockSpec(memory_space={"a": pl.ANY, "s": pltpu.SMEM, "v": pltpu.VMEM}[i]) for i in ins]
    moved = sum(math.prod(o.shape) * o.dtype.itemsize for o in list(outs) + list(operands))
    return pl.pallas_call(
        kernel,
        name=name,
        out_shape=outs,
        in_specs=specs,
        out_specs=[pl.BlockSpec(memory_space=pltpu.VMEM) for _ in outs],
        scratch_shapes=list(scratch),
        cost_estimate=pl.CostEstimate(flops=flops, bytes_accessed=moved, transcendentals=0),
        compiler_params=pltpu.CompilerParams(vmem_limit_bytes=limit),
    )(*operands)


def sds(shape, dtype):
    return jax.ShapeDtypeStruct(shape, dtype)


def exchange(payloads, plan, tiles):
    return [
        lax.ppermute(p, "tile", [(i, (i + route[0]) % tiles) for i in range(tiles)]) for p, route in zip(payloads, plan)
    ]


def swap(value, mask, total):
    return lax.ppermute(value, AXES, [(i, i ^ mask) for i in range(total)])


def reduce_gradients(keep, send, total, work, near=None, far=None):
    rows, channels = keep.shape
    quarter = rows // 4
    wire = BF16 if total <= 32 else F32
    me = lax.axis_index(AXES)
    other = swap(send, 1, total)
    plane = (me >> 1) & 3

    def chunk(index):
        first = lax.dynamic_index_in_dim(keep.reshape(4, quarter, channels), index, 0, keepdims=False)
        second = lax.dynamic_index_in_dim(other.reshape(4, quarter, channels), index, 0, keepdims=False)
        return first + second.astype(F32)

    arrived = {}
    for m in (3, 1, 2):
        message = chunk(plane ^ m).astype(wire)
        if m == 2 and near is not None:
            message = jnp.concatenate([message, near], axis=0)
        arrived[m] = swap(message, m << 1, total)
    part = chunk(plane)
    for m in (3, 1, 2):
        part = part + arrived[m][:quarter].astype(F32)
    part, done = work(part)
    extras = None
    if near is not None:
        across = arrived[2][quarter:]
        extent = far.shape[0] // 4
        starts = near_starts(lax.axis_index("tile") ^ 1, extent)
        direct, one, three = [lax.dynamic_slice_in_dim(across, start, 2 * extent, 0) for start in starts]
        riders = {1: (one,), 2: (far, across[-16:]), 3: (three,)}
    bit = 8
    while bit < total:
        mine = part.astype(wire)
        if 2 * bit < total:
            got = {}
            for m in (3, 2, 1):
                message = mine
                if near is not None:
                    message = jnp.concatenate([mine, *riders[m]], axis=0)
                got[m] = swap(message, m * bit, total)
            part = (mine.astype(F32) + got[1][:quarter].astype(F32)) + (got[2][:quarter].astype(F32) + got[3][:quarter].astype(F32))
            if near is not None:
                extras = [direct, got[1][quarter:], got[3][quarter:], got[2][quarter:-16], got[2][-16:]]
            bit *= 4
        else:
            part = mine.astype(F32) + swap(mine, bit, total).astype(F32)
            bit *= 2
    part, done = lax.optimization_barrier((part, done))
    mine = part.astype(wire)
    ring = jnp.stack([mine] + [swap(mine, m << 1, total) for m in (1, 2, 3)])
    whole = jnp.concatenate([lax.dynamic_index_in_dim(ring, plane ^ j, 0) for j in range(4)], axis=0)
    return whole, extras, done


def join_cores(whole, total):
    other = swap(whole, 1, total)
    low = (lax.axis_index(AXES) & 1) == 0
    return jnp.where(low, whole, other), jnp.where(low, other, whole)


def reach_neighbours(across, one, three, far, total):
    across, three, one = swap(across, 4, total), swap(three, 28, total), swap(one, 12, total)
    two = swap(jnp.concatenate([far, across[-16:]], axis=0), 16, total)
    return [across, one, three, two[:-16], two[-16:]]


def per_device(inputs, weight_one, weight_two, cotangent, edge_code, corner_code):
    tiles, members = lax.axis_size("tile"), lax.axis_size("dp")
    extent, channels = inputs.shape[2], inputs.shape[4]
    count = extent * extent
    factor = 1.0 / math.sqrt(inputs.shape[0] * members * tiles * count)
    source = inputs.reshape(count, channels)
    grad_out = cotangent.reshape(count, channels)
    w_one = weight_one.reshape(9 * channels, channels)
    w_two = weight_two.reshape(9 * channels, channels)
    plan = routes(tiles)
    total = tiles * members
    hops = relayed(tiles)
    near_b, far_b, corner_b = sds((4 * extent + 16, channels), BF16), sds((4 * extent, channels), BF16), sds((16, channels), BF16)
    pair_b = sds((2 * extent, channels), BF16)
    if hops:
        first_routed, second_routed = [sds((2 * extent + 16, channels), BF16), pair_b, pair_b, far_b], [near_b, far_b]
        n_routes = 5
    else:
        first_routed = second_routed = [sds((route_rows(r, extent), channels), BF16) for r in plan]
        n_routes = len(plan)
    n_first, n_second = len(first_routed), len(second_routed)

    def write_first(a, b, outs, near_ref):
        if hops:
            write_near(a, b, near_ref, extent)
            write_far(a, b, outs[3], extent)
            for start, out in zip(near_starts(lax.axis_index("tile"), extent), outs):
                out[0 : 2 * extent, :] = near_ref[pl.ds(pl.multiple_of(start, 16), 2 * extent), :]
            outs[0][2 * extent : 2 * extent + 16, :] = near_ref[4 * extent : 4 * extent + 16, :]
        else:
            write_routes(a, b, plan, outs, extent)

    def write_second(a, b, outs):
        if hops:
            write_near(a, b, outs[0], extent)
            write_far(a, b, outs[1], extent)
        else:
            write_routes(a, b, plan, outs, extent)

    def read(refs):
        return read_relay(refs, extent) if hops else read_routes(plan, refs, extent)

    image_b, image_f = sds((count, channels), BF16), sds((count, channels), F32)
    columns_b = sds((count + 2 * extent, 3 * channels), BF16)
    taps_b, taps_f = sds((9 * channels, channels), BF16), sds((9 * channels, channels), F32)
    conv = 2 * count * 9 * channels * channels

    strip_rows = block_starts(extent)[3] + extent
    scatter_b, column_b = sds((count, strip_rows), BF16), sds((count, 4 * extent), BF16)
    pieces = 2

    def first_strips(x_hbm, g_hbm, edge_hbm, corner_hbm, *refs):
        outs = refs[:n_first]
        x_ref, g_ref, near_ref, edge_ref, corner_ref, sems = refs[n_first:]
        pairs = [(edge_hbm, edge_ref), (corner_hbm, corner_ref)]
        step = count // pieces
        for source_ref, target_ref in ((x_hbm, x_ref), (g_hbm, g_ref)):
            for i in range(pieces):
                pairs.append((source_ref.at[pl.ds(i * step, step)], target_ref.at[pl.ds(i * step, step)]))
        copies = [pltpu.make_async_copy(a, b, sems.at[i]) for i, (a, b) in enumerate(pairs)]
        for copy in copies:
            copy.start()
        fixed = block_choice(*fixed_lines(extent), extent)
        for copy in copies[:2]:
            copy.wait()
        seam = block_choice(*seam_lines(edge_ref, corner_ref, extent), extent)
        for copy in copies[2:]:
            copy.wait()
        a = gather_blocks(seam, x_ref[...], extent)
        b = gather_blocks(fixed, g_ref[...], extent)
        write_first(a, b, outs, near_ref)

    first = call(
        first_strips,
        "first_strips",
        first_routed,
        "aaaa",
        (source, grad_out, edge_code.T, corner_code.T),
        scratch=[
            pltpu.VMEM((count, channels), BF16),
            pltpu.VMEM((count, channels), BF16),
            pltpu.VMEM(near_b.shape, BF16),
            pltpu.SMEM((4, tiles), jnp.int32),
            pltpu.SMEM((4, tiles), jnp.int32),
            pltpu.SemaphoreType.DMA((2 + 2 * pieces,)),
        ],
        limit=ALONE,
        flops=10 * conv,
    )
    first_arrived = reach_neighbours(*first, total) if hops else exchange(first, plan, tiles)

    border = 4 * extent
    border_b, border_f = sds((border, channels), BF16), sds((border, channels), F32)
    windows_b = sds((border, 9 * channels), BF16)

    def inner(edge_ref, corner_ref, x_ref, g_ref, w1_ref, w2_ref, *refs):
        hid_ref, dpre_ref, preb_ref, dhb_ref, sum_ref, seam_ref, back_ref, wx_ref, wg_ref = refs[:9]
        qx_ref, qg_ref, qd_ref, pre_ref, dh_ref, wide_ref = refs[9:]
        wide_ref[...] = x_ref[...].astype(F32)
        write_columns(qx_ref, x_ref[...], True, extent)
        border_windows(wx_ref, wide_ref, qx_ref, True, extent)
        window_product(qx_ref, w1_ref[...], True, extent, pre_ref)
        wide_ref[...] = g_ref[...].astype(F32)
        write_columns(qg_ref, g_ref[...], False, extent)
        border_windows(wg_ref, wide_ref, qg_ref, False, extent)
        window_product(qg_ref, w2_ref[...], False, extent, dh_ref)
        preb_ref[...] = border_of(pre_ref, extent)
        dhb_ref[...] = border_of(dh_ref, extent)
        place = iota((count, 1), 0)
        row, column = place // extent, place % extent
        inside = (row > 0) & (row < extent - 1) & (column > 0) & (column < extent - 1)
        value, slope = gelu_parts(pre_ref[...])
        value = jnp.where(inside, value, 0.0)
        hid_ref[...] = value.astype(BF16)
        dpre_ref[...] = jnp.where(inside, dh_ref[...] * slope, 0.0).astype(BF16)
        write_columns(qd_ref, dpre_ref[...], False, extent)
        weight_sum(sum_ref.at[0], jnp.transpose(x_ref[...].astype(F32)).astype(BF16), qd_ref, extent)
        weight_sum(sum_ref.at[1], jnp.transpose(value).astype(BF16), qg_ref, extent)
        lines, pixels = seam_lines(edge_ref, corner_ref, extent)
        across = border_index(iota((1, border), 1), extent, True)
        seam_ref[...] = (block_index(lines, pixels, 0, extent) == across).astype(F32).astype(BF16)
        down = border_index(iota((border, 1), 0), extent, False)
        back_ref[...] = (down == block_index(lines, pixels, 1, extent)).astype(F32).astype(BF16)

    hid_in, dpre_in, pre_b, dh_b, sums, seam_b, back_b, wx_b, wg_b = call(
        inner,
        "inner_products",
        [
            image_b,
            image_b,
            border_f,
            border_f,
            sds((2,) + taps_f.shape, F32),
            sds((strip_rows, border), BF16),
            sds((border, strip_rows), BF16),
            windows_b,
            windows_b,
        ],
        "ssvvvv",
        (edge_code.T, corner_code.T, source, grad_out, w_one, w_two),
        scratch=[pltpu.VMEM(columns_b.shape, BF16)] * 3 + [pltpu.VMEM(image_f.shape, F32)] * 3,
        flops=4 * conv,
    )

    def middle(preb_ref, dhb_ref, sums_ref, seam_ref, back_ref, wx_ref, wg_ref, w1_ref, w2_ref, *refs):
        arrived = refs[:n_routes]
        keep_ref, send_ref, hid_ref, dpre_ref = refs[n_routes : n_routes + 4]
        outs = refs[n_routes + 4 : n_routes + 4 + n_second]
        (sum_ref,) = refs[n_routes + 4 + n_second :]
        x_strips, g_strips = read(arrived)
        columns = strip_columns(g_strips, extent)
        adds = margin_adds(x_strips, w1_ref[...], extent)
        row = iota((extent, 1), 0)
        first, final = row == 0, row == extent - 1

        def ends(low, high):
            return jnp.where(first, low, 0.0) + jnp.where(final, high, 0.0)

        def end_rows(part):
            return adds[part][0:1], adds[part][extent - 1 : extent]

        (east_low, east_high), (west_low, west_high) = end_rows(2), end_rows(3)
        north = preb_ref[0:extent, :] + adds[0] + ends(west_low, east_low)
        south = preb_ref[extent : 2 * extent, :] + adds[1] + ends(west_high, east_high)

        def side(part, at):
            value = preb_ref[part * extent : (part + 1) * extent, :] + adds[part]
            return jnp.where(first, north[at : at + 1], jnp.where(final, south[at : at + 1], value))

        value, slope = gelu_parts(jnp.concatenate([north, south, side(2, extent - 1), side(3, 0)], axis=0))
        dadds = [dot_nt(columns[i], tap_columns(w2_ref[...], block_taps(i), channels)) for i in range(4)]
        high, low = halves(jnp.concatenate(dadds, axis=0))
        d_hidden = dhb_ref[...] + dot(back_ref[...], high) + dot(back_ref[...], low)
        d_pre = d_hidden * slope
        hidden = without_repeats(value, extent).astype(BF16)
        hid_ref[...] = hidden
        d_once = without_repeats(d_pre, extent).astype(BF16)
        dpre_ref[...] = d_once
        strips = dot(seam_ref[...], hidden).astype(BF16)
        a = [strips[start : start + rows] for start, rows in zip(block_starts(extent), block_rows(extent))]
        b = []
        tall = iota((16, 1), 0)
        for part in range(4):
            block = d_pre[part * extent : (part + 1) * extent]
            if part < 2:
                tile = jnp.where(tall == 0, block[0:1], jnp.where(tall == 1, block[extent - 1 : extent], 0.0))
                block = jnp.concatenate([block, tile], axis=0)
            b.append(block.astype(BF16))
        write_second(a, b, outs)
        own = dot_t(wx_ref[...], d_once)
        margin = margin_weight(x_strips, strip_columns(b, extent))
        for tap in range(9):
            span = slice(tap * channels, (tap + 1) * channels)
            total = sums_ref[0, span, :] + own[span]
            sum_ref[0, span, :] = total if margin[tap] is None else total + margin[tap]
        own = dot_t(hidden, wg_ref[...])
        margin = margin_weight(a, columns)
        for tap in range(9):
            span = slice(tap * channels, (tap + 1) * channels)
            total = sums_ref[1, span, :] + own[:, span]
            sum_ref[1, span, :] = total if margin[tap] is None else total + margin[tap]
        core = lax.axis_index("dp") % 2
        keep_ref[...] = sum_ref[core]
        send_ref[...] = sum_ref[1 - core].astype(BF16)

    results = call(
        middle,
        "gradients",
        [taps_f, taps_b, border_b, border_b] + second_routed,
        "v" * (9 + n_routes),
        (pre_b, dh_b, sums, seam_b, back_b, wx_b, wg_b, w_one, w_two, *first_arrived),
        scratch=[pltpu.VMEM((2,) + taps_f.shape, F32)],
        flops=conv // 4,
    )
    keep, send, hid_edge, dpre_edge = results[:4]

    def later(edge_ref, corner_ref, x_ref, g_ref, hid_ref, dpre_ref, hidb_ref, dpreb_ref, w1_ref, w2_ref, out_ref, dx_ref, scatter_ref, column_ref, q_ref):
        lines, pixels = seam_lines(edge_ref, corner_ref, extent)
        scatter_ref[...] = seam_scatter(lines, pixels, extent)
        column_ref[...] = column_scatter(extent)
        choice = border_choice(extent)
        hidden = hid_ref[...].astype(F32) + dot_t(choice, hidb_ref[...])
        d_pre = dpre_ref[...].astype(F32) + dot_t(choice, dpreb_ref[...])
        write_columns(q_ref, hidden, True, extent)
        window_product(q_ref, w2_ref[...], True, extent, out_ref)
        out_ref[...] = out_ref[...] + x_ref[...].astype(F32)
        write_columns(q_ref, d_pre, False, extent)
        window_product(q_ref, w1_ref[...], False, extent, dx_ref)
        dx_ref[...] = dx_ref[...] + g_ref[...].astype(F32)

    def later_parts(token):
        token, inner_arrays = lax.optimization_barrier((token, (hid_in, dpre_in, hid_edge, dpre_edge)))
        return token, call(
            later,
            "later_products",
            [image_f, image_f, scatter_b, column_b],
            "ss" + "v" * 8,
            (edge_code.T, corner_code.T, source, grad_out, *inner_arrays, w_one, w_two),
            scratch=[pltpu.VMEM(columns_b.shape, BF16)],
            flops=2 * conv,
        )

    if hops:
        whole, second_arrived, parts = reduce_gradients(keep, send, total, later_parts, *results[4:])
    else:
        second_arrived = exchange(results[4:], plan, tiles)
        whole, _, parts = reduce_gradients(keep, send, total, later_parts)

    def last(part_ref, dpart_ref, scatter_ref, column_ref, w1_ref, w2_ref, *refs):
        arrived = refs[:n_routes]
        out_ref, dx_ref = refs[n_routes:]
        h_strips, d_strips = read(arrived)
        out_ref[...] = (part_ref[...] + margin_forward(h_strips, w2_ref[...], column_ref[...], extent)).astype(BF16)
        add = margin_backward(strip_columns(d_strips, extent), w1_ref[...], scatter_ref[...], extent)
        dx_ref[...] = (dpart_ref[...] + add).astype(BF16)

    output, d_input = call(
        last,
        "outputs",
        [image_b, image_b],
        "v" * (6 + n_routes),
        (*parts, w_one, w_two, *second_arrived),
        flops=conv // 4,
    )
    whole, output, d_input = lax.optimization_barrier((whole, output, d_input))
    one, two = join_cores(whole, total)
    shape = (9, channels, channels)
    return (
        output.reshape(inputs.shape),
        d_input.reshape(inputs.shape),
        (one.astype(F32) * factor).reshape(shape),
        (two.astype(F32) * factor).reshape(shape),
    )


def solution(mesh):
    split = P("dp", "tile", None, None, None)
    return jax.shard_map(
        per_device,
        mesh=mesh,
        in_specs=(split, P(), P(), split, P(), P()),
        out_specs=(split, split, P(), P()),
        check_vma=False,
    )
```

```python
import math

import jax
import jax.numpy as jnp
from jax import lax
from jax.experimental import pallas as pl
from jax.experimental.pallas import tpu as pltpu
from jax.sharding import PartitionSpec as P

RW = 4
SIDES = (-RW, 1, RW, -1)
CORNERS = (-RW - 1, -RW + 1, RW + 1, RW - 1)
F32 = jnp.float32
BF16 = jnp.bfloat16
AXES = ("tile", "dp")
LIMIT = 20 * 1024 * 1024
ALONE = 60 * 1024 * 1024

BLOCKS = ((0, (0, 1)), (2, (3, 2)), (1, ()), (3, ()))


def block_rows(extent):
    return (extent + 16, extent + 16, extent, extent)


def block_starts(extent):
    rows = block_rows(extent)
    return (0, rows[0], rows[0] + rows[1], rows[0] + rows[1] + rows[2])


def block_taps(position):
    return ((0, 1, 2), (6, 7, 8), (2, 5, 8), (0, 3, 6))[position]


def routes(tiles):
    found = {}
    for kind, offsets in (("a", SIDES), ("b", SIDES), ("ac", CORNERS), ("bc", CORNERS)):
        for which, offset in enumerate(offsets):
            distance = (-offset if kind[0] == "a" else offset) % tiles
            found.setdefault(distance, []).append((kind, which))
    plan = []
    for distance, parts in found.items():
        sides = [p for p in parts if len(p[0]) == 1]
        corners = [p for p in parts if len(p[0]) == 2]
        plan.append((distance, sides, corners))
    return plan


def route_rows(route, extent):
    return extent * len(route[1]) + (16 if route[2] else 0)


def iota(shape, axis):
    return lax.broadcasted_iota(jnp.int32, shape, axis)


def dot(a, b):
    return lax.dot_general(a, b, (((1,), (0,)), ((), ())), preferred_element_type=F32)


def dot_nt(a, b):
    return lax.dot_general(a, b, (((1,), (1,)), ((), ())), preferred_element_type=F32)


def dot_t(a, b):
    return lax.dot_general(a, b, (((0,), (0,)), ((), ())), preferred_element_type=F32)


def corner_pixel(code, extent):
    last = extent - 1
    return jnp.where(code == 0, 0, jnp.where(code == 1, last, jnp.where(code == 2, extent * extent - 1, extent * last)))


def side_line(code, extent):
    last = extent - 1
    border = code % 4
    base = jnp.where(border == 1, last, jnp.where(border == 2, extent * last, 0))
    step = jnp.where(border % 2 == 0, 1, extent)
    return jnp.where(code >= 4, base + last * step, base), jnp.where(code >= 4, -step, step)


def seam_lines(edge_ref, corner_ref, extent):
    tiles = edge_ref.shape[1]
    mine = lax.axis_index("tile")
    lines = [side_line(edge_ref[k, (mine - o + tiles + RW * tiles) % tiles], extent) for k, o in enumerate(SIDES)]
    pixels = [corner_pixel(corner_ref[q, (mine - o + tiles + RW * tiles) % tiles], extent) for q, o in enumerate(CORNERS)]
    return lines, pixels


def fixed_lines(extent):
    last = extent - 1
    lines = [(0, 1), (last, extent), (extent * last, 1), (0, extent)]
    return lines, [0, last, extent * extent - 1, extent * last]


def pick_rows(indices, count):
    return (iota((indices.shape[0], count), 1) == indices).astype(F32).astype(BF16)


def line_rows(line, extent, count):
    return pick_rows(line[0] + line[1] * iota((extent, 1), 0), count)


def spot_rows(spots, count):
    rows = iota((16, 1), 0)
    index = jnp.full((16, 1), -1, jnp.int32)
    for row, pixel in spots:
        index = jnp.where(rows == row, pixel, index)
    return pick_rows(index, count)


def block_choice(lines, pixels, extent):
    count = extent * extent
    rows = []
    for side, corners in BLOCKS:
        rows.append(line_rows(lines[side], extent, count))
        if corners:
            rows.append(spot_rows([(i, pixels[q]) for i, q in enumerate(corners)], count))
    return jnp.concatenate(rows, axis=0)


def block_index(lines, pixels, axis, extent):
    starts = block_starts(extent)
    total = starts[3] + extent
    place = iota((total, 1) if axis == 0 else (1, total), axis)
    index = jnp.full(place.shape, -1, jnp.int32)
    for start, (side, ends) in zip(starts, BLOCKS):
        base, step = lines[side]
        index = jnp.where((place >= start) & (place < start + extent), base + step * (place - start), index)
        for i, q in enumerate(ends):
            index = jnp.where(place == start + extent + i, pixels[q], index)
    return index


def seam_scatter(lines, pixels, extent):
    return (iota((extent * extent, 1), 0) == block_index(lines, pixels, 1, extent)).astype(F32).astype(BF16)


def column_scatter(extent):
    lane = iota((1, 4 * extent), 1)
    target = (lane % extent) * extent + jnp.where(lane < 2 * extent, extent - 1, 0)
    return (iota((extent * extent, 1), 0) == target).astype(F32).astype(BF16)


def gather_blocks(choice, image, extent):
    strips = dot(choice, image).astype(BF16)
    starts = block_starts(extent)
    return [strips[start : start + rows] for start, rows in zip(starts, block_rows(extent))]


def write_routes(a_blocks, b_blocks, plan, out_refs, extent):
    side_at = {side: i for i, (side, _) in enumerate(BLOCKS)}
    corner_at = {q: (i, extent + j) for i, (_, corners) in enumerate(BLOCKS) for j, q in enumerate(corners)}
    for route, out in zip(plan, out_refs):
        at = 0
        for kind, side in route[1]:
            blocks = a_blocks if kind == "a" else b_blocks
            out[at : at + extent, :] = blocks[side_at[side]][:extent]
            at += extent
        if route[2]:
            rows = iota((16, 1), 0)
            tile = jnp.zeros((16, out.shape[1]), F32)
            for i, (kind, q) in enumerate(route[2]):
                block, row = corner_at[q]
                source = (a_blocks if kind == "ac" else b_blocks)[block][extent : extent + 16].astype(F32)
                tile = jnp.where(rows == i, source[row - extent : row - extent + 1], tile)
            out[at : at + 16, :] = tile.astype(BF16)


def read_routes(plan, in_refs, extent):
    sides, corners = {}, {}
    for route, ref in zip(plan, in_refs):
        at = 0
        for key in route[1]:
            sides[key] = ref[at : at + extent, :]
            at += extent
        if route[2]:
            tile = ref[at : at + 16, :].astype(F32)
            for i, key in enumerate(route[2]):
                corners[key] = tile[i : i + 1]
    result = []
    rows = iota((16, 1), 0)
    for kind in ("a", "b"):
        blocks = []
        for side, ends in BLOCKS:
            block = sides[(kind, side)]
            if ends:
                tile = jnp.zeros((16, block.shape[1]), F32)
                for i, q in enumerate(ends):
                    tile = jnp.where(rows == i, corners[(kind + "c", q)], tile)
                block = jnp.concatenate([block, tile.astype(BF16)], axis=0)
            blocks.append(block)
        result.append(blocks)
    return result


def relayed(tiles):
    return tiles == 8


def write_near(a_blocks, b_blocks, near_ref, extent):
    for i, block in enumerate((a_blocks[3], b_blocks[2], a_blocks[2], b_blocks[3])):
        near_ref[i * extent : (i + 1) * extent, :] = block
    rows = iota((16, 1), 0)
    tile = jnp.zeros((16, near_ref.shape[1]), F32)
    at = 0
    for blocks in (a_blocks, b_blocks):
        ends = [blocks[i][extent : extent + 16].astype(F32) for i in range(2)]
        for block, row in ((0, 0), (0, 1), (1, 1), (1, 0)):
            tile = jnp.where(rows == at, ends[block][row : row + 1], tile)
            at += 1
    near_ref[4 * extent : 4 * extent + 16, :] = tile.astype(BF16)


def write_far(a_blocks, b_blocks, far_ref, extent):
    for i, block in enumerate((a_blocks[0], a_blocks[1], b_blocks[0], b_blocks[1])):
        far_ref[i * extent : (i + 1) * extent, :] = block[:extent]


def near_starts(tile, extent):
    right = tile % 2
    odd = (tile // 2) % 2
    corners = 2 * extent + 16
    side = jnp.where(right == 1, 0, 2 * extent)
    one = jnp.where(right == odd, corners, side)
    three = jnp.where(right == odd, side, corners)
    return side_of_partner(right, extent), one, three


def side_of_partner(right, extent):
    return jnp.where(right == 1, 2 * extent, 0)


def read_relay(refs, extent):
    across, one, three, far, opposite = refs
    mine = lax.axis_index("tile")
    left = mine % 2 == 0
    odd = (mine // 2 + mine) % 2 == 1

    def rows_of(ref, start, count):
        return ref[start : start + count, :].astype(F32)

    def choose(start, count):
        return jnp.where(odd, rows_of(one, start, count), rows_of(three, start, count))

    pair = [(rows_of(across, i * extent, extent), choose(i * extent, extent)) for i in range(2)]
    a_east, b_west = [jnp.where(left, here, there).astype(BF16) for here, there in pair]
    a_west, b_east = [jnp.where(left, there, here).astype(BF16) for here, there in pair]
    tail = 2 * extent - 16
    beside = jnp.where(odd, rows_of(three, tail, 16), rows_of(one, tail, 16))
    beyond = opposite[0:16, :].astype(F32)
    third = jnp.where(left, beside, beyond)
    fifth = jnp.where(left, beyond, beside)
    corners = {("a", 0): third[0:1], ("a", 3): third[3:4], ("b", 1): third[5:6], ("b", 2): third[6:7]}
    corners.update({("a", 1): fifth[1:2], ("a", 2): fifth[2:3], ("b", 0): fifth[4:5], ("b", 3): fifth[7:8]})
    rows = iota((16, 1), 0)
    result = []
    for kind, first, east, west in (("a", 0, a_east, a_west), ("b", 2, b_east, b_west)):
        blocks = []
        for i, ends in enumerate(((0, 1), (3, 2))):
            tile = jnp.where(rows == 0, corners[(kind, ends[0])], jnp.where(rows == 1, corners[(kind, ends[1])], 0.0))
            strip = far[(first + i) * extent : (first + i + 1) * extent, :]
            blocks.append(jnp.concatenate([strip, tile.astype(BF16)], axis=0))
        result.append(blocks + [east, west])
    return result


def shifted(image, by, extent):
    if by == 0:
        return image
    column = iota((image.shape[0], 1), 0) % extent
    rolled = pltpu.roll(image, (-by) % image.shape[0], 0)
    return jnp.where(column == (extent - 1 if by == 1 else 0), 0.0, rolled)


def write_columns(q_ref, image, forward, extent):
    count, channels = image.shape
    zero = jnp.zeros((extent, q_ref.shape[1]), BF16)
    q_ref[0:extent, :] = zero
    q_ref[extent + count : 2 * extent + count, :] = zero
    wide = image.astype(F32)
    for b in range(3):
        by = b - 1 if forward else 1 - b
        q_ref[extent : extent + count, b * channels : (b + 1) * channels] = shifted(wide, by, extent).astype(BF16)


def window_product(q_ref, weight, forward, extent, out_ref, chunk=8):
    channels = weight.shape[1]
    if forward:
        taps = tap_weight(weight, range(9), channels)
        nothing = jnp.zeros((3 * channels, channels), weight.dtype)
        both = jnp.concatenate([jnp.concatenate([taps, nothing], axis=0), jnp.concatenate([nothing, taps], axis=0)], axis=1)
    else:
        taps = tap_columns(weight, (6, 7, 8, 3, 4, 5, 0, 1, 2), channels)
        nothing = jnp.zeros((channels, 3 * channels), weight.dtype)
        both = jnp.concatenate([jnp.concatenate([taps, nothing], axis=1), jnp.concatenate([nothing, taps], axis=1)], axis=0)
    for start in range(0, extent // 2, chunk):
        rows = []
        for a in range(4):
            rows.append(jnp.concatenate([q_ref[(2 * i + a) * extent : (2 * i + a + 1) * extent, :] for i in range(start, start + chunk)], axis=0))
        product = (dot if forward else dot_nt)(jnp.concatenate(rows, axis=1), both)
        for i in range(chunk):
            for half in range(2):
                at = (2 * (start + i) + half) * extent
                out_ref[at : at + extent, :] = product[i * extent : (i + 1) * extent, half * channels : (half + 1) * channels]


def tap_weight(weight, taps, channels):
    return jnp.concatenate([weight[t * channels : (t + 1) * channels, :] for t in taps], axis=0)


def tap_columns(weight, taps, channels):
    return jnp.concatenate([weight[t * channels : (t + 1) * channels, :] for t in taps], axis=1)


def halves(values):
    high = values.astype(BF16)
    return high, (values - high.astype(F32)).astype(BF16)


def margin_adds(strips, weight, extent):
    channels = strips[0].shape[1]
    adds = []
    for position, (side, ends) in enumerate(BLOCKS):
        middle = strips[position][:extent].astype(F32)
        row = iota((extent, 1), 0)
        before, after = 0.0, 0.0
        if ends:
            tile = strips[position][extent : extent + 16].astype(F32)
            before, after = tile[0:1], tile[1:2]
        left = jnp.where(row == 0, before, pltpu.roll(middle, 1, 0))
        right = jnp.where(row == extent - 1, after, pltpu.roll(middle, extent - 1, 0))
        window = jnp.concatenate([left, middle, right], axis=1).astype(BF16)
        adds.append(dot(window, tap_weight(weight, block_taps(position), channels)))
    return adds


def margin_forward(strips, weight, columns, extent):
    count = extent * extent
    adds = margin_adds(strips, weight, extent)
    spread = jnp.concatenate(list(halves(adds[2])) + list(halves(adds[3])), axis=0)
    image = dot(columns, spread)
    top = image[:extent] + adds[0]
    bottom = image[count - extent :] + adds[1]
    return jnp.concatenate([top, image[extent : count - extent], bottom], axis=0)


def strip_columns(strips, extent):
    result = []
    for position, (side, ends) in enumerate(BLOCKS):
        middle = strips[position][:extent].astype(F32)
        row = iota((extent, 1), 0)
        after = jnp.where(row == extent - 1, 0.0, pltpu.roll(middle, extent - 1, 0))
        before = jnp.where(row == 0, 0.0, pltpu.roll(middle, 1, 0))
        columns = jnp.concatenate([after, middle, before], axis=1)
        if ends:
            tile = strips[position][extent : extent + 16].astype(F32)
            row = iota((16, 1), 0)
            low = jnp.where(row == 0, tile, 0.0)
            high = jnp.where(row == 1, tile, 0.0)
            columns = jnp.concatenate([columns, jnp.concatenate([low, jnp.zeros_like(tile), high], axis=1)], axis=0)
        result.append(columns.astype(BF16))
    return result


def margin_backward(columns, weight, scatter, extent):
    channels = weight.shape[1]
    adds = [dot_nt(columns[i], tap_columns(weight, block_taps(i), channels)) for i in range(4)]
    high, low = halves(jnp.concatenate(adds, axis=0))
    return dot(scatter, high) + dot(scatter, low)


def weight_sum(out_ref, image_t, q_ref, extent):
    channels = image_t.shape[0]
    count = image_t.shape[1]
    rows = jnp.concatenate([q_ref[(2 - a) * extent : (2 - a) * extent + count, :] for a in range(3)], axis=1)
    product = dot(image_t, rows)
    for tap in range(9):
        out_ref[tap * channels : (tap + 1) * channels, :] = product[:, tap * channels : (tap + 1) * channels]


def margin_weight(strips, columns):
    channels = strips[0].shape[1]
    wide = [dot_t(strips[i], columns[i]) for i in range(4)]
    result = []
    for tap in range(9):
        value = None
        for position in range(4):
            taps = block_taps(position)
            if tap in taps:
                at = taps.index(tap)
                part = wide[position][:, at * channels : (at + 1) * channels]
                value = part if value is None else value + part
        result.append(value)
    return result


def border_index(place, extent, unique):
    last = extent - 1
    part, j = place // extent, place % extent
    index = jnp.where(part == 0, j, jnp.where(part == 1, extent * last + j, jnp.where(part == 2, extent * j + last, extent * j)))
    if unique:
        index = jnp.where((part >= 2) & ((j == 0) | (j == last)), -2, index)
    return index


def border_choice(extent):
    return pick_rows(border_index(iota((4 * extent, 1), 0), extent, True), extent * extent)


def border_of(ref, extent):
    count = extent * extent
    east = ref[pl.ds(extent - 1, extent, stride=extent), :]
    west = ref[pl.ds(0, extent, stride=extent), :]
    return jnp.concatenate([ref[0:extent, :], ref[count - extent : count, :], east, west], axis=0)


def without_repeats(border, extent):
    place = iota((border.shape[0], 1), 0)
    return jnp.where(border_index(place, extent, True) < 0, 0.0, border)


def moved(column, by, extent):
    if by == 0:
        return column
    row = iota((extent, 1), 0)
    return jnp.where(row == (extent - 1 if by == 1 else 0), 0.0, pltpu.roll(column, (-by) % extent, 0))


def border_windows(out_ref, wide_ref, q_ref, forward, extent):
    count, channels = wide_ref.shape
    columns = {c: wide_ref[pl.ds(c, extent, stride=extent), :] for c in (0, 1, extent - 2, extent - 1)}
    nothing = jnp.zeros((extent, channels), F32)
    row = iota((extent, 1), 0)
    inside = (row > 0) & (row < extent - 1)
    for a in range(3):
        start = (a if forward else 2 - a) * extent
        lanes = slice(a * 3 * channels, (a + 1) * 3 * channels)
        out_ref[0:extent, lanes] = q_ref[start : start + extent, :]
        out_ref[extent : 2 * extent, lanes] = q_ref[start + count - extent : start + count, :]
        for part, column in ((2, extent - 1), (3, 0)):
            pieces = []
            for b in range(3):
                at = column + (b - 1 if forward else 1 - b)
                pieces.append(moved(columns[at], a - 1 if forward else 1 - a, extent) if at in columns else nothing)
            value = jnp.where(inside, jnp.concatenate(pieces, axis=1), 0.0)
            out_ref[part * extent : (part + 1) * extent, lanes] = value.astype(BF16)


def gelu_parts(u):
    scale = math.sqrt(2.0 / math.pi)
    square = u * u
    half = 0.5 * u
    t = jnp.tanh(u * (scale + (scale * 0.044715) * square))
    value = half + half * t
    slope = (0.5 + 0.5 * t) + (half * (1.0 - t * t)) * (scale + (scale * 3.0 * 0.044715) * square)
    return value, slope


def call(kernel, name, outs, ins, operands, scratch=(), flops=0, limit=LIMIT):
    specs = [pl.BlockSpec(memory_space={"a": pl.ANY, "s": pltpu.SMEM, "v": pltpu.VMEM}[i]) for i in ins]
    moved = sum(math.prod(o.shape) * o.dtype.itemsize for o in list(outs) + list(operands))
    return pl.pallas_call(
        kernel,
        name=name,
        out_shape=outs,
        in_specs=specs,
        out_specs=[pl.BlockSpec(memory_space=pltpu.VMEM) for _ in outs],
        scratch_shapes=list(scratch),
        cost_estimate=pl.CostEstimate(flops=flops, bytes_accessed=moved, transcendentals=0),
        compiler_params=pltpu.CompilerParams(vmem_limit_bytes=limit),
    )(*operands)


def sds(shape, dtype):
    return jax.ShapeDtypeStruct(shape, dtype)


def exchange(payloads, plan, tiles):
    return [
        lax.ppermute(p, "tile", [(i, (i + route[0]) % tiles) for i in range(tiles)]) for p, route in zip(payloads, plan)
    ]


def swap(value, mask, total):
    return lax.ppermute(value, AXES, [(i, i ^ mask) for i in range(total)])


def reduce_gradients(keep, send, total, work, near=None, far=None):
    rows, channels = keep.shape
    quarter = rows // 4
    wire = BF16 if total <= 32 else F32
    me = lax.axis_index(AXES)
    other = swap(send, 1, total)
    plane = (me >> 1) & 3

    def chunk(index):
        first = lax.dynamic_index_in_dim(keep.reshape(4, quarter, channels), index, 0, keepdims=False)
        second = lax.dynamic_index_in_dim(other.reshape(4, quarter, channels), index, 0, keepdims=False)
        return first + second.astype(F32)

    arrived = {}
    for m in (3, 1, 2):
        message = chunk(plane ^ m).astype(wire)
        if m == 2 and near is not None:
            message = jnp.concatenate([message, near], axis=0)
        arrived[m] = swap(message, m << 1, total)
    part = chunk(plane)
    for m in (3, 1, 2):
        part = part + arrived[m][:quarter].astype(F32)
    part, done = work(part)
    extras = None
    if near is not None:
        across = arrived[2][quarter:]
        extent = far.shape[0] // 4
        starts = near_starts(lax.axis_index("tile") ^ 1, extent)
        direct, one, three = [lax.dynamic_slice_in_dim(across, start, 2 * extent, 0) for start in starts]
        riders = {1: (one,), 2: (far, across[-16:]), 3: (three,)}
    bit = 8
    while bit < total:
        mine = part.astype(wire)
        if 2 * bit < total:
            got = {}
            for m in (3, 2, 1):
                message = mine
                if near is not None:
                    message = jnp.concatenate([mine, *riders[m]], axis=0)
                got[m] = swap(message, m * bit, total)
            part = (mine.astype(F32) + got[1][:quarter].astype(F32)) + (got[2][:quarter].astype(F32) + got[3][:quarter].astype(F32))
            if near is not None:
                extras = [direct, got[1][quarter:], got[3][quarter:], got[2][quarter:-16], got[2][-16:]]
            bit *= 4
        else:
            part = mine.astype(F32) + swap(mine, bit, total).astype(F32)
            bit *= 2
    part, done = lax.optimization_barrier((part, done))
    mine = part.astype(wire)
    ring = jnp.stack([mine] + [swap(mine, m << 1, total) for m in (1, 2, 3)])
    whole = jnp.concatenate([lax.dynamic_index_in_dim(ring, plane ^ j, 0) for j in range(4)], axis=0)
    return whole, extras, done


def join_cores(whole, total):
    other = swap(whole, 1, total)
    low = (lax.axis_index(AXES) & 1) == 0
    return jnp.where(low, whole, other), jnp.where(low, other, whole)


def reach_neighbours(across, one, three, far, total):
    two, three, one = swap(far, 16, total), swap(three, 28, total), swap(one, 12, total)
    across = swap(jnp.concatenate([across, two[-16:]], axis=0), 4, total)
    return [across, one, three, two[:-16], across[-16:]]


def per_device(inputs, weight_one, weight_two, cotangent, edge_code, corner_code):
    tiles, members = lax.axis_size("tile"), lax.axis_size("dp")
    extent, channels = inputs.shape[2], inputs.shape[4]
    count = extent * extent
    factor = 1.0 / math.sqrt(inputs.shape[0] * members * tiles * count)
    source = inputs.reshape(count, channels)
    grad_out = cotangent.reshape(count, channels)
    w_one = weight_one.reshape(9 * channels, channels)
    w_two = weight_two.reshape(9 * channels, channels)
    plan = routes(tiles)
    total = tiles * members
    hops = relayed(tiles)
    near_b, far_b, corner_b = sds((4 * extent + 16, channels), BF16), sds((4 * extent, channels), BF16), sds((16, channels), BF16)
    pair_b = sds((2 * extent, channels), BF16)
    if hops:
        first_routed, second_routed = [pair_b, pair_b, pair_b, sds((4 * extent + 16, channels), BF16)], [near_b, far_b]
        n_routes = 5
    else:
        first_routed = second_routed = [sds((route_rows(r, extent), channels), BF16) for r in plan]
        n_routes = len(plan)
    n_first, n_second = len(first_routed), len(second_routed)

    def write_first(a, b, outs, near_ref):
        if hops:
            write_near(a, b, near_ref, extent)
            write_far(a, b, outs[3], extent)
            for start, out in zip(near_starts(lax.axis_index("tile"), extent), outs):
                out[...] = near_ref[pl.ds(pl.multiple_of(start, 16), 2 * extent), :]
            outs[3][4 * extent : 4 * extent + 16, :] = near_ref[4 * extent : 4 * extent + 16, :]
        else:
            write_routes(a, b, plan, outs, extent)

    def write_second(a, b, outs):
        if hops:
            write_near(a, b, outs[0], extent)
            write_far(a, b, outs[1], extent)
        else:
            write_routes(a, b, plan, outs, extent)

    def read(refs):
        return read_relay(refs, extent) if hops else read_routes(plan, refs, extent)

    image_b, image_f = sds((count, channels), BF16), sds((count, channels), F32)
    columns_b = sds((count + 2 * extent, 3 * channels), BF16)
    taps_b, taps_f = sds((9 * channels, channels), BF16), sds((9 * channels, channels), F32)
    conv = 2 * count * 9 * channels * channels

    strip_rows = block_starts(extent)[3] + extent
    scatter_b, column_b = sds((count, strip_rows), BF16), sds((count, 4 * extent), BF16)
    pieces = 2

    def first_strips(x_hbm, g_hbm, edge_hbm, corner_hbm, *refs):
        outs = refs[:n_first]
        x_ref, g_ref, near_ref, edge_ref, corner_ref, sems = refs[n_first:]
        pairs = [(edge_hbm, edge_ref), (corner_hbm, corner_ref)]
        step = count // pieces
        for source_ref, target_ref in ((x_hbm, x_ref), (g_hbm, g_ref)):
            for i in range(pieces):
                pairs.append((source_ref.at[pl.ds(i * step, step)], target_ref.at[pl.ds(i * step, step)]))
        copies = [pltpu.make_async_copy(a, b, sems.at[i]) for i, (a, b) in enumerate(pairs)]
        for copy in copies:
            copy.start()
        fixed = block_choice(*fixed_lines(extent), extent)
        for copy in copies[:2]:
            copy.wait()
        seam = block_choice(*seam_lines(edge_ref, corner_ref, extent), extent)
        for copy in copies[2:]:
            copy.wait()
        a = gather_blocks(seam, x_ref[...], extent)
        b = gather_blocks(fixed, g_ref[...], extent)
        write_first(a, b, outs, near_ref)

    first = call(
        first_strips,
        "first_strips",
        first_routed,
        "aaaa",
        (source, grad_out, edge_code.T, corner_code.T),
        scratch=[
            pltpu.VMEM((count, channels), BF16),
            pltpu.VMEM((count, channels), BF16),
            pltpu.VMEM(near_b.shape, BF16),
            pltpu.SMEM((4, tiles), jnp.int32),
            pltpu.SMEM((4, tiles), jnp.int32),
            pltpu.SemaphoreType.DMA((2 + 2 * pieces,)),
        ],
        limit=ALONE,
        flops=10 * conv,
    )
    first_arrived = reach_neighbours(*first, total) if hops else exchange(first, plan, tiles)

    border = 4 * extent
    border_b, border_f = sds((border, channels), BF16), sds((border, channels), F32)
    windows_b = sds((border, 9 * channels), BF16)

    def inner(edge_ref, corner_ref, x_ref, g_ref, w1_ref, w2_ref, *refs):
        hid_ref, dpre_ref, preb_ref, dhb_ref, sum_ref, seam_ref, back_ref, wx_ref, wg_ref = refs[:9]
        qx_ref, qg_ref, qd_ref, pre_ref, dh_ref, wide_ref = refs[9:]
        wide_ref[...] = x_ref[...].astype(F32)
        write_columns(qx_ref, x_ref[...], True, extent)
        border_windows(wx_ref, wide_ref, qx_ref, True, extent)
        window_product(qx_ref, w1_ref[...], True, extent, pre_ref)
        wide_ref[...] = g_ref[...].astype(F32)
        write_columns(qg_ref, g_ref[...], False, extent)
        border_windows(wg_ref, wide_ref, qg_ref, False, extent)
        window_product(qg_ref, w2_ref[...], False, extent, dh_ref)
        preb_ref[...] = border_of(pre_ref, extent)
        dhb_ref[...] = border_of(dh_ref, extent)
        place = iota((count, 1), 0)
        row, column = place // extent, place % extent
        inside = (row > 0) & (row < extent - 1) & (column > 0) & (column < extent - 1)
        value, slope = gelu_parts(pre_ref[...])
        value = jnp.where(inside, value, 0.0)
        hid_ref[...] = value.astype(BF16)
        dpre_ref[...] = jnp.where(inside, dh_ref[...] * slope, 0.0).astype(BF16)
        write_columns(qd_ref, dpre_ref[...], False, extent)
        weight_sum(sum_ref.at[0], jnp.transpose(x_ref[...].astype(F32)).astype(BF16), qd_ref, extent)
        weight_sum(sum_ref.at[1], jnp.transpose(value).astype(BF16), qg_ref, extent)
        lines, pixels = seam_lines(edge_ref, corner_ref, extent)
        across = border_index(iota((1, border), 1), extent, True)
        seam_ref[...] = (block_index(lines, pixels, 0, extent) == across).astype(F32).astype(BF16)
        down = border_index(iota((border, 1), 0), extent, False)
        back_ref[...] = (down == block_index(lines, pixels, 1, extent)).astype(F32).astype(BF16)

    hid_in, dpre_in, pre_b, dh_b, sums, seam_b, back_b, wx_b, wg_b = call(
        inner,
        "inner_products",
        [
            image_b,
            image_b,
            border_f,
            border_f,
            sds((2,) + taps_f.shape, F32),
            sds((strip_rows, border), BF16),
            sds((border, strip_rows), BF16),
            windows_b,
            windows_b,
        ],
        "ssvvvv",
        (edge_code.T, corner_code.T, source, grad_out, w_one, w_two),
        scratch=[pltpu.VMEM(columns_b.shape, BF16)] * 3 + [pltpu.VMEM(image_f.shape, F32)] * 3,
        flops=4 * conv,
    )

    def middle(preb_ref, dhb_ref, sums_ref, seam_ref, back_ref, wx_ref, wg_ref, w1_ref, w2_ref, *refs):
        arrived = refs[:n_routes]
        keep_ref, send_ref, hid_ref, dpre_ref = refs[n_routes : n_routes + 4]
        outs = refs[n_routes + 4 : n_routes + 4 + n_second]
        (sum_ref,) = refs[n_routes + 4 + n_second :]
        x_strips, g_strips = read(arrived)
        columns = strip_columns(g_strips, extent)
        adds = margin_adds(x_strips, w1_ref[...], extent)
        row = iota((extent, 1), 0)
        first, final = row == 0, row == extent - 1

        def ends(low, high):
            return jnp.where(first, low, 0.0) + jnp.where(final, high, 0.0)

        def end_rows(part):
            return adds[part][0:1], adds[part][extent - 1 : extent]

        (east_low, east_high), (west_low, west_high) = end_rows(2), end_rows(3)
        north = preb_ref[0:extent, :] + adds[0] + ends(west_low, east_low)
        south = preb_ref[extent : 2 * extent, :] + adds[1] + ends(west_high, east_high)

        def side(part, at):
            value = preb_ref[part * extent : (part + 1) * extent, :] + adds[part]
            return jnp.where(first, north[at : at + 1], jnp.where(final, south[at : at + 1], value))

        value, slope = gelu_parts(jnp.concatenate([north, south, side(2, extent - 1), side(3, 0)], axis=0))
        dadds = [dot_nt(columns[i], tap_columns(w2_ref[...], block_taps(i), channels)) for i in range(4)]
        high, low = halves(jnp.concatenate(dadds, axis=0))
        d_hidden = dhb_ref[...] + dot(back_ref[...], high) + dot(back_ref[...], low)
        d_pre = d_hidden * slope
        hidden = without_repeats(value, extent).astype(BF16)
        hid_ref[...] = hidden
        d_once = without_repeats(d_pre, extent).astype(BF16)
        dpre_ref[...] = d_once
        strips = dot(seam_ref[...], hidden).astype(BF16)
        a = [strips[start : start + rows] for start, rows in zip(block_starts(extent), block_rows(extent))]
        b = []
        tall = iota((16, 1), 0)
        for part in range(4):
            block = d_pre[part * extent : (part + 1) * extent]
            if part < 2:
                tile = jnp.where(tall == 0, block[0:1], jnp.where(tall == 1, block[extent - 1 : extent], 0.0))
                block = jnp.concatenate([block, tile], axis=0)
            b.append(block.astype(BF16))
        write_second(a, b, outs)
        own = dot_t(wx_ref[...], d_once)
        margin = margin_weight(x_strips, strip_columns(b, extent))
        for tap in range(9):
            span = slice(tap * channels, (tap + 1) * channels)
            total = sums_ref[0, span, :] + own[span]
            sum_ref[0, span, :] = total if margin[tap] is None else total + margin[tap]
        own = dot_t(hidden, wg_ref[...])
        margin = margin_weight(a, columns)
        for tap in range(9):
            span = slice(tap * channels, (tap + 1) * channels)
            total = sums_ref[1, span, :] + own[:, span]
            sum_ref[1, span, :] = total if margin[tap] is None else total + margin[tap]
        core = lax.axis_index("dp") % 2
        keep_ref[...] = sum_ref[core]
        send_ref[...] = sum_ref[1 - core].astype(BF16)

    results = call(
        middle,
        "gradients",
        [taps_f, taps_b, border_b, border_b] + second_routed,
        "v" * (9 + n_routes),
        (pre_b, dh_b, sums, seam_b, back_b, wx_b, wg_b, w_one, w_two, *first_arrived),
        scratch=[pltpu.VMEM((2,) + taps_f.shape, F32)],
        flops=conv // 4,
    )
    keep, send, hid_edge, dpre_edge = results[:4]

    def later(edge_ref, corner_ref, x_ref, g_ref, hid_ref, dpre_ref, hidb_ref, dpreb_ref, w1_ref, w2_ref, out_ref, dx_ref, scatter_ref, column_ref, q_ref):
        lines, pixels = seam_lines(edge_ref, corner_ref, extent)
        scatter_ref[...] = seam_scatter(lines, pixels, extent)
        column_ref[...] = column_scatter(extent)
        choice = border_choice(extent)
        hidden = hid_ref[...].astype(F32) + dot_t(choice, hidb_ref[...])
        d_pre = dpre_ref[...].astype(F32) + dot_t(choice, dpreb_ref[...])
        write_columns(q_ref, hidden, True, extent)
        window_product(q_ref, w2_ref[...], True, extent, out_ref)
        out_ref[...] = out_ref[...] + x_ref[...].astype(F32)
        write_columns(q_ref, d_pre, False, extent)
        window_product(q_ref, w1_ref[...], False, extent, dx_ref)
        dx_ref[...] = dx_ref[...] + g_ref[...].astype(F32)

    def later_parts(token):
        token, inner_arrays = lax.optimization_barrier((token, (hid_in, dpre_in, hid_edge, dpre_edge)))
        return token, call(
            later,
            "later_products",
            [image_f, image_f, scatter_b, column_b],
            "ss" + "v" * 8,
            (edge_code.T, corner_code.T, source, grad_out, *inner_arrays, w_one, w_two),
            scratch=[pltpu.VMEM(columns_b.shape, BF16)],
            flops=2 * conv,
        )

    if hops:
        whole, second_arrived, parts = reduce_gradients(keep, send, total, later_parts, *results[4:])
    else:
        second_arrived = exchange(results[4:], plan, tiles)
        whole, _, parts = reduce_gradients(keep, send, total, later_parts)

    def last(part_ref, dpart_ref, scatter_ref, column_ref, w1_ref, w2_ref, *refs):
        arrived = refs[:n_routes]
        out_ref, dx_ref = refs[n_routes:]
        h_strips, d_strips = read(arrived)
        out_ref[...] = (part_ref[...] + margin_forward(h_strips, w2_ref[...], column_ref[...], extent)).astype(BF16)
        add = margin_backward(strip_columns(d_strips, extent), w1_ref[...], scatter_ref[...], extent)
        dx_ref[...] = (dpart_ref[...] + add).astype(BF16)

    output, d_input = call(
        last,
        "outputs",
        [image_b, image_b],
        "v" * (6 + n_routes),
        (*parts, w_one, w_two, *second_arrived),
        flops=conv // 4,
    )
    whole, output, d_input = lax.optimization_barrier((whole, output, d_input))
    one, two = join_cores(whole, total)
    shape = (9, channels, channels)
    return (
        output.reshape(inputs.shape),
        d_input.reshape(inputs.shape),
        (one.astype(F32) * factor).reshape(shape),
        (two.astype(F32) * factor).reshape(shape),
    )


def solution(mesh):
    split = P("dp", "tile", None, None, None)
    return jax.shard_map(
        per_device,
        mesh=mesh,
        in_specs=(split, P(), P(), split, P(), P()),
        out_specs=(split, split, P(), P()),
        check_vma=False,
    )
```

```python
import functools
import math

import jax
import jax.numpy as jnp
from jax import lax
from jax.experimental import pallas as pl
from jax.experimental.pallas import tpu as pltpu
from jax.sharding import PartitionSpec as P

RW = 4
SIDES = (-RW, 1, RW, -1)
CORNERS = (-RW - 1, -RW + 1, RW + 1, RW - 1)
F32 = jnp.float32
BF16 = jnp.bfloat16
AXES = ("tile", "dp")
LIMIT = 20 * 1024 * 1024
ALONE = 60 * 1024 * 1024

BLOCKS = ((0, (0, 1)), (2, (3, 2)), (1, ()), (3, ()))


def block_rows(extent):
    return (extent + 16, extent + 16, extent, extent)


def block_starts(extent):
    rows = block_rows(extent)
    return (0, rows[0], rows[0] + rows[1], rows[0] + rows[1] + rows[2])


def block_taps(position):
    return ((0, 1, 2), (6, 7, 8), (2, 5, 8), (0, 3, 6))[position]


def routes(tiles):
    found = {}
    for kind, offsets in (("a", SIDES), ("b", SIDES), ("ac", CORNERS), ("bc", CORNERS)):
        for which, offset in enumerate(offsets):
            distance = (-offset if kind[0] == "a" else offset) % tiles
            found.setdefault(distance, []).append((kind, which))
    plan = []
    for distance, parts in found.items():
        sides = [p for p in parts if len(p[0]) == 1]
        corners = [p for p in parts if len(p[0]) == 2]
        plan.append((distance, sides, corners))
    return plan


def route_rows(route, extent):
    return extent * len(route[1]) + (16 if route[2] else 0)


def iota(shape, axis):
    return lax.broadcasted_iota(jnp.int32, shape, axis)


def dot(a, b):
    return lax.dot_general(a, b, (((1,), (0,)), ((), ())), preferred_element_type=F32)


def dot_nt(a, b):
    return lax.dot_general(a, b, (((1,), (1,)), ((), ())), preferred_element_type=F32)


def dot_t(a, b):
    return lax.dot_general(a, b, (((0,), (0,)), ((), ())), preferred_element_type=F32)


def corner_pixel(code, extent):
    last = extent - 1
    return jnp.where(code == 0, 0, jnp.where(code == 1, last, jnp.where(code == 2, extent * extent - 1, extent * last)))


def side_line(code, extent):
    last = extent - 1
    border = code % 4
    base = jnp.where(border == 1, last, jnp.where(border == 2, extent * last, 0))
    step = jnp.where(border % 2 == 0, 1, extent)
    return jnp.where(code >= 4, base + last * step, base), jnp.where(code >= 4, -step, step)


def seam_lines(edge_ref, corner_ref, extent):
    tiles = edge_ref.shape[1]
    mine = lax.axis_index("tile")
    lines = [side_line(edge_ref[k, (mine - o + tiles + RW * tiles) % tiles], extent) for k, o in enumerate(SIDES)]
    pixels = [corner_pixel(corner_ref[q, (mine - o + tiles + RW * tiles) % tiles], extent) for q, o in enumerate(CORNERS)]
    return lines, pixels


def fixed_lines(extent):
    last = extent - 1
    lines = [(0, 1), (last, extent), (extent * last, 1), (0, extent)]
    return lines, [0, last, extent * extent - 1, extent * last]


def pick_rows(indices, count):
    return (iota((indices.shape[0], count), 1) == indices).astype(F32).astype(BF16)


def line_rows(line, extent, count):
    return pick_rows(line[0] + line[1] * iota((extent, 1), 0), count)


def spot_rows(spots, count):
    rows = iota((16, 1), 0)
    index = jnp.full((16, 1), -1, jnp.int32)
    for row, pixel in spots:
        index = jnp.where(rows == row, pixel, index)
    return pick_rows(index, count)


def block_choice(lines, pixels, extent):
    count = extent * extent
    rows = []
    for side, corners in BLOCKS:
        rows.append(line_rows(lines[side], extent, count))
        if corners:
            rows.append(spot_rows([(i, pixels[q]) for i, q in enumerate(corners)], count))
    return jnp.concatenate(rows, axis=0)


def block_index(lines, pixels, axis, extent):
    starts = block_starts(extent)
    total = starts[3] + extent
    place = iota((total, 1) if axis == 0 else (1, total), axis)
    index = jnp.full(place.shape, -1, jnp.int32)
    for start, (side, ends) in zip(starts, BLOCKS):
        base, step = lines[side]
        index = jnp.where((place >= start) & (place < start + extent), base + step * (place - start), index)
        for i, q in enumerate(ends):
            index = jnp.where(place == start + extent + i, pixels[q], index)
    return index


def seam_scatter(lines, pixels, extent):
    return (iota((extent * extent, 1), 0) == block_index(lines, pixels, 1, extent)).astype(F32).astype(BF16)


def column_scatter(extent):
    lane = iota((1, 4 * extent), 1)
    target = (lane % extent) * extent + jnp.where(lane < 2 * extent, extent - 1, 0)
    return (iota((extent * extent, 1), 0) == target).astype(F32).astype(BF16)


def gather_blocks(choice, image, extent):
    strips = dot(choice, image).astype(BF16)
    starts = block_starts(extent)
    return [strips[start : start + rows] for start, rows in zip(starts, block_rows(extent))]


def write_routes(a_blocks, b_blocks, plan, out_refs, extent):
    side_at = {side: i for i, (side, _) in enumerate(BLOCKS)}
    corner_at = {q: (i, extent + j) for i, (_, corners) in enumerate(BLOCKS) for j, q in enumerate(corners)}
    for route, out in zip(plan, out_refs):
        at = 0
        for kind, side in route[1]:
            blocks = a_blocks if kind == "a" else b_blocks
            out[at : at + extent, :] = blocks[side_at[side]][:extent]
            at += extent
        if route[2]:
            rows = iota((16, 1), 0)
            tile = jnp.zeros((16, out.shape[1]), F32)
            for i, (kind, q) in enumerate(route[2]):
                block, row = corner_at[q]
                source = (a_blocks if kind == "ac" else b_blocks)[block][extent : extent + 16].astype(F32)
                tile = jnp.where(rows == i, source[row - extent : row - extent + 1], tile)
            out[at : at + 16, :] = tile.astype(BF16)


def read_routes(plan, in_refs, extent):
    sides, corners = {}, {}
    for route, ref in zip(plan, in_refs):
        at = 0
        for key in route[1]:
            sides[key] = ref[at : at + extent, :]
            at += extent
        if route[2]:
            tile = ref[at : at + 16, :].astype(F32)
            for i, key in enumerate(route[2]):
                corners[key] = tile[i : i + 1]
    result = []
    rows = iota((16, 1), 0)
    for kind in ("a", "b"):
        blocks = []
        for side, ends in BLOCKS:
            block = sides[(kind, side)]
            if ends:
                tile = jnp.zeros((16, block.shape[1]), F32)
                for i, q in enumerate(ends):
                    tile = jnp.where(rows == i, corners[(kind + "c", q)], tile)
                block = jnp.concatenate([block, tile.astype(BF16)], axis=0)
            blocks.append(block)
        result.append(blocks)
    return result


def relayed(tiles):
    return tiles == 8


def write_near(a_blocks, b_blocks, near_ref, extent):
    for i, block in enumerate((a_blocks[3], b_blocks[2], a_blocks[2], b_blocks[3])):
        near_ref[i * extent : (i + 1) * extent, :] = block
    rows = iota((16, 1), 0)
    tile = jnp.zeros((16, near_ref.shape[1]), F32)
    at = 0
    for blocks in (a_blocks, b_blocks):
        ends = [blocks[i][extent : extent + 16].astype(F32) for i in range(2)]
        for block, row in ((0, 0), (0, 1), (1, 1), (1, 0)):
            tile = jnp.where(rows == at, ends[block][row : row + 1], tile)
            at += 1
    near_ref[4 * extent : 4 * extent + 16, :] = tile.astype(BF16)


def write_far(a_blocks, b_blocks, far_ref, extent):
    for i, block in enumerate((a_blocks[0], a_blocks[1], b_blocks[0], b_blocks[1])):
        far_ref[i * extent : (i + 1) * extent, :] = block[:extent]


def near_starts(tile, extent):
    right = tile % 2
    odd = (tile // 2) % 2
    corners = 2 * extent + 16
    side = jnp.where(right == 1, 0, 2 * extent)
    one = jnp.where(right == odd, corners, side)
    three = jnp.where(right == odd, side, corners)
    return side_of_partner(right, extent), one, three


def side_of_partner(right, extent):
    return jnp.where(right == 1, 2 * extent, 0)


def read_relay(refs, extent):
    across, one, three, far, opposite = refs
    mine = lax.axis_index("tile")
    left = mine % 2 == 0
    odd = (mine // 2 + mine) % 2 == 1

    def rows_of(ref, start, count):
        return ref[start : start + count, :].astype(F32)

    def choose(start, count):
        return jnp.where(odd, rows_of(one, start, count), rows_of(three, start, count))

    pair = [(rows_of(across, i * extent, extent), choose(i * extent, extent)) for i in range(2)]
    a_east, b_west = [jnp.where(left, here, there).astype(BF16) for here, there in pair]
    a_west, b_east = [jnp.where(left, there, here).astype(BF16) for here, there in pair]
    tail = 2 * extent - 16
    beside = jnp.where(odd, rows_of(three, tail, 16), rows_of(one, tail, 16))
    beyond = opposite[0:16, :].astype(F32)
    third = jnp.where(left, beside, beyond)
    fifth = jnp.where(left, beyond, beside)
    corners = {("a", 0): third[0:1], ("a", 3): third[3:4], ("b", 1): third[5:6], ("b", 2): third[6:7]}
    corners.update({("a", 1): fifth[1:2], ("a", 2): fifth[2:3], ("b", 0): fifth[4:5], ("b", 3): fifth[7:8]})
    rows = iota((16, 1), 0)
    result = []
    for kind, first, east, west in (("a", 0, a_east, a_west), ("b", 2, b_east, b_west)):
        blocks = []
        for i, ends in enumerate(((0, 1), (3, 2))):
            tile = jnp.where(rows == 0, corners[(kind, ends[0])], jnp.where(rows == 1, corners[(kind, ends[1])], 0.0))
            strip = far[(first + i) * extent : (first + i + 1) * extent, :]
            blocks.append(jnp.concatenate([strip, tile.astype(BF16)], axis=0))
        result.append(blocks + [east, west])
    return result


def shifted(image, by, extent):
    if by == 0:
        return image
    column = iota((image.shape[0], 1), 0) % extent
    rolled = pltpu.roll(image, (-by) % image.shape[0], 0)
    return jnp.where(column == (extent - 1 if by == 1 else 0), 0.0, rolled)


def write_columns(q_ref, image, forward, extent):
    count, channels = image.shape
    zero = jnp.zeros((extent, q_ref.shape[1]), BF16)
    q_ref[0:extent, :] = zero
    q_ref[extent + count : 2 * extent + count, :] = zero
    wide = image.astype(F32)
    for b in range(3):
        by = b - 1 if forward else 1 - b
        q_ref[extent : extent + count, b * channels : (b + 1) * channels] = shifted(wide, by, extent).astype(BF16)


def window_product(q_ref, weight, forward, extent, out_ref, chunk=8):
    channels = weight.shape[1]
    if forward:
        taps = tap_weight(weight, range(9), channels)
        nothing = jnp.zeros((3 * channels, channels), weight.dtype)
        both = jnp.concatenate([jnp.concatenate([taps, nothing], axis=0), jnp.concatenate([nothing, taps], axis=0)], axis=1)
    else:
        taps = tap_columns(weight, (6, 7, 8, 3, 4, 5, 0, 1, 2), channels)
        nothing = jnp.zeros((channels, 3 * channels), weight.dtype)
        both = jnp.concatenate([jnp.concatenate([taps, nothing], axis=1), jnp.concatenate([nothing, taps], axis=1)], axis=0)
    for start in range(0, extent // 2, chunk):
        rows = []
        for a in range(4):
            rows.append(jnp.concatenate([q_ref[(2 * i + a) * extent : (2 * i + a + 1) * extent, :] for i in range(start, start + chunk)], axis=0))
        product = (dot if forward else dot_nt)(jnp.concatenate(rows, axis=1), both)
        for i in range(chunk):
            for half in range(2):
                at = (2 * (start + i) + half) * extent
                out_ref[at : at + extent, :] = product[i * extent : (i + 1) * extent, half * channels : (half + 1) * channels]


def tap_weight(weight, taps, channels):
    return jnp.concatenate([weight[t * channels : (t + 1) * channels, :] for t in taps], axis=0)


def tap_columns(weight, taps, channels):
    return jnp.concatenate([weight[t * channels : (t + 1) * channels, :] for t in taps], axis=1)


def halves(values):
    high = values.astype(BF16)
    return high, (values - high.astype(F32)).astype(BF16)


def margin_adds(strips, weight, extent):
    channels = strips[0].shape[1]
    adds = []
    for position, (side, ends) in enumerate(BLOCKS):
        middle = strips[position][:extent].astype(F32)
        row = iota((extent, 1), 0)
        before, after = 0.0, 0.0
        if ends:
            tile = strips[position][extent : extent + 16].astype(F32)
            before, after = tile[0:1], tile[1:2]
        left = jnp.where(row == 0, before, pltpu.roll(middle, 1, 0))
        right = jnp.where(row == extent - 1, after, pltpu.roll(middle, extent - 1, 0))
        window = jnp.concatenate([left, middle, right], axis=1).astype(BF16)
        adds.append(dot(window, tap_weight(weight, block_taps(position), channels)))
    return adds


def margin_forward(strips, weight, columns, extent):
    count = extent * extent
    adds = margin_adds(strips, weight, extent)
    spread = jnp.concatenate(list(halves(adds[2])) + list(halves(adds[3])), axis=0)
    image = dot(columns, spread)
    top = image[:extent] + adds[0]
    bottom = image[count - extent :] + adds[1]
    return jnp.concatenate([top, image[extent : count - extent], bottom], axis=0)


def strip_columns(strips, extent):
    result = []
    for position, (side, ends) in enumerate(BLOCKS):
        middle = strips[position][:extent].astype(F32)
        row = iota((extent, 1), 0)
        after = jnp.where(row == extent - 1, 0.0, pltpu.roll(middle, extent - 1, 0))
        before = jnp.where(row == 0, 0.0, pltpu.roll(middle, 1, 0))
        columns = jnp.concatenate([after, middle, before], axis=1)
        if ends:
            tile = strips[position][extent : extent + 16].astype(F32)
            row = iota((16, 1), 0)
            low = jnp.where(row == 0, tile, 0.0)
            high = jnp.where(row == 1, tile, 0.0)
            columns = jnp.concatenate([columns, jnp.concatenate([low, jnp.zeros_like(tile), high], axis=1)], axis=0)
        result.append(columns.astype(BF16))
    return result


def margin_backward(columns, weight, scatter, extent):
    channels = weight.shape[1]
    adds = [dot_nt(columns[i], tap_columns(weight, block_taps(i), channels)) for i in range(4)]
    high, low = halves(jnp.concatenate(adds, axis=0))
    return dot(scatter, high) + dot(scatter, low)


def weight_sum(out_ref, image_t, q_ref, extent):
    channels = image_t.shape[0]
    count = image_t.shape[1]
    rows = jnp.concatenate([q_ref[(2 - a) * extent : (2 - a) * extent + count, :] for a in range(3)], axis=1)
    product = dot(image_t, rows)
    for tap in range(9):
        out_ref[tap * channels : (tap + 1) * channels, :] = product[:, tap * channels : (tap + 1) * channels]


def margin_weight(strips, columns):
    channels = strips[0].shape[1]
    wide = [dot_t(strips[i], columns[i]) for i in range(4)]
    result = []
    for tap in range(9):
        value = None
        for position in range(4):
            taps = block_taps(position)
            if tap in taps:
                at = taps.index(tap)
                part = wide[position][:, at * channels : (at + 1) * channels]
                value = part if value is None else value + part
        result.append(value)
    return result


def border_index(place, extent, unique):
    last = extent - 1
    part, j = place // extent, place % extent
    index = jnp.where(part == 0, j, jnp.where(part == 1, extent * last + j, jnp.where(part == 2, extent * j + last, extent * j)))
    if unique:
        index = jnp.where((part >= 2) & ((j == 0) | (j == last)), -2, index)
    return index


def border_choice(extent):
    return pick_rows(border_index(iota((4 * extent, 1), 0), extent, True), extent * extent)


def border_of(ref, extent):
    count = extent * extent
    east = ref[pl.ds(extent - 1, extent, stride=extent), :]
    west = ref[pl.ds(0, extent, stride=extent), :]
    return jnp.concatenate([ref[0:extent, :], ref[count - extent : count, :], east, west], axis=0)


def without_repeats(border, extent):
    place = iota((border.shape[0], 1), 0)
    return jnp.where(border_index(place, extent, True) < 0, 0.0, border)


def moved(column, by, extent):
    if by == 0:
        return column
    row = iota((extent, 1), 0)
    return jnp.where(row == (extent - 1 if by == 1 else 0), 0.0, pltpu.roll(column, (-by) % extent, 0))


def border_windows(out_ref, wide_ref, q_ref, forward, extent):
    count, channels = wide_ref.shape
    columns = {c: wide_ref[pl.ds(c, extent, stride=extent), :] for c in (0, 1, extent - 2, extent - 1)}
    nothing = jnp.zeros((extent, channels), F32)
    row = iota((extent, 1), 0)
    inside = (row > 0) & (row < extent - 1)
    for a in range(3):
        start = (a if forward else 2 - a) * extent
        lanes = slice(a * 3 * channels, (a + 1) * 3 * channels)
        out_ref[0:extent, lanes] = q_ref[start : start + extent, :]
        out_ref[extent : 2 * extent, lanes] = q_ref[start + count - extent : start + count, :]
        for part, column in ((2, extent - 1), (3, 0)):
            pieces = []
            for b in range(3):
                at = column + (b - 1 if forward else 1 - b)
                pieces.append(moved(columns[at], a - 1 if forward else 1 - a, extent) if at in columns else nothing)
            value = jnp.where(inside, jnp.concatenate(pieces, axis=1), 0.0)
            out_ref[part * extent : (part + 1) * extent, lanes] = value.astype(BF16)


def gelu_parts(u):
    scale = math.sqrt(2.0 / math.pi)
    square = u * u
    half = 0.5 * u
    t = jnp.tanh(u * (scale + (scale * 0.044715) * square))
    value = half + half * t
    slope = (0.5 + 0.5 * t) + (half * (1.0 - t * t)) * (scale + (scale * 3.0 * 0.044715) * square)
    return value, slope


def call(kernel, name, outs, ins, operands, scratch=(), flops=0, limit=LIMIT):
    specs = [pl.BlockSpec(memory_space={"a": pl.ANY, "s": pltpu.SMEM, "v": pltpu.VMEM}[i]) for i in ins]
    moved = sum(math.prod(o.shape) * o.dtype.itemsize for o in list(outs) + list(operands))
    return pl.pallas_call(
        kernel,
        name=name,
        out_shape=outs,
        in_specs=specs,
        out_specs=[pl.BlockSpec(memory_space=pltpu.VMEM) for _ in outs],
        scratch_shapes=list(scratch),
        cost_estimate=pl.CostEstimate(flops=flops, bytes_accessed=moved, transcendentals=0),
        compiler_params=pltpu.CompilerParams(vmem_limit_bytes=limit),
    )(*operands)


def sds(shape, dtype):
    return jax.ShapeDtypeStruct(shape, dtype)


def exchange(payloads, plan, tiles):
    return [
        lax.ppermute(p, "tile", [(i, (i + route[0]) % tiles) for i in range(tiles)]) for p, route in zip(payloads, plan)
    ]


def swap(value, mask, total):
    return lax.ppermute(value, AXES, [(i, i ^ mask) for i in range(total)])


def reduce_gradients(keep, send, total, work, near=None, far=None):
    rows, channels = keep.shape
    quarter = rows // 4
    wire = BF16 if total <= 32 else F32
    me = lax.axis_index(AXES)
    other = swap(send, 1, total)
    plane = (me >> 1) & 3

    def chunk(index):
        first = lax.dynamic_index_in_dim(keep.reshape(4, quarter, channels), index, 0, keepdims=False)
        second = lax.dynamic_index_in_dim(other.reshape(4, quarter, channels), index, 0, keepdims=False)
        return first + second.astype(F32)

    arrived = {}
    for m in (3, 1, 2):
        message = chunk(plane ^ m).astype(wire)
        if m == 2 and near is not None:
            message = jnp.concatenate([message, near], axis=0)
        arrived[m] = swap(message, m << 1, total)
    part = chunk(plane)
    for m in (3, 1, 2):
        part = part + arrived[m][:quarter].astype(F32)
    part, done = work(part)
    extras = None
    if near is not None:
        across = arrived[2][quarter:]
        extent = far.shape[0] // 4
        starts = near_starts(lax.axis_index("tile") ^ 1, extent)
        direct, one, three = [lax.dynamic_slice_in_dim(across, start, 2 * extent, 0) for start in starts]
        riders = {1: (one,), 2: (far, across[-16:]), 3: (three,)}
    bit = 8
    while bit < total:
        mine = part.astype(wire)
        if 2 * bit < total:
            got = {}
            for m in (3, 2, 1):
                message = mine
                if near is not None:
                    message = jnp.concatenate([mine, *riders[m]], axis=0)
                got[m] = swap(message, m * bit, total)
            part = (mine.astype(F32) + got[1][:quarter].astype(F32)) + (got[2][:quarter].astype(F32) + got[3][:quarter].astype(F32))
            if near is not None:
                extras = [direct, got[1][quarter:], got[3][quarter:], got[2][quarter:-16], got[2][-16:]]
            bit *= 4
        else:
            part = mine.astype(F32) + swap(mine, bit, total).astype(F32)
            bit *= 2
    part, done = lax.optimization_barrier((part, done))
    mine = part.astype(wire)
    ring = jnp.stack([mine] + [swap(mine, m << 1, total) for m in (1, 2, 3)])
    whole = jnp.concatenate([lax.dynamic_index_in_dim(ring, plane ^ j, 0) for j in range(4)], axis=0)
    return whole, extras, done


def join_cores(whole, factor, total):
    rows, channels = whole.shape
    half = sds(whole.shape, F32)
    pieces = 2
    step = rows // pieces

    def write(flip, value_ref, outs, scaled_ref, sems):
        mine = (lax.axis_index("dp") + flip) % 2

        def send(out_ref):
            copies = []
            for i in range(pieces):
                span = pl.ds(i * step, step)
                scaled_ref[span, :] = value_ref[span, :].astype(F32) * factor
                copies.append(pltpu.make_async_copy(scaled_ref.at[span], out_ref.at[span], sems.at[i]))
                copies[-1].start()
            for copy in copies:
                copy.wait()

        for which in range(2):
            pl.when(mine == which)(functools.partial(send, outs[which]))

    def own_half(value_ref, one_ref, two_ref, scaled_ref, sems):
        write(0, value_ref, (one_ref, two_ref), scaled_ref, sems)

    def other_half(value_ref, one_in, two_in, one_ref, two_ref, scaled_ref, sems):
        write(1, value_ref, (one_ref, two_ref), scaled_ref, sems)

    def run(kernel, name, operands, aliases):
        anywhere = pl.BlockSpec(memory_space=pl.ANY)
        return pl.pallas_call(
            kernel,
            name=name,
            out_shape=[half, half],
            in_specs=[pl.BlockSpec(memory_space=pltpu.VMEM)] + [anywhere] * (len(operands) - 1),
            out_specs=[anywhere, anywhere],
            scratch_shapes=[pltpu.VMEM(half.shape, F32), pltpu.SemaphoreType.DMA((pieces,))],
            input_output_aliases=aliases,
            cost_estimate=pl.CostEstimate(flops=rows * channels, bytes_accessed=6 * rows * channels, transcendentals=0),
            compiler_params=pltpu.CompilerParams(vmem_limit_bytes=LIMIT),
        )(*operands)

    other = swap(whole, 1, total)
    begun = run(own_half, "own_half", (whole,), {})
    return run(other_half, "other_half", (other, *begun), {1: 0, 2: 1})


def reach_neighbours(across, one, three, far, total):
    two, three, one = swap(far, 16, total), swap(three, 28, total), swap(one, 12, total)
    across = swap(jnp.concatenate([across, two[-16:]], axis=0), 4, total)
    return [across, one, three, two[:-16], across[-16:]]


def per_device(inputs, weight_one, weight_two, cotangent, edge_code, corner_code):
    tiles, members = lax.axis_size("tile"), lax.axis_size("dp")
    extent, channels = inputs.shape[2], inputs.shape[4]
    count = extent * extent
    factor = 1.0 / math.sqrt(inputs.shape[0] * members * tiles * count)
    source = inputs.reshape(count, channels)
    grad_out = cotangent.reshape(count, channels)
    w_one = weight_one.reshape(9 * channels, channels)
    w_two = weight_two.reshape(9 * channels, channels)
    plan = routes(tiles)
    total = tiles * members
    hops = relayed(tiles)
    near_b, far_b, corner_b = sds((4 * extent + 16, channels), BF16), sds((4 * extent, channels), BF16), sds((16, channels), BF16)
    pair_b = sds((2 * extent, channels), BF16)
    if hops:
        first_routed, second_routed = [pair_b, pair_b, pair_b, sds((4 * extent + 16, channels), BF16)], [near_b, far_b]
        n_routes = 5
    else:
        first_routed = second_routed = [sds((route_rows(r, extent), channels), BF16) for r in plan]
        n_routes = len(plan)
    n_first, n_second = len(first_routed), len(second_routed)

    def write_first(a, b, outs, near_ref):
        if hops:
            write_near(a, b, near_ref, extent)
            write_far(a, b, outs[3], extent)
            for start, out in zip(near_starts(lax.axis_index("tile"), extent), outs):
                out[...] = near_ref[pl.ds(pl.multiple_of(start, 16), 2 * extent), :]
            outs[3][4 * extent : 4 * extent + 16, :] = near_ref[4 * extent : 4 * extent + 16, :]
        else:
            write_routes(a, b, plan, outs, extent)

    def write_second(a, b, outs):
        if hops:
            write_near(a, b, outs[0], extent)
            write_far(a, b, outs[1], extent)
        else:
            write_routes(a, b, plan, outs, extent)

    def read(refs):
        return read_relay(refs, extent) if hops else read_routes(plan, refs, extent)

    image_b, image_f = sds((count, channels), BF16), sds((count, channels), F32)
    columns_b = sds((count + 2 * extent, 3 * channels), BF16)
    taps_b, taps_f = sds((9 * channels, channels), BF16), sds((9 * channels, channels), F32)
    conv = 2 * count * 9 * channels * channels

    strip_rows = block_starts(extent)[3] + extent
    scatter_b, column_b = sds((count, strip_rows), BF16), sds((count, 4 * extent), BF16)
    pieces = 2

    def first_strips(x_hbm, g_hbm, edge_hbm, corner_hbm, *refs):
        outs = refs[:n_first]
        x_ref, g_ref, near_ref, edge_ref, corner_ref, sems = refs[n_first:]
        pairs = [(edge_hbm, edge_ref), (corner_hbm, corner_ref)]
        step = count // pieces
        for source_ref, target_ref in ((x_hbm, x_ref), (g_hbm, g_ref)):
            for i in range(pieces):
                pairs.append((source_ref.at[pl.ds(i * step, step)], target_ref.at[pl.ds(i * step, step)]))
        copies = [pltpu.make_async_copy(a, b, sems.at[i]) for i, (a, b) in enumerate(pairs)]
        for copy in copies:
            copy.start()
        fixed = block_choice(*fixed_lines(extent), extent)
        for copy in copies[:2]:
            copy.wait()
        seam = block_choice(*seam_lines(edge_ref, corner_ref, extent), extent)
        for copy in copies[2:]:
            copy.wait()
        a = gather_blocks(seam, x_ref[...], extent)
        b = gather_blocks(fixed, g_ref[...], extent)
        write_first(a, b, outs, near_ref)

    first = call(
        first_strips,
        "first_strips",
        first_routed,
        "aaaa",
        (source, grad_out, edge_code.T, corner_code.T),
        scratch=[
            pltpu.VMEM((count, channels), BF16),
            pltpu.VMEM((count, channels), BF16),
            pltpu.VMEM(near_b.shape, BF16),
            pltpu.SMEM((4, tiles), jnp.int32),
            pltpu.SMEM((4, tiles), jnp.int32),
            pltpu.SemaphoreType.DMA((2 + 2 * pieces,)),
        ],
        limit=ALONE,
        flops=10 * conv,
    )
    first_arrived = reach_neighbours(*first, total) if hops else exchange(first, plan, tiles)

    border = 4 * extent
    border_b, border_f = sds((border, channels), BF16), sds((border, channels), F32)
    windows_b = sds((border, 9 * channels), BF16)

    def inner(edge_ref, corner_ref, x_ref, g_ref, w1_ref, w2_ref, *refs):
        hid_ref, dpre_ref, preb_ref, dhb_ref, sum_ref, seam_ref, back_ref, wx_ref, wg_ref = refs[:9]
        qx_ref, qg_ref, qd_ref, pre_ref, dh_ref, wide_ref = refs[9:]
        wide_ref[...] = x_ref[...].astype(F32)
        write_columns(qx_ref, x_ref[...], True, extent)
        border_windows(wx_ref, wide_ref, qx_ref, True, extent)
        window_product(qx_ref, w1_ref[...], True, extent, pre_ref)
        wide_ref[...] = g_ref[...].astype(F32)
        write_columns(qg_ref, g_ref[...], False, extent)
        border_windows(wg_ref, wide_ref, qg_ref, False, extent)
        window_product(qg_ref, w2_ref[...], False, extent, dh_ref)
        preb_ref[...] = border_of(pre_ref, extent)
        dhb_ref[...] = border_of(dh_ref, extent)
        place = iota((count, 1), 0)
        row, column = place // extent, place % extent
        inside = (row > 0) & (row < extent - 1) & (column > 0) & (column < extent - 1)
        value, slope = gelu_parts(pre_ref[...])
        value = jnp.where(inside, value, 0.0)
        hid_ref[...] = value.astype(BF16)
        dpre_ref[...] = jnp.where(inside, dh_ref[...] * slope, 0.0).astype(BF16)
        write_columns(qd_ref, dpre_ref[...], False, extent)
        weight_sum(sum_ref.at[0], jnp.transpose(x_ref[...].astype(F32)).astype(BF16), qd_ref, extent)
        weight_sum(sum_ref.at[1], jnp.transpose(value).astype(BF16), qg_ref, extent)
        lines, pixels = seam_lines(edge_ref, corner_ref, extent)
        across = border_index(iota((1, border), 1), extent, True)
        seam_ref[...] = (block_index(lines, pixels, 0, extent) == across).astype(F32).astype(BF16)
        down = border_index(iota((border, 1), 0), extent, False)
        back_ref[...] = (down == block_index(lines, pixels, 1, extent)).astype(F32).astype(BF16)

    hid_in, dpre_in, pre_b, dh_b, sums, seam_b, back_b, wx_b, wg_b = call(
        inner,
        "inner_products",
        [
            image_b,
            image_b,
            border_f,
            border_f,
            sds((2,) + taps_f.shape, F32),
            sds((strip_rows, border), BF16),
            sds((border, strip_rows), BF16),
            windows_b,
            windows_b,
        ],
        "ssvvvv",
        (edge_code.T, corner_code.T, source, grad_out, w_one, w_two),
        scratch=[pltpu.VMEM(columns_b.shape, BF16)] * 3 + [pltpu.VMEM(image_f.shape, F32)] * 3,
        flops=4 * conv,
    )

    def middle(preb_ref, dhb_ref, sums_ref, seam_ref, back_ref, wx_ref, wg_ref, w1_ref, w2_ref, *refs):
        arrived = refs[:n_routes]
        keep_ref, send_ref, hid_ref, dpre_ref = refs[n_routes : n_routes + 4]
        outs = refs[n_routes + 4 : n_routes + 4 + n_second]
        (sum_ref,) = refs[n_routes + 4 + n_second :]
        x_strips, g_strips = read(arrived)
        columns = strip_columns(g_strips, extent)
        adds = margin_adds(x_strips, w1_ref[...], extent)
        row = iota((extent, 1), 0)
        first, final = row == 0, row == extent - 1

        def ends(low, high):
            return jnp.where(first, low, 0.0) + jnp.where(final, high, 0.0)

        def end_rows(part):
            return adds[part][0:1], adds[part][extent - 1 : extent]

        (east_low, east_high), (west_low, west_high) = end_rows(2), end_rows(3)
        north = preb_ref[0:extent, :] + adds[0] + ends(west_low, east_low)
        south = preb_ref[extent : 2 * extent, :] + adds[1] + ends(west_high, east_high)

        def side(part, at):
            value = preb_ref[part * extent : (part + 1) * extent, :] + adds[part]
            return jnp.where(first, north[at : at + 1], jnp.where(final, south[at : at + 1], value))

        value, slope = gelu_parts(jnp.concatenate([north, south, side(2, extent - 1), side(3, 0)], axis=0))
        dadds = [dot_nt(columns[i], tap_columns(w2_ref[...], block_taps(i), channels)) for i in range(4)]
        high, low = halves(jnp.concatenate(dadds, axis=0))
        d_hidden = dhb_ref[...] + dot(back_ref[...], high) + dot(back_ref[...], low)
        d_pre = d_hidden * slope
        hidden = without_repeats(value, extent).astype(BF16)
        hid_ref[...] = hidden
        d_once = without_repeats(d_pre, extent).astype(BF16)
        dpre_ref[...] = d_once
        strips = dot(seam_ref[...], hidden).astype(BF16)
        a = [strips[start : start + rows] for start, rows in zip(block_starts(extent), block_rows(extent))]
        b = []
        tall = iota((16, 1), 0)
        for part in range(4):
            block = d_pre[part * extent : (part + 1) * extent]
            if part < 2:
                tile = jnp.where(tall == 0, block[0:1], jnp.where(tall == 1, block[extent - 1 : extent], 0.0))
                block = jnp.concatenate([block, tile], axis=0)
            b.append(block.astype(BF16))
        write_second(a, b, outs)
        own = dot_t(wx_ref[...], d_once)
        margin = margin_weight(x_strips, strip_columns(b, extent))
        for tap in range(9):
            span = slice(tap * channels, (tap + 1) * channels)
            total = sums_ref[0, span, :] + own[span]
            sum_ref[0, span, :] = total if margin[tap] is None else total + margin[tap]
        own = dot_t(hidden, wg_ref[...])
        margin = margin_weight(a, columns)
        for tap in range(9):
            span = slice(tap * channels, (tap + 1) * channels)
            total = sums_ref[1, span, :] + own[:, span]
            sum_ref[1, span, :] = total if margin[tap] is None else total + margin[tap]
        core = lax.axis_index("dp") % 2
        keep_ref[...] = sum_ref[core]
        send_ref[...] = sum_ref[1 - core].astype(BF16)

    results = call(
        middle,
        "gradients",
        [taps_f, taps_b, border_b, border_b] + second_routed,
        "v" * (9 + n_routes),
        (pre_b, dh_b, sums, seam_b, back_b, wx_b, wg_b, w_one, w_two, *first_arrived),
        scratch=[pltpu.VMEM((2,) + taps_f.shape, F32)],
        flops=conv // 4,
    )
    keep, send, hid_edge, dpre_edge = results[:4]

    def later(edge_ref, corner_ref, x_ref, g_ref, hid_ref, dpre_ref, hidb_ref, dpreb_ref, w1_ref, w2_ref, out_ref, dx_ref, scatter_ref, column_ref, q_ref):
        lines, pixels = seam_lines(edge_ref, corner_ref, extent)
        scatter_ref[...] = seam_scatter(lines, pixels, extent)
        column_ref[...] = column_scatter(extent)
        choice = border_choice(extent)
        hidden = hid_ref[...].astype(F32) + dot_t(choice, hidb_ref[...])
        d_pre = dpre_ref[...].astype(F32) + dot_t(choice, dpreb_ref[...])
        write_columns(q_ref, hidden, True, extent)
        window_product(q_ref, w2_ref[...], True, extent, out_ref)
        out_ref[...] = out_ref[...] + x_ref[...].astype(F32)
        write_columns(q_ref, d_pre, False, extent)
        window_product(q_ref, w1_ref[...], False, extent, dx_ref)
        dx_ref[...] = dx_ref[...] + g_ref[...].astype(F32)

    def later_parts(token):
        token, inner_arrays = lax.optimization_barrier((token, (hid_in, dpre_in, hid_edge, dpre_edge)))
        return token, call(
            later,
            "later_products",
            [image_f, image_f, scatter_b, column_b],
            "ss" + "v" * 8,
            (edge_code.T, corner_code.T, source, grad_out, *inner_arrays, w_one, w_two),
            scratch=[pltpu.VMEM(columns_b.shape, BF16)],
            flops=2 * conv,
        )

    if hops:
        whole, second_arrived, parts = reduce_gradients(keep, send, total, later_parts, *results[4:])
    else:
        second_arrived = exchange(results[4:], plan, tiles)
        whole, _, parts = reduce_gradients(keep, send, total, later_parts)

    def last(part_ref, dpart_ref, scatter_ref, column_ref, w1_ref, w2_ref, *refs):
        arrived = refs[:n_routes]
        out_ref, dx_ref = refs[n_routes:]
        h_strips, d_strips = read(arrived)
        out_ref[...] = (part_ref[...] + margin_forward(h_strips, w2_ref[...], column_ref[...], extent)).astype(BF16)
        add = margin_backward(strip_columns(d_strips, extent), w1_ref[...], scatter_ref[...], extent)
        dx_ref[...] = (dpart_ref[...] + add).astype(BF16)

    output, d_input = call(
        last,
        "outputs",
        [image_b, image_b],
        "v" * (6 + n_routes),
        (*parts, w_one, w_two, *second_arrived),
        flops=conv // 4,
    )
    whole, output, d_input = lax.optimization_barrier((whole, output, d_input))
    one, two = join_cores(whole.reshape(9 * channels, channels), factor, total)
    shape = (9, channels, channels)
    return (
        output.reshape(inputs.shape),
        d_input.reshape(inputs.shape),
        one.reshape(shape),
        two.reshape(shape),
    )


def solution(mesh):
    split = P("dp", "tile", None, None, None)
    return jax.shard_map(
        per_device,
        mesh=mesh,
        in_specs=(split, P(), P(), split, P(), P()),
        out_specs=(split, split, P(), P()),
        check_vma=False,
    )
```

```python
import functools
import math

import jax
import jax.numpy as jnp
from jax import lax
from jax.experimental import pallas as pl
from jax.experimental.pallas import tpu as pltpu
from jax.sharding import PartitionSpec as P

RW = 4
SIDES = (-RW, 1, RW, -1)
CORNERS = (-RW - 1, -RW + 1, RW + 1, RW - 1)
F32 = jnp.float32
BF16 = jnp.bfloat16
AXES = ("tile", "dp")
LIMIT = 20 * 1024 * 1024
ALONE = 60 * 1024 * 1024

BLOCKS = ((0, (0, 1)), (2, (3, 2)), (1, ()), (3, ()))


def block_rows(extent):
    return (extent + 16, extent + 16, extent, extent)


def block_starts(extent):
    rows = block_rows(extent)
    return (0, rows[0], rows[0] + rows[1], rows[0] + rows[1] + rows[2])


def block_taps(position):
    return ((0, 1, 2), (6, 7, 8), (2, 5, 8), (0, 3, 6))[position]


def routes(tiles):
    found = {}
    for kind, offsets in (("a", SIDES), ("b", SIDES), ("ac", CORNERS), ("bc", CORNERS)):
        for which, offset in enumerate(offsets):
            distance = (-offset if kind[0] == "a" else offset) % tiles
            found.setdefault(distance, []).append((kind, which))
    plan = []
    for distance, parts in found.items():
        sides = [p for p in parts if len(p[0]) == 1]
        corners = [p for p in parts if len(p[0]) == 2]
        plan.append((distance, sides, corners))
    return plan


def route_rows(route, extent):
    return extent * len(route[1]) + (16 if route[2] else 0)


def iota(shape, axis):
    return lax.broadcasted_iota(jnp.int32, shape, axis)


def dot(a, b):
    return lax.dot_general(a, b, (((1,), (0,)), ((), ())), preferred_element_type=F32)


def dot_nt(a, b):
    return lax.dot_general(a, b, (((1,), (1,)), ((), ())), preferred_element_type=F32)


def dot_t(a, b):
    return lax.dot_general(a, b, (((0,), (0,)), ((), ())), preferred_element_type=F32)


def corner_pixel(code, extent):
    last = extent - 1
    return jnp.where(code == 0, 0, jnp.where(code == 1, last, jnp.where(code == 2, extent * extent - 1, extent * last)))


def side_line(code, extent):
    last = extent - 1
    border = code % 4
    base = jnp.where(border == 1, last, jnp.where(border == 2, extent * last, 0))
    step = jnp.where(border % 2 == 0, 1, extent)
    return jnp.where(code >= 4, base + last * step, base), jnp.where(code >= 4, -step, step)


def seam_lines(edge_ref, corner_ref, extent):
    tiles = edge_ref.shape[1]
    mine = lax.axis_index("tile")
    lines = [side_line(edge_ref[k, (mine - o + tiles + RW * tiles) % tiles], extent) for k, o in enumerate(SIDES)]
    pixels = [corner_pixel(corner_ref[q, (mine - o + tiles + RW * tiles) % tiles], extent) for q, o in enumerate(CORNERS)]
    return lines, pixels


def fixed_lines(extent):
    last = extent - 1
    lines = [(0, 1), (last, extent), (extent * last, 1), (0, extent)]
    return lines, [0, last, extent * extent - 1, extent * last]


def pick_rows(indices, count):
    return (iota((indices.shape[0], count), 1) == indices).astype(F32).astype(BF16)


def line_rows(line, extent, count):
    return pick_rows(line[0] + line[1] * iota((extent, 1), 0), count)


def spot_rows(spots, count):
    rows = iota((16, 1), 0)
    index = jnp.full((16, 1), -1, jnp.int32)
    for row, pixel in spots:
        index = jnp.where(rows == row, pixel, index)
    return pick_rows(index, count)


def block_choice(lines, pixels, extent):
    count = extent * extent
    rows = []
    for side, corners in BLOCKS:
        rows.append(line_rows(lines[side], extent, count))
        if corners:
            rows.append(spot_rows([(i, pixels[q]) for i, q in enumerate(corners)], count))
    return jnp.concatenate(rows, axis=0)


def block_index(lines, pixels, axis, extent):
    starts = block_starts(extent)
    total = starts[3] + extent
    place = iota((total, 1) if axis == 0 else (1, total), axis)
    index = jnp.full(place.shape, -1, jnp.int32)
    for start, (side, ends) in zip(starts, BLOCKS):
        base, step = lines[side]
        index = jnp.where((place >= start) & (place < start + extent), base + step * (place - start), index)
        for i, q in enumerate(ends):
            index = jnp.where(place == start + extent + i, pixels[q], index)
    return index


def seam_scatter(lines, pixels, extent):
    return (iota((extent * extent, 1), 0) == block_index(lines, pixels, 1, extent)).astype(F32).astype(BF16)


def column_scatter(extent):
    lane = iota((1, 4 * extent), 1)
    target = (lane % extent) * extent + jnp.where(lane < 2 * extent, extent - 1, 0)
    return (iota((extent * extent, 1), 0) == target).astype(F32).astype(BF16)


def gather_blocks(choice, image, extent):
    strips = dot(choice, image).astype(BF16)
    starts = block_starts(extent)
    return [strips[start : start + rows] for start, rows in zip(starts, block_rows(extent))]


def write_routes(a_blocks, b_blocks, plan, out_refs, extent):
    side_at = {side: i for i, (side, _) in enumerate(BLOCKS)}
    corner_at = {q: (i, extent + j) for i, (_, corners) in enumerate(BLOCKS) for j, q in enumerate(corners)}
    for route, out in zip(plan, out_refs):
        at = 0
        for kind, side in route[1]:
            blocks = a_blocks if kind == "a" else b_blocks
            out[at : at + extent, :] = blocks[side_at[side]][:extent]
            at += extent
        if route[2]:
            rows = iota((16, 1), 0)
            tile = jnp.zeros((16, out.shape[1]), F32)
            for i, (kind, q) in enumerate(route[2]):
                block, row = corner_at[q]
                source = (a_blocks if kind == "ac" else b_blocks)[block][extent : extent + 16].astype(F32)
                tile = jnp.where(rows == i, source[row - extent : row - extent + 1], tile)
            out[at : at + 16, :] = tile.astype(BF16)


def read_routes(plan, in_refs, extent):
    sides, corners = {}, {}
    for route, ref in zip(plan, in_refs):
        at = 0
        for key in route[1]:
            sides[key] = ref[at : at + extent, :]
            at += extent
        if route[2]:
            tile = ref[at : at + 16, :].astype(F32)
            for i, key in enumerate(route[2]):
                corners[key] = tile[i : i + 1]
    result = []
    rows = iota((16, 1), 0)
    for kind in ("a", "b"):
        blocks = []
        for side, ends in BLOCKS:
            block = sides[(kind, side)]
            if ends:
                tile = jnp.zeros((16, block.shape[1]), F32)
                for i, q in enumerate(ends):
                    tile = jnp.where(rows == i, corners[(kind + "c", q)], tile)
                block = jnp.concatenate([block, tile.astype(BF16)], axis=0)
            blocks.append(block)
        result.append(blocks)
    return result


def relayed(tiles):
    return tiles == 8


def write_near(a_blocks, b_blocks, near_ref, extent):
    for i, block in enumerate((a_blocks[3], b_blocks[2], a_blocks[2], b_blocks[3])):
        near_ref[i * extent : (i + 1) * extent, :] = block
    rows = iota((16, 1), 0)
    tile = jnp.zeros((16, near_ref.shape[1]), F32)
    at = 0
    for blocks in (a_blocks, b_blocks):
        ends = [blocks[i][extent : extent + 16].astype(F32) for i in range(2)]
        for block, row in ((0, 0), (0, 1), (1, 1), (1, 0)):
            tile = jnp.where(rows == at, ends[block][row : row + 1], tile)
            at += 1
    near_ref[4 * extent : 4 * extent + 16, :] = tile.astype(BF16)


def write_far(a_blocks, b_blocks, far_ref, extent):
    for i, block in enumerate((a_blocks[0], a_blocks[1], b_blocks[0], b_blocks[1])):
        far_ref[i * extent : (i + 1) * extent, :] = block[:extent]


def near_starts(tile, extent):
    right = tile % 2
    odd = (tile // 2) % 2
    corners = 2 * extent + 16
    side = jnp.where(right == 1, 0, 2 * extent)
    one = jnp.where(right == odd, corners, side)
    three = jnp.where(right == odd, side, corners)
    return side_of_partner(right, extent), one, three


def side_of_partner(right, extent):
    return jnp.where(right == 1, 2 * extent, 0)


def read_relay(refs, extent):
    across, one, three, far, opposite = refs
    mine = lax.axis_index("tile")
    left = mine % 2 == 0
    odd = (mine // 2 + mine) % 2 == 1

    def rows_of(ref, start, count):
        return ref[start : start + count, :].astype(F32)

    def choose(start, count):
        return jnp.where(odd, rows_of(one, start, count), rows_of(three, start, count))

    pair = [(rows_of(across, i * extent, extent), choose(i * extent, extent)) for i in range(2)]
    a_east, b_west = [jnp.where(left, here, there).astype(BF16) for here, there in pair]
    a_west, b_east = [jnp.where(left, there, here).astype(BF16) for here, there in pair]
    tail = 2 * extent - 16
    beside = jnp.where(odd, rows_of(three, tail, 16), rows_of(one, tail, 16))
    beyond = opposite[0:16, :].astype(F32)
    third = jnp.where(left, beside, beyond)
    fifth = jnp.where(left, beyond, beside)
    corners = {("a", 0): third[0:1], ("a", 3): third[3:4], ("b", 1): third[5:6], ("b", 2): third[6:7]}
    corners.update({("a", 1): fifth[1:2], ("a", 2): fifth[2:3], ("b", 0): fifth[4:5], ("b", 3): fifth[7:8]})
    rows = iota((16, 1), 0)
    result = []
    for kind, first, east, west in (("a", 0, a_east, a_west), ("b", 2, b_east, b_west)):
        blocks = []
        for i, ends in enumerate(((0, 1), (3, 2))):
            tile = jnp.where(rows == 0, corners[(kind, ends[0])], jnp.where(rows == 1, corners[(kind, ends[1])], 0.0))
            strip = far[(first + i) * extent : (first + i + 1) * extent, :]
            blocks.append(jnp.concatenate([strip, tile.astype(BF16)], axis=0))
        result.append(blocks + [east, west])
    return result


def shifted(image, by, extent):
    if by == 0:
        return image
    column = iota((image.shape[0], 1), 0) % extent
    rolled = pltpu.roll(image, (-by) % image.shape[0], 0)
    return jnp.where(column == (extent - 1 if by == 1 else 0), 0.0, rolled)


def write_columns(q_ref, image, forward, extent):
    count, channels = image.shape
    zero = jnp.zeros((extent, q_ref.shape[1]), BF16)
    q_ref[0:extent, :] = zero
    q_ref[extent + count : 2 * extent + count, :] = zero
    wide = image.astype(F32)
    for b in range(3):
        by = b - 1 if forward else 1 - b
        q_ref[extent : extent + count, b * channels : (b + 1) * channels] = shifted(wide, by, extent).astype(BF16)


def window_product(q_ref, weight, forward, extent, out_ref, chunk=8):
    channels = weight.shape[1]
    if forward:
        taps = tap_weight(weight, range(9), channels)
        nothing = jnp.zeros((3 * channels, channels), weight.dtype)
        both = jnp.concatenate([jnp.concatenate([taps, nothing], axis=0), jnp.concatenate([nothing, taps], axis=0)], axis=1)
    else:
        taps = tap_columns(weight, (6, 7, 8, 3, 4, 5, 0, 1, 2), channels)
        nothing = jnp.zeros((channels, 3 * channels), weight.dtype)
        both = jnp.concatenate([jnp.concatenate([taps, nothing], axis=1), jnp.concatenate([nothing, taps], axis=1)], axis=0)
    for start in range(0, extent // 2, chunk):
        rows = []
        for a in range(4):
            rows.append(jnp.concatenate([q_ref[(2 * i + a) * extent : (2 * i + a + 1) * extent, :] for i in range(start, start + chunk)], axis=0))
        product = (dot if forward else dot_nt)(jnp.concatenate(rows, axis=1), both)
        for i in range(chunk):
            for half in range(2):
                at = (2 * (start + i) + half) * extent
                out_ref[at : at + extent, :] = product[i * extent : (i + 1) * extent, half * channels : (half + 1) * channels]


def tap_weight(weight, taps, channels):
    return jnp.concatenate([weight[t * channels : (t + 1) * channels, :] for t in taps], axis=0)


def tap_columns(weight, taps, channels):
    return jnp.concatenate([weight[t * channels : (t + 1) * channels, :] for t in taps], axis=1)


def halves(values):
    high = values.astype(BF16)
    return high, (values - high.astype(F32)).astype(BF16)


def margin_adds(strips, weight, extent):
    channels = strips[0].shape[1]
    adds = []
    for position, (side, ends) in enumerate(BLOCKS):
        middle = strips[position][:extent].astype(F32)
        row = iota((extent, 1), 0)
        before, after = 0.0, 0.0
        if ends:
            tile = strips[position][extent : extent + 16].astype(F32)
            before, after = tile[0:1], tile[1:2]
        left = jnp.where(row == 0, before, pltpu.roll(middle, 1, 0))
        right = jnp.where(row == extent - 1, after, pltpu.roll(middle, extent - 1, 0))
        window = jnp.concatenate([left, middle, right], axis=1).astype(BF16)
        adds.append(dot(window, tap_weight(weight, block_taps(position), channels)))
    return adds


def margin_forward(strips, weight, columns, extent):
    count = extent * extent
    adds = margin_adds(strips, weight, extent)
    spread = jnp.concatenate(list(halves(adds[2])) + list(halves(adds[3])), axis=0)
    image = dot(columns, spread)
    top = image[:extent] + adds[0]
    bottom = image[count - extent :] + adds[1]
    return jnp.concatenate([top, image[extent : count - extent], bottom], axis=0)


def strip_columns(strips, extent):
    result = []
    for position, (side, ends) in enumerate(BLOCKS):
        middle = strips[position][:extent].astype(F32)
        row = iota((extent, 1), 0)
        after = jnp.where(row == extent - 1, 0.0, pltpu.roll(middle, extent - 1, 0))
        before = jnp.where(row == 0, 0.0, pltpu.roll(middle, 1, 0))
        columns = jnp.concatenate([after, middle, before], axis=1)
        if ends:
            tile = strips[position][extent : extent + 16].astype(F32)
            row = iota((16, 1), 0)
            low = jnp.where(row == 0, tile, 0.0)
            high = jnp.where(row == 1, tile, 0.0)
            columns = jnp.concatenate([columns, jnp.concatenate([low, jnp.zeros_like(tile), high], axis=1)], axis=0)
        result.append(columns.astype(BF16))
    return result


def margin_backward(columns, weight, scatter, extent):
    channels = weight.shape[1]
    adds = [dot_nt(columns[i], tap_columns(weight, block_taps(i), channels)) for i in range(4)]
    high, low = halves(jnp.concatenate(adds, axis=0))
    return dot(scatter, high) + dot(scatter, low)


def weight_sum(out_ref, image_t, q_ref, extent):
    channels = image_t.shape[0]
    count = image_t.shape[1]
    rows = jnp.concatenate([q_ref[(2 - a) * extent : (2 - a) * extent + count, :] for a in range(3)], axis=1)
    product = dot(image_t, rows)
    for tap in range(9):
        out_ref[tap * channels : (tap + 1) * channels, :] = product[:, tap * channels : (tap + 1) * channels]


def margin_weight(strips, columns):
    channels = strips[0].shape[1]
    wide = [dot_t(strips[i], columns[i]) for i in range(4)]
    result = []
    for tap in range(9):
        value = None
        for position in range(4):
            taps = block_taps(position)
            if tap in taps:
                at = taps.index(tap)
                part = wide[position][:, at * channels : (at + 1) * channels]
                value = part if value is None else value + part
        result.append(value)
    return result


def border_index(place, extent, unique):
    last = extent - 1
    part, j = place // extent, place % extent
    index = jnp.where(part == 0, j, jnp.where(part == 1, extent * last + j, jnp.where(part == 2, extent * j + last, extent * j)))
    if unique:
        index = jnp.where((part >= 2) & ((j == 0) | (j == last)), -2, index)
    return index


def border_choice(extent):
    return pick_rows(border_index(iota((4 * extent, 1), 0), extent, True), extent * extent)


def border_of(ref, extent):
    count = extent * extent
    east = ref[pl.ds(extent - 1, extent, stride=extent), :]
    west = ref[pl.ds(0, extent, stride=extent), :]
    return jnp.concatenate([ref[0:extent, :], ref[count - extent : count, :], east, west], axis=0)


def without_repeats(border, extent):
    place = iota((border.shape[0], 1), 0)
    return jnp.where(border_index(place, extent, True) < 0, 0.0, border)


def moved(column, by, extent):
    if by == 0:
        return column
    row = iota((extent, 1), 0)
    return jnp.where(row == (extent - 1 if by == 1 else 0), 0.0, pltpu.roll(column, (-by) % extent, 0))


def border_windows(out_ref, wide_ref, q_ref, forward, extent):
    count, channels = wide_ref.shape
    columns = {c: wide_ref[pl.ds(c, extent, stride=extent), :] for c in (0, 1, extent - 2, extent - 1)}
    nothing = jnp.zeros((extent, channels), F32)
    row = iota((extent, 1), 0)
    inside = (row > 0) & (row < extent - 1)
    for a in range(3):
        start = (a if forward else 2 - a) * extent
        lanes = slice(a * 3 * channels, (a + 1) * 3 * channels)
        out_ref[0:extent, lanes] = q_ref[start : start + extent, :]
        out_ref[extent : 2 * extent, lanes] = q_ref[start + count - extent : start + count, :]
        for part, column in ((2, extent - 1), (3, 0)):
            pieces = []
            for b in range(3):
                at = column + (b - 1 if forward else 1 - b)
                pieces.append(moved(columns[at], a - 1 if forward else 1 - a, extent) if at in columns else nothing)
            value = jnp.where(inside, jnp.concatenate(pieces, axis=1), 0.0)
            out_ref[part * extent : (part + 1) * extent, lanes] = value.astype(BF16)


def gelu_parts(u):
    scale = math.sqrt(2.0 / math.pi)
    square = u * u
    half = 0.5 * u
    t = jnp.tanh(u * (scale + (scale * 0.044715) * square))
    value = half + half * t
    slope = (0.5 + 0.5 * t) + (half * (1.0 - t * t)) * (scale + (scale * 3.0 * 0.044715) * square)
    return value, slope


def call(kernel, name, outs, ins, operands, scratch=(), flops=0, limit=LIMIT):
    specs = [pl.BlockSpec(memory_space={"a": pl.ANY, "s": pltpu.SMEM, "v": pltpu.VMEM}[i]) for i in ins]
    moved = sum(math.prod(o.shape) * o.dtype.itemsize for o in list(outs) + list(operands))
    return pl.pallas_call(
        kernel,
        name=name,
        out_shape=outs,
        in_specs=specs,
        out_specs=[pl.BlockSpec(memory_space=pltpu.VMEM) for _ in outs],
        scratch_shapes=list(scratch),
        cost_estimate=pl.CostEstimate(flops=flops, bytes_accessed=moved, transcendentals=0),
        compiler_params=pltpu.CompilerParams(vmem_limit_bytes=limit),
    )(*operands)


def sds(shape, dtype):
    return jax.ShapeDtypeStruct(shape, dtype)


def exchange(payloads, plan, tiles):
    return [
        lax.ppermute(p, "tile", [(i, (i + route[0]) % tiles) for i in range(tiles)]) for p, route in zip(payloads, plan)
    ]


def swap(value, mask, total):
    return lax.ppermute(value, AXES, [(i, i ^ mask) for i in range(total)])


def reduce_gradients(keep, send, total, work, near=None, far=None):
    rows, channels = keep.shape
    quarter = rows // 4
    wire = BF16 if total <= 32 else F32
    me = lax.axis_index(AXES)
    other = swap(send, 1, total)
    plane = (me >> 1) & 3

    def chunk(index):
        first = lax.dynamic_index_in_dim(keep.reshape(4, quarter, channels), index, 0, keepdims=False)
        second = lax.dynamic_index_in_dim(other.reshape(4, quarter, channels), index, 0, keepdims=False)
        return first + second.astype(F32)

    arrived = {}
    for m in (3, 1, 2):
        message = chunk(plane ^ m).astype(wire)
        if m == 2 and near is not None:
            message = jnp.concatenate([message, near], axis=0)
        arrived[m] = swap(message, m << 1, total)
    part = chunk(plane)
    for m in (3, 1, 2):
        part = part + arrived[m][:quarter].astype(F32)
    part, done = work(part)
    extras = None
    if near is not None:
        across = arrived[2][quarter:]
        extent = far.shape[0] // 4
        starts = near_starts(lax.axis_index("tile") ^ 1, extent)
        direct, one, three = [lax.dynamic_slice_in_dim(across, start, 2 * extent, 0) for start in starts]
        riders = {1: (one,), 2: (far, across[-16:]), 3: (three,)}
    bit = 8
    while bit < total:
        mine = part.astype(wire)
        if 2 * bit < total:
            got = {}
            for m in (3, 2, 1):
                message = mine
                if near is not None:
                    message = jnp.concatenate([mine, *riders[m]], axis=0)
                got[m] = swap(message, m * bit, total)
            part = (mine.astype(F32) + got[1][:quarter].astype(F32)) + (got[2][:quarter].astype(F32) + got[3][:quarter].astype(F32))
            if near is not None:
                extras = [direct, got[1][quarter:], got[3][quarter:], got[2][quarter:-16], got[2][-16:]]
            bit *= 4
        else:
            part = mine.astype(F32) + swap(mine, bit, total).astype(F32)
            bit *= 2
    part, done = lax.optimization_barrier((part, done))
    mine = part.astype(wire)
    ring = jnp.stack([mine] + [swap(mine, m << 1, total) for m in (1, 2, 3)])
    whole = jnp.concatenate([lax.dynamic_index_in_dim(ring, plane ^ j, 0) for j in range(4)], axis=0)
    return whole, extras, done


def join_cores(whole, factor, total):
    rows, channels = whole.shape
    half = sds(whole.shape, F32)
    pieces = 2
    step = rows // pieces

    def write(flip, value_ref, outs, scaled_ref, sems):
        mine = (lax.axis_index("dp") + flip) % 2

        def send(out_ref):
            copies = []
            for i in range(pieces):
                span = pl.ds(i * step, step)
                scaled_ref[span, :] = value_ref[span, :].astype(F32) * factor
                copies.append(pltpu.make_async_copy(scaled_ref.at[span], out_ref.at[span], sems.at[i]))
                copies[-1].start()
            for copy in copies:
                copy.wait()

        for which in range(2):
            pl.when(mine == which)(functools.partial(send, outs[which]))

    def own_half(value_ref, one_ref, two_ref, scaled_ref, sems):
        write(0, value_ref, (one_ref, two_ref), scaled_ref, sems)

    def other_half(value_ref, one_in, two_in, one_ref, two_ref, scaled_ref, sems):
        write(1, value_ref, (one_ref, two_ref), scaled_ref, sems)

    def run(kernel, name, operands, aliases):
        anywhere = pl.BlockSpec(memory_space=pl.ANY)
        return pl.pallas_call(
            kernel,
            name=name,
            out_shape=[half, half],
            in_specs=[pl.BlockSpec(memory_space=pltpu.VMEM)] + [anywhere] * (len(operands) - 1),
            out_specs=[anywhere, anywhere],
            scratch_shapes=[pltpu.VMEM(half.shape, F32), pltpu.SemaphoreType.DMA((pieces,))],
            input_output_aliases=aliases,
            cost_estimate=pl.CostEstimate(flops=rows * channels, bytes_accessed=6 * rows * channels, transcendentals=0),
            compiler_params=pltpu.CompilerParams(vmem_limit_bytes=LIMIT),
        )(*operands)

    other = swap(whole, 1, total)
    begun = run(own_half, "own_half", (whole,), {})
    return run(other_half, "other_half", (other, *begun), {1: 0, 2: 1})


def reach_neighbours(across, one, three, far, total):
    two, three, one = swap(far, 16, total), swap(three, 28, total), swap(one, 12, total)
    across = swap(jnp.concatenate([across, two[-16:]], axis=0), 4, total)
    return [across, one, three, two[:-16], across[-16:]]


def per_device(inputs, weight_one, weight_two, cotangent, edge_code, corner_code):
    tiles, members = lax.axis_size("tile"), lax.axis_size("dp")
    extent, channels = inputs.shape[2], inputs.shape[4]
    count = extent * extent
    factor = 1.0 / math.sqrt(inputs.shape[0] * members * tiles * count)
    source = inputs.reshape(count, channels)
    grad_out = cotangent.reshape(count, channels)
    w_one = weight_one.reshape(9 * channels, channels)
    w_two = weight_two.reshape(9 * channels, channels)
    plan = routes(tiles)
    total = tiles * members
    hops = relayed(tiles)
    near_b, far_b, corner_b = sds((4 * extent + 16, channels), BF16), sds((4 * extent, channels), BF16), sds((16, channels), BF16)
    pair_b = sds((2 * extent, channels), BF16)
    if hops:
        first_routed, second_routed = [pair_b, pair_b, pair_b, sds((4 * extent + 16, channels), BF16)], [near_b, far_b]
        n_routes = 5
    else:
        first_routed = second_routed = [sds((route_rows(r, extent), channels), BF16) for r in plan]
        n_routes = len(plan)
    n_first, n_second = len(first_routed), len(second_routed)

    def write_first(a, b, outs, near_ref):
        if hops:
            write_near(a, b, near_ref, extent)
            write_far(a, b, outs[3], extent)
            for start, out in zip(near_starts(lax.axis_index("tile"), extent), outs):
                out[...] = near_ref[pl.ds(pl.multiple_of(start, 16), 2 * extent), :]
            outs[3][4 * extent : 4 * extent + 16, :] = near_ref[4 * extent : 4 * extent + 16, :]
        else:
            write_routes(a, b, plan, outs, extent)

    def write_second(a, b, outs):
        if hops:
            write_near(a, b, outs[0], extent)
            write_far(a, b, outs[1], extent)
        else:
            write_routes(a, b, plan, outs, extent)

    def read(refs):
        return read_relay(refs, extent) if hops else read_routes(plan, refs, extent)

    image_b, image_f = sds((count, channels), BF16), sds((count, channels), F32)
    columns_b = sds((count + 2 * extent, 3 * channels), BF16)
    taps_b, taps_f = sds((9 * channels, channels), BF16), sds((9 * channels, channels), F32)
    conv = 2 * count * 9 * channels * channels

    strip_rows = block_starts(extent)[3] + extent
    scatter_b, column_b = sds((count, strip_rows), BF16), sds((count, 4 * extent), BF16)
    pieces = 2

    def first_strips(x_hbm, g_hbm, edge_hbm, corner_hbm, *refs):
        outs = refs[:n_first]
        x_ref, g_ref, near_ref, edge_ref, corner_ref, sems = refs[n_first:]
        pairs = [(edge_hbm, edge_ref), (corner_hbm, corner_ref)]
        step = count // pieces
        for source_ref, target_ref in ((g_hbm, g_ref), (x_hbm, x_ref)):
            for i in range(pieces):
                pairs.append((source_ref.at[pl.ds(i * step, step)], target_ref.at[pl.ds(i * step, step)]))
        copies = [pltpu.make_async_copy(a, b, sems.at[i]) for i, (a, b) in enumerate(pairs)]
        for copy in copies:
            copy.start()

        def gather_pieces(choice, image_ref, arriving):
            strips = 0.0
            for i, copy in enumerate(arriving):
                copy.wait()
                span = slice(i * step, (i + 1) * step)
                strips = strips + dot(choice[:, span], image_ref[span, :])
            strips = strips.astype(BF16)
            return [strips[start : start + rows] for start, rows in zip(block_starts(extent), block_rows(extent))]

        b = gather_pieces(block_choice(*fixed_lines(extent), extent), g_ref, copies[2 : 2 + pieces])
        for copy in copies[:2]:
            copy.wait()
        a = gather_pieces(block_choice(*seam_lines(edge_ref, corner_ref, extent), extent), x_ref, copies[2 + pieces :])
        write_first(a, b, outs, near_ref)

    first = call(
        first_strips,
        "first_strips",
        first_routed,
        "aaaa",
        (source, grad_out, edge_code.T, corner_code.T),
        scratch=[
            pltpu.VMEM((count, channels), BF16),
            pltpu.VMEM((count, channels), BF16),
            pltpu.VMEM(near_b.shape, BF16),
            pltpu.SMEM((4, tiles), jnp.int32),
            pltpu.SMEM((4, tiles), jnp.int32),
            pltpu.SemaphoreType.DMA((2 + 2 * pieces,)),
        ],
        limit=ALONE,
        flops=10 * conv,
    )
    first_arrived = reach_neighbours(*first, total) if hops else exchange(first, plan, tiles)

    border = 4 * extent
    border_b, border_f = sds((border, channels), BF16), sds((border, channels), F32)
    windows_b = sds((border, 9 * channels), BF16)

    def inner(edge_ref, corner_ref, x_ref, g_ref, w1_ref, w2_ref, *refs):
        hid_ref, dpre_ref, preb_ref, dhb_ref, sum_ref, seam_ref, back_ref, wx_ref, wg_ref = refs[:9]
        qx_ref, qg_ref, qd_ref, pre_ref, dh_ref, wide_ref = refs[9:]
        wide_ref[...] = x_ref[...].astype(F32)
        write_columns(qx_ref, x_ref[...], True, extent)
        border_windows(wx_ref, wide_ref, qx_ref, True, extent)
        window_product(qx_ref, w1_ref[...], True, extent, pre_ref)
        wide_ref[...] = g_ref[...].astype(F32)
        write_columns(qg_ref, g_ref[...], False, extent)
        border_windows(wg_ref, wide_ref, qg_ref, False, extent)
        window_product(qg_ref, w2_ref[...], False, extent, dh_ref)
        preb_ref[...] = border_of(pre_ref, extent)
        dhb_ref[...] = border_of(dh_ref, extent)
        place = iota((count, 1), 0)
        row, column = place // extent, place % extent
        inside = (row > 0) & (row < extent - 1) & (column > 0) & (column < extent - 1)
        value, slope = gelu_parts(pre_ref[...])
        value = jnp.where(inside, value, 0.0)
        hid_ref[...] = value.astype(BF16)
        dpre_ref[...] = jnp.where(inside, dh_ref[...] * slope, 0.0).astype(BF16)
        write_columns(qd_ref, dpre_ref[...], False, extent)
        weight_sum(sum_ref.at[0], jnp.transpose(x_ref[...].astype(F32)).astype(BF16), qd_ref, extent)
        weight_sum(sum_ref.at[1], jnp.transpose(value).astype(BF16), qg_ref, extent)
        lines, pixels = seam_lines(edge_ref, corner_ref, extent)
        across = border_index(iota((1, border), 1), extent, True)
        seam_ref[...] = (block_index(lines, pixels, 0, extent) == across).astype(F32).astype(BF16)
        down = border_index(iota((border, 1), 0), extent, False)
        back_ref[...] = (down == block_index(lines, pixels, 1, extent)).astype(F32).astype(BF16)

    hid_in, dpre_in, pre_b, dh_b, sums, seam_b, back_b, wx_b, wg_b = call(
        inner,
        "inner_products",
        [
            image_b,
            image_b,
            border_f,
            border_f,
            sds((2,) + taps_f.shape, F32),
            sds((strip_rows, border), BF16),
            sds((border, strip_rows), BF16),
            windows_b,
            windows_b,
        ],
        "ssvvvv",
        (edge_code.T, corner_code.T, source, grad_out, w_one, w_two),
        scratch=[pltpu.VMEM(columns_b.shape, BF16)] * 3 + [pltpu.VMEM(image_f.shape, F32)] * 3,
        flops=4 * conv,
    )

    def middle(preb_ref, dhb_ref, sums_ref, seam_ref, back_ref, wx_ref, wg_ref, w1_ref, w2_ref, *refs):
        arrived = refs[:n_routes]
        keep_ref, send_ref, hid_ref, dpre_ref = refs[n_routes : n_routes + 4]
        outs = refs[n_routes + 4 : n_routes + 4 + n_second]
        (sum_ref,) = refs[n_routes + 4 + n_second :]
        x_strips, g_strips = read(arrived)
        columns = strip_columns(g_strips, extent)
        adds = margin_adds(x_strips, w1_ref[...], extent)
        row = iota((extent, 1), 0)
        first, final = row == 0, row == extent - 1

        def ends(low, high):
            return jnp.where(first, low, 0.0) + jnp.where(final, high, 0.0)

        def end_rows(part):
            return adds[part][0:1], adds[part][extent - 1 : extent]

        (east_low, east_high), (west_low, west_high) = end_rows(2), end_rows(3)
        north = preb_ref[0:extent, :] + adds[0] + ends(west_low, east_low)
        south = preb_ref[extent : 2 * extent, :] + adds[1] + ends(west_high, east_high)

        def side(part, at):
            value = preb_ref[part * extent : (part + 1) * extent, :] + adds[part]
            return jnp.where(first, north[at : at + 1], jnp.where(final, south[at : at + 1], value))

        value, slope = gelu_parts(jnp.concatenate([north, south, side(2, extent - 1), side(3, 0)], axis=0))
        dadds = [dot_nt(columns[i], tap_columns(w2_ref[...], block_taps(i), channels)) for i in range(4)]
        high, low = halves(jnp.concatenate(dadds, axis=0))
        d_hidden = dhb_ref[...] + dot(back_ref[...], high) + dot(back_ref[...], low)
        d_pre = d_hidden * slope
        hidden = without_repeats(value, extent).astype(BF16)
        hid_ref[...] = hidden
        d_once = without_repeats(d_pre, extent).astype(BF16)
        dpre_ref[...] = d_once
        strips = dot(seam_ref[...], hidden).astype(BF16)
        a = [strips[start : start + rows] for start, rows in zip(block_starts(extent), block_rows(extent))]
        b = []
        tall = iota((16, 1), 0)
        for part in range(4):
            block = d_pre[part * extent : (part + 1) * extent]
            if part < 2:
                tile = jnp.where(tall == 0, block[0:1], jnp.where(tall == 1, block[extent - 1 : extent], 0.0))
                block = jnp.concatenate([block, tile], axis=0)
            b.append(block.astype(BF16))
        write_second(a, b, outs)
        own = dot_t(wx_ref[...], d_once)
        margin = margin_weight(x_strips, strip_columns(b, extent))
        for tap in range(9):
            span = slice(tap * channels, (tap + 1) * channels)
            total = sums_ref[0, span, :] + own[span]
            sum_ref[0, span, :] = total if margin[tap] is None else total + margin[tap]
        own = dot_t(hidden, wg_ref[...])
        margin = margin_weight(a, columns)
        for tap in range(9):
            span = slice(tap * channels, (tap + 1) * channels)
            total = sums_ref[1, span, :] + own[:, span]
            sum_ref[1, span, :] = total if margin[tap] is None else total + margin[tap]
        core = lax.axis_index("dp") % 2
        keep_ref[...] = sum_ref[core]
        send_ref[...] = sum_ref[1 - core].astype(BF16)

    results = call(
        middle,
        "gradients",
        [taps_f, taps_b, border_b, border_b] + second_routed,
        "v" * (9 + n_routes),
        (pre_b, dh_b, sums, seam_b, back_b, wx_b, wg_b, w_one, w_two, *first_arrived),
        scratch=[pltpu.VMEM((2,) + taps_f.shape, F32)],
        flops=conv // 4,
    )
    keep, send, hid_edge, dpre_edge = results[:4]

    def later(edge_ref, corner_ref, x_ref, g_ref, hid_ref, dpre_ref, hidb_ref, dpreb_ref, w1_ref, w2_ref, out_ref, dx_ref, scatter_ref, column_ref, q_ref):
        lines, pixels = seam_lines(edge_ref, corner_ref, extent)
        scatter_ref[...] = seam_scatter(lines, pixels, extent)
        column_ref[...] = column_scatter(extent)
        choice = border_choice(extent)
        hidden = hid_ref[...].astype(F32) + dot_t(choice, hidb_ref[...])
        d_pre = dpre_ref[...].astype(F32) + dot_t(choice, dpreb_ref[...])
        write_columns(q_ref, hidden, True, extent)
        window_product(q_ref, w2_ref[...], True, extent, out_ref)
        out_ref[...] = out_ref[...] + x_ref[...].astype(F32)
        write_columns(q_ref, d_pre, False, extent)
        window_product(q_ref, w1_ref[...], False, extent, dx_ref)
        dx_ref[...] = dx_ref[...] + g_ref[...].astype(F32)

    def later_parts(token):
        token, inner_arrays = lax.optimization_barrier((token, (hid_in, dpre_in, hid_edge, dpre_edge)))
        return token, call(
            later,
            "later_products",
            [image_f, image_f, scatter_b, column_b],
            "ss" + "v" * 8,
            (edge_code.T, corner_code.T, source, grad_out, *inner_arrays, w_one, w_two),
            scratch=[pltpu.VMEM(columns_b.shape, BF16)],
            flops=2 * conv,
        )

    if hops:
        whole, second_arrived, parts = reduce_gradients(keep, send, total, later_parts, *results[4:])
    else:
        second_arrived = exchange(results[4:], plan, tiles)
        whole, _, parts = reduce_gradients(keep, send, total, later_parts)

    def last(part_ref, dpart_ref, scatter_ref, column_ref, w1_ref, w2_ref, *refs):
        arrived = refs[:n_routes]
        out_ref, dx_ref = refs[n_routes:]
        h_strips, d_strips = read(arrived)
        out_ref[...] = (part_ref[...] + margin_forward(h_strips, w2_ref[...], column_ref[...], extent)).astype(BF16)
        add = margin_backward(strip_columns(d_strips, extent), w1_ref[...], scatter_ref[...], extent)
        dx_ref[...] = (dpart_ref[...] + add).astype(BF16)

    output, d_input = call(
        last,
        "outputs",
        [image_b, image_b],
        "v" * (6 + n_routes),
        (*parts, w_one, w_two, *second_arrived),
        flops=conv // 4,
    )
    whole, output, d_input = lax.optimization_barrier((whole, output, d_input))
    one, two = join_cores(whole.reshape(9 * channels, channels), factor, total)
    shape = (9, channels, channels)
    return (
        output.reshape(inputs.shape),
        d_input.reshape(inputs.shape),
        one.reshape(shape),
        two.reshape(shape),
    )


def solution(mesh):
    split = P("dp", "tile", None, None, None)
    return jax.shard_map(
        per_device,
        mesh=mesh,
        in_specs=(split, P(), P(), split, P(), P()),
        out_specs=(split, split, P(), P()),
        check_vma=False,
    )
```
